32 devices in a mesh: dp: 8 (over z, x), tensor: 4 (over y, core).
Axes of the slice: x: 2, y: 2, z: 4, core: 2. Of those that a mesh axis runs over, the one named last changes fastest.
Arguments:
- tokens: bfloat16 [1024, 16, 1024], P(None, 'dp'), may hold values from -6 to 6
- condition: bfloat16 [16, 1024], P('dp'), may hold values from -6 to 6
- modulation_weight: bfloat16 [1024, 6144], replicated, may hold values from -0.1875 to 0.1875
- modulation_bias: bfloat16 [6144], replicated, may hold values from -3 to 3
- qkv_weight: bfloat16 [1024, 3, 1024], P(None, None, 'tensor'), may hold values from -0.1875 to 0.1875
- qv_bias: bfloat16 [2, 1024], P(None, 'tensor'), may hold values from -2 to 2
- proj_weight: bfloat16 [1024, 1024], P('tensor'), may hold values from -3 to 3
- proj_bias: bfloat16 [1024], replicated, may hold values from -6 to 6
- up_weight: bfloat16 [1024, 4096], P(None, 'tensor'), may hold values from -0.1875 to 0.1875
- up_bias: bfloat16 [4096], P('tensor'), may hold values from -3 to 3
- down_weight: bfloat16 [4096, 1024], P('tensor'), may hold values from -0.09375 to 0.09375
- down_bias: bfloat16 [1024], replicated, may hold values from -3 to 3
- cotangent: bfloat16 [1024, 16, 1024], P(None, 'dp'), may hold values from -6 to 6
Outputs:
- output: bfloat16 [1024, 16, 1024], P('tensor', 'dp')
- grad_tokens: float32 [1024, 16, 1024], P('tensor', 'dp')
- grad_condition: float32 [16, 1024], P('dp')
- grad_modulation_weight: float32 [1024, 6144], P('dp', 'tensor')
- grad_modulation_bias: float32 [6144], P('tensor')
- grad_qkv_weight: float32 [1024, 3, 1024], P('dp', None, 'tensor')
- grad_qv_bias: float32 [2, 1024], P(None, 'tensor')
- grad_proj_weight: float32 [1024, 1024], P('tensor', 'dp')
- grad_proj_bias: float32 [1024], replicated
- grad_up_weight: float32 [1024, 4096], P('dp', 'tensor')
- grad_up_bias: float32 [4096], P('tensor')
- grad_down_weight: float32 [4096, 1024], P('tensor', 'dp')
- grad_down_bias: float32 [1024], replicated
The draws below stay inside these ranges and needn't reach their ends.
All inputs are finite; a program needn't handle non-finite values.
Results may differ from the reference program's by a relative error of at most 0.013.
The reference program's roundings to bfloat16 on the way count: a program that leaves them out, or rounds other values in their place, can miss the bound.
Values may be sent and summed in bfloat16 or wider, within the bound.
No kernel may reach another device: no remote copies, remote signals or barrier semaphores. Data moves between devices by JAX's collectives and lax.ppermute only.
A program may use at most 192 MiB of HBM per device.

```python
import jax
import jax.numpy as jnp
from jax import lax

D = 1024
HEADS = 16
HEAD_DIM = 64
FF = 4096
SEQ = 1024
LATENTS = 16


def with_spikes(values, stream_key, source, target, blocks, factor):
    def block_of(dim):
        return (jnp.arange(values.shape[dim]) // (values.shape[dim] // blocks)).reshape((-1,) + (1,) * (values.ndim - 1 - dim))

    first = jax.random.permutation(stream_key, blocks)[block_of(target)]
    second = (block_of(target) + blocks // 2) % blocks
    return jnp.where((block_of(source) == first) | (block_of(source) == second), factor * values, values)


def level_of(own_key, extent, cuts, least, high):
    level, own = 1.0, jax.random.fold_in(own_key, 6)
    for axis_at, shards_of in cuts:
        steps = jnp.exp(jax.random.uniform(jax.random.fold_in(own, axis_at), (shards_of,), jnp.float32, least / len(cuts), high / len(cuts)))
        level = level * jnp.repeat(steps, extent[axis_at] // shards_of).reshape([-1 if axis == axis_at else 1 for axis in range(len(extent))])
    return level


def centred(key, extent, scale, most, cuts=(), dtype=jnp.bfloat16):
    values = jax.random.normal(key, extent, jnp.float32) * scale
    if len(cuts) > 0:
        values = level_of(key, extent, cuts, -0.22, 0.18) * values
    return jnp.clip(values, min=-most, max=most).astype(dtype)


def noise_with(rng, extent, spread, limit, pieces, heavy, kind=jnp.bfloat16):
    entries = spread * jax.random.normal(rng, extent, jnp.float32)
    if pieces:
        entries = entries * level_of(rng, extent, pieces, -0.22, 0.18)
    return jnp.clip(with_spikes(entries, jax.random.fold_in(rng, 3), *heavy), -limit, limit).astype(kind)


def setup_inputs(seed: int = 0) -> dict:
    splits = jax.random.split(jax.random.key(seed), 14)
    return {
        "tokens": centred(splits[0], (SEQ, LATENTS, D), 1.0, 6.0, ((1, 8),)),
        "condition": centred(splits[1], (LATENTS, D), 1.0, 6.0, ((0, 8),)),
        "modulation_weight": centred(splits[2], (D, 6 * D), D ** -0.5, 0.1875),
        "modulation_bias": centred(splits[3], (6 * D,), 0.5, 3.0),
        "qkv_weight": centred(splits[4], (D, 3, D), D ** -0.5, 0.1875, ((2, 4),)),
        "qv_bias": centred(splits[5], (2, D), 0.3, 2.0, ((1, 4),)),
        "proj_weight": centred(splits[6], (D, D), (max(D // 256, 1)) ** -0.5, 3.0, ((0, 4),)),
        "proj_bias": centred(splits[7], (D,), 1.5, 6.0),
        "up_weight": centred(splits[8], (D, FF), D ** -0.5, 0.1875, ((1, 4),)),
        "up_bias": centred(splits[9], (FF,), 0.5, 3.0, ((0, 4),)),
        "down_weight": centred(splits[10], (FF, D), FF ** -0.5, 0.09375, ((0, 4),)),
        "down_bias": centred(splits[11], (D,), 0.5, 3.0),
        "cotangent": noise_with(splits[12], (SEQ, LATENTS, D), 1.0, 6.0, ((1, 8),), (1, 2, 8, 2.0)),
    }


HIGH = lax.Precision.HIGHEST
EPS = 1e-06

@jax.custom_vjp
def low(v):
    return lax.optimization_barrier(v.astype(jnp.bfloat16)).astype(jnp.float32)

@jax.custom_vjp
def low_back(v):
    return v

def low_keep(v):
    return (low(v), None)

def low_pass(kept, grad):
    return (grad,)

def back_keep(v):
    return (v, None)

def back_low(kept, grad):
    return (low(grad),)
low.defvjp(low_keep, low_pass)
low_back.defvjp(back_keep, back_low)

def hdot(left, right):
    return jnp.dot(left, right, precision=HIGH, preferred_element_type=jnp.float32)

def normalize(values):
    centre = values - lax.optimization_barrier(jnp.mean(values, axis=-1, keepdims=True))
    return centre * lax.rsqrt(lax.optimization_barrier(jnp.mean(centre * centre, axis=-1, keepdims=True)) + EPS)

def attention(query, key, value):
    block = min(SEQ, 512)
    scale = HEAD_DIM ** (-0.5)

    def one_block(query_block):
        scores = low_back(jnp.einsum('qhd,khd->hqk', query_block, key, precision=HIGH) * scale)
        largest = lax.optimization_barrier(jnp.max(scores, axis=-1, keepdims=True))
        powers = jnp.exp(scores - largest)
        probs = powers / lax.optimization_barrier(jnp.sum(powers, axis=-1, keepdims=True))
        return jnp.einsum('hqk,khd->qhd', low(probs), value, precision=HIGH)
    blocks = query.reshape(SEQ // block, block, HEADS, HEAD_DIM)
    mixed = lax.map(jax.checkpoint(one_block), blocks)
    return mixed.reshape(SEQ, HEADS * HEAD_DIM)

def layer(tokens, condition, modulation_weight, modulation_bias, qkv_weight, qv_bias, proj_weight, proj_bias, up_weight, up_bias, down_weight, down_bias):
    silu_cond = low(jax.nn.silu(condition))
    modulation = low_back(hdot(silu_cond, modulation_weight) + modulation_bias).reshape(6, D)
    shift_one = modulation[0]
    scale_one = modulation[1]
    gate_one = modulation[2]
    shift_two = modulation[3]
    scale_two = modulation[4]
    gate_two = modulation[5]
    attend_in = low(normalize(tokens) * (1.0 + scale_one) + shift_one)
    projected = hdot(attend_in, qkv_weight.reshape(D, 3 * D)).reshape(SEQ, 3, D)
    query = low_back(low(projected[:, 0] + qv_bias[0]))
    key = low_back(low(projected[:, 1]))
    value = low_back(low(projected[:, 2] + qv_bias[1]))
    head_shape = (SEQ, HEADS, HEAD_DIM)
    mixed = low_back(low(attention(query.reshape(head_shape), key.reshape(head_shape), value.reshape(head_shape))))
    attend_update = low_back(hdot(mixed, proj_weight) + proj_bias)
    stream = tokens + gate_one * attend_update
    mlp_in = low(normalize(stream) * (1.0 + scale_two) + shift_two)
    hidden_pre = low_back(hdot(mlp_in, up_weight) + up_bias)
    hidden = low(jax.nn.gelu(hidden_pre, approximate=True))
    mlp_update = low_back(hdot(hidden, down_weight) + down_bias)
    return stream + gate_two * mlp_update

def reference(tokens, condition, modulation_weight, modulation_bias, qkv_weight, qv_bias, proj_weight, proj_bias, up_weight, up_bias, down_weight, down_bias, cotangent):
    params = tuple((item.astype(jnp.float32) for item in (modulation_weight, modulation_bias, qkv_weight, qv_bias, proj_weight, proj_bias, up_weight, up_bias, down_weight, down_bias)))
    latents = jnp.moveaxis(tokens, 1, 0).astype(jnp.float32)
    conditions = condition.astype(jnp.float32)
    cotangents = jnp.moveaxis(cotangent, 1, 0).astype(jnp.float32)
    zeros = tuple((jnp.zeros(item.shape, jnp.float32) for item in params))

    def one_latent(totals, items):
        latent, cond_row, grad_row = items
        result, pull = jax.vjp(layer, latent, cond_row, *params)
        grads = pull(grad_row)
        totals = tuple((total + grad for total, grad in zip(totals, grads[2:])))
        return (totals, (result.astype(jnp.bfloat16), grads[0], grads[1]))
    totals, (results, grad_latents, grad_conditions) = lax.scan(one_latent, zeros, (latents, conditions, cotangents))
    return (jnp.moveaxis(results, 0, 1), jnp.moveaxis(grad_latents, 0, 1), grad_conditions, totals[0], totals[1], totals[2], totals[3], totals[4], totals[5], totals[6], totals[7], totals[8], totals[9])
```

```python
import jax
import jax.numpy as jnp
from jax import lax
from jax.sharding import PartitionSpec as P

HEAD_DIM = 64
EPS = 1e-06
BF = jnp.bfloat16
F32 = jnp.float32


def dot(left, right, dims=((1,), (0,))):
    return lax.dot_general(left, right, (dims, ((), ())), preferred_element_type=F32)


ROWS = ((0,), (0,))
COLS = ((1,), (1,))


def swap(value, axis, bit):
    pairs = [(i, i ^ bit) for i in range(lax.axis_size(axis))]
    return lax.ppermute(value, axis, pairs)


def normalize(values):
    centre = values - jnp.mean(values, axis=-1, keepdims=True)
    inverse = lax.rsqrt(jnp.mean(centre * centre, axis=-1, keepdims=True) + EPS)
    return centre * inverse, inverse


def norm_back(grad, normed, inverse):
    return inverse * (
        grad
        - jnp.mean(grad, axis=-1, keepdims=True)
        - normed * jnp.mean(grad * normed, axis=-1, keepdims=True)
    )


def gelu_pair(v):
    root = 0.7978845608028654
    inner = jnp.tanh(root * (v + 0.044715 * (v * v * v)))
    half = 0.5 * (1.0 + inner)
    slope = half + 0.5 * v * (1.0 - inner * inner) * (root * (1.0 + 3 * 0.044715 * (v * v)))
    return v * half, slope


def attend(query, key, value):
    seq, cols = query.shape
    heads = cols // HEAD_DIM
    mixed, totals = [], []
    for h in range(heads):
        part = slice(h * HEAD_DIM, (h + 1) * HEAD_DIM)
        scores = dot(query[:, part], key[:, part], COLS) * HEAD_DIM**-0.5
        largest = jnp.max(scores, axis=-1, keepdims=True)
        powers = jnp.exp(scores - largest)
        total = jnp.sum(powers, axis=-1, keepdims=True)
        mixed.append(dot((powers / total).astype(BF), value[:, part]).astype(BF))
        totals.append(largest + jnp.log(total))
    return jnp.concatenate(mixed, 1), jnp.concatenate(totals, 1)


def attend_back(query, key, value, log_total, grad_mixed):
    scale = HEAD_DIM**-0.5
    out = ([], [], [])
    for h in range(query.shape[1] // HEAD_DIM):
        part = slice(h * HEAD_DIM, (h + 1) * HEAD_DIM)
        q, k, v, g = query[:, part], key[:, part], value[:, part], grad_mixed[:, part]
        probs = jnp.exp(dot(q, k, COLS) * scale - log_total[:, h : h + 1])
        grad_probs = dot(g, v, COLS)
        inner = jnp.sum(probs * grad_probs, axis=-1, keepdims=True)
        grad_scores = (probs * (grad_probs - inner)).astype(BF)
        out[0].append((dot(grad_scores, k) * scale).astype(BF))
        out[1].append((dot(grad_scores, q, ROWS) * scale).astype(BF))
        out[2].append(dot(probs.astype(BF), g, ROWS).astype(BF))
    return [jnp.concatenate(o, 1) for o in out]


def quarters(values, place, order):
    rows = values.shape[0] // 4
    return jnp.concatenate(
        [lax.dynamic_slice_in_dim(values, (place ^ k) * rows, rows, 0) for k in order], 0
    )


def token_scatter(partial, place):
    rows = partial.shape[0] // 4
    kept = quarters(partial, place, (2, 0)) + swap(quarters(partial, place, (3, 1)), "tensor", 1)
    return kept[rows:] + swap(kept[:rows].astype(BF), "tensor", 2).astype(F32)


def pieces(own):
    far = swap(own, "tensor", 2)
    return own, far, swap(own, "tensor", 1), swap(far, "tensor", 1)


def halve(value, bit):
    mine = (lax.axis_index("dp") // bit) % 2
    half = value.shape[0] // 2
    keep = lax.dynamic_slice_in_dim(value, mine * half, half, 0)
    send = lax.dynamic_slice_in_dim(value, (1 - mine) * half, half, 0)
    return keep + swap(send.astype(BF), "dp", bit).astype(F32)


def dp_scatter(value):
    size = lax.axis_size("dp")
    rows = value.shape[0] // size
    bits = [1 << i for i in range(size.bit_length() - 1)]
    shape = (2,) * len(bits) + (rows,) + value.shape[1:]
    order = tuple(reversed(range(len(bits)))) + tuple(range(len(bits), len(shape)))
    value = jnp.transpose(value.reshape(shape), order).reshape(value.shape)
    for bit in bits:
        value = halve(value, bit)
    return value


def shards(
    tokens,
    condition,
    modulation_weight,
    modulation_bias,
    qkv_weight,
    qv_bias,
    proj_weight,
    proj_bias,
    up_weight,
    up_bias,
    down_weight,
    down_bias,
    cotangent,
):
    seq, lats, width = tokens.shape
    place = lax.axis_index("tensor")
    quarter = seq // 4
    mod_cols = modulation_weight.shape[1] // 4
    proj = pieces(proj_weight)
    cond = condition.astype(F32)
    silu_low = jax.nn.silu(cond).astype(BF)
    modulation = (dot(silu_low, modulation_weight) + modulation_bias.astype(F32)).reshape(
        lats, 6, width
    )
    qkv_flat = qkv_weight.reshape(width, -1)
    heads = qkv_weight.shape[2]
    qv_float = qv_bias.astype(F32)
    span = range(lats)
    tok = [tokens[:, l] for l in span]
    cot = [cotangent[:, l] for l in span]
    here = lambda value: lax.dynamic_slice_in_dim(value, place * quarter, quarter, 0)
    row = lambda l, i: modulation[l, i : i + 1]

    attend_in, query, key, value = [], [], [], []
    for l in span:
        normed, _ = normalize(tok[l].astype(F32))
        attend_in.append((normed * (1.0 + row(l, 1)) + row(l, 0)).astype(BF))
        projected = dot(attend_in[l], qkv_flat)
        query.append((projected[:, :heads] + qv_float[0]).astype(BF))
        key.append(projected[:, heads : 2 * heads].astype(BF))
        value.append((projected[:, 2 * heads :] + qv_float[1]).astype(BF))

    mixed, log_total, mixed_all = [], [], []
    for l in span:
        m, t = attend(query[l], key[l], value[l])
        mixed.append(m)
        log_total.append(t)
        mixed_all.append(pieces(m))

    update, mlp_in, hidden, grad_pre, grad_mlp, mlp_sum, grad_mlp_in = [], [], [], [], [], [], []
    for l in span:
        u = sum(dot(m, p) for m, p in zip(mixed_all[l], proj)) + proj_bias.astype(F32)
        update.append(here(u))
        stream = tok[l].astype(F32) + row(l, 2) * u
        normed, _ = normalize(stream)
        mlp_in.append((normed * (1.0 + row(l, 4)) + row(l, 3)).astype(BF))
        act, slope = gelu_pair(dot(mlp_in[l], up_weight) + up_bias.astype(F32))
        hidden.append(act.astype(BF))
        mlp_sum.append(token_scatter(dot(hidden[l], down_weight), place))
        grad_mlp.append((row(l, 5) * cot[l].astype(F32)).astype(BF))
        grad_pre.append((dot(grad_mlp[l], down_weight, COLS) * slope).astype(BF))
        grad_mlp_in.append(token_scatter(dot(grad_pre[l], up_weight, COLS), place))

    grad_up = sum(dot(mlp_in[l], grad_pre[l], ROWS) for l in span)
    grad_down = sum(dot(grad_mlp[l], hidden[l], ROWS) for l in span)
    row_sum = lambda values: sum(jnp.sum(v, axis=0, dtype=F32) for v in values)
    up_shard = dp_scatter(grad_up)
    down_shard = dp_scatter(grad_down).T

    grad_stream, grad_update, stats, outs = [], [], [], []
    for l in span:
        stream = here(tok[l]).astype(F32) + row(l, 2) * update[l]
        normed, inverse = normalize(stream)
        cot_here = here(cot[l]).astype(F32)
        g = cot_here + norm_back(grad_mlp_in[l] * (1.0 + row(l, 4)), normed, inverse)
        grad_stream.append(g)
        grad_update.append(pieces((row(l, 2) * g).astype(BF)))
        mlp_update = mlp_sum[l] + down_bias.astype(F32)
        outs.append((stream + row(l, 5) * mlp_update).astype(BF))
        total = lambda v: jnp.sum(v, axis=0)
        stats.append(
            [
                total(g * update[l]),
                total(grad_mlp_in[l]),
                total(grad_mlp_in[l] * normed),
                total(cot_here * mlp_update),
            ]
        )

    grad_qkv_low, grad_proj, grad_tokens, mod_part = [], [], [], []
    for l in span:
        near = grad_update[l]
        whole = jnp.zeros((seq, width), BF)
        for k, piece in zip((0, 2, 1, 3), near):
            whole = lax.dynamic_update_slice_in_dim(whole, piece, (place ^ k) * quarter, 0)
        grad_proj.append(dot(whole, mixed[l], ROWS))
        grad_mixed = dot(whole, proj_weight, COLS).astype(BF)
        grads = attend_back(query[l], key[l], value[l], log_total[l], grad_mixed)
        grad_qkv_low.append(jnp.concatenate(grads, 1))
        grad_in = token_scatter(dot(grad_qkv_low[l], qkv_flat, COLS), place)
        normed, inverse = normalize(here(tok[l]).astype(F32))
        grad_tokens.append(
            grad_stream[l] + norm_back(grad_in * (1.0 + row(l, 1)), normed, inverse)
        )
        mod_part.append(jnp.stack([jnp.sum(grad_in, axis=0), jnp.sum(grad_in * normed, axis=0)] + stats[l]))

    grad_qkv = sum(dot(attend_in[l], grad_qkv_low[l], ROWS) for l in span)
    qkv_shard = dp_scatter(grad_qkv).reshape(-1, 3, heads)
    proj_shard = dp_scatter(sum(grad_proj)).T

    mod = jnp.stack(mod_part).reshape(lats, -1)
    mod = mod + swap(mod, "tensor", 1)
    mod = mod + swap(mod, "tensor", 2)
    grad_modulation = mod.astype(BF)
    own_cols = lax.dynamic_slice_in_dim(grad_modulation, place * mod_cols, mod_cols, 1)
    own_weight = lax.dynamic_slice_in_dim(modulation_weight, place * mod_cols, mod_cols, 1)
    grad_silu = dot(own_cols, own_weight, COLS)
    grad_silu = grad_silu + swap(grad_silu, "tensor", 1)
    grad_silu = grad_silu + swap(grad_silu, "tensor", 2)
    grad_condition = jax.vjp(jax.nn.silu, cond)[1](grad_silu)[0]

    qkv_sum = row_sum(grad_qkv_low)
    biases = jnp.concatenate(
        [
            row_sum(grad_pre),
            row_sum(grad_mlp),
            row_sum([p for l in span for p in grad_update[l]]),
            qkv_sum[:heads],
            qkv_sum[2 * heads :],
        ]
    )
    gathered = jnp.concatenate([silu_low.astype(F32), own_cols.astype(F32)], 1)
    size = lax.axis_size("dp")
    index = lax.axis_index("dp")
    for bit in [1 << i for i in range(size.bit_length() - 1)]:
        other = swap(jnp.concatenate([gathered.reshape(-1), biases]), "dp", bit)
        theirs = other[: gathered.size].reshape(gathered.shape)
        biases = biases + other[gathered.size :]
        low = (index // bit) % 2 == 0
        gathered = jnp.concatenate(
            [jnp.where(low, gathered, theirs), jnp.where(low, theirs, gathered)], 0
        )
    all_silu = gathered[:, :width].astype(BF)
    all_cols = gathered[:, width:].astype(BF)
    mod_rows = width // size
    my_silu = lax.dynamic_slice_in_dim(all_silu, index * mod_rows, mod_rows, 1)
    mod_shard = dot(my_silu, all_cols, ROWS)
    mod_bias_sum = jnp.sum(all_cols, axis=0, dtype=F32)
    ff = up_weight.shape[1]
    ends = [ff, ff + width, ff + 2 * width, ff + 2 * width + heads]
    up_bias_sum, down_bias_sum, proj_bias_sum, q_sum, v_sum = jnp.split(biases, ends)
    return (
        jnp.stack(outs, 1),
        jnp.stack(grad_tokens, 1),
        grad_condition,
        mod_shard,
        mod_bias_sum,
        qkv_shard,
        jnp.stack([q_sum, v_sum]),
        proj_shard,
        proj_bias_sum,
        up_shard,
        up_bias_sum,
        down_shard,
        down_bias_sum,
    )


def solution(mesh):
    in_specs = (
        P(None, "dp", None),
        P("dp", None),
        P(),
        P(),
        P(None, None, "tensor"),
        P(None, "tensor"),
        P("tensor", None),
        P(),
        P(None, "tensor"),
        P("tensor"),
        P("tensor", None),
        P(),
        P(None, "dp", None),
    )
    out_specs = (
        P("tensor", "dp", None),
        P("tensor", "dp", None),
        P("dp", None),
        P("dp", "tensor"),
        P("tensor"),
        P("dp", None, "tensor"),
        P(None, "tensor"),
        P("tensor", "dp"),
        P(),
        P("dp", "tensor"),
        P("tensor"),
        P("tensor", "dp"),
        P(),
    )
    return jax.shard_map(shards, mesh=mesh, in_specs=in_specs, out_specs=out_specs, check_vma=False)
```

```python
import functools

import jax
import jax.numpy as jnp
from jax import lax
from jax.experimental import pallas as pl
from jax.experimental.pallas import tpu as pltpu
from jax.sharding import PartitionSpec as P

HEAD_DIM = 64
EPS = 1e-06
BF = jnp.bfloat16
F32 = jnp.float32
ROWS = ((0,), (0,))
COLS = ((1,), (1,))
MIB = 1 << 20
SCALE = HEAD_DIM**-0.5
SEND_FIRST = (3, 1, 2, 0)
NEAR_FIRST = (0, 2, 1, 3)


def dot(left, right, dims=((1,), (0,))):
    return lax.dot_general(left, right, (dims, ((), ())), preferred_element_type=F32)


def swap(value, axis, bit):
    pairs = [(i, i ^ bit) for i in range(lax.axis_size(axis))]
    return lax.ppermute(value, axis, pairs)


def normalize(values):
    centre = values - jnp.mean(values, axis=-1, keepdims=True)
    inverse = lax.rsqrt(jnp.mean(centre * centre, axis=-1, keepdims=True) + EPS)
    return centre * inverse, inverse


def norm_back(grad, normed, inverse):
    return inverse * (
        grad
        - jnp.mean(grad, axis=-1, keepdims=True)
        - normed * jnp.mean(grad * normed, axis=-1, keepdims=True)
    )


def gelu_pair(v):
    root = 0.7978845608028654
    square = v * v
    inner = jnp.tanh(v * (root + (root * 0.044715) * square))
    half = 0.5 + 0.5 * inner
    slope = half + (0.5 * v) * (1.0 - inner * inner) * (root + (3 * root * 0.044715) * square)
    return v * half, slope


def head_lanes(rows, cols, h):
    return lax.broadcasted_iota(jnp.int32, (rows, cols), 1) // HEAD_DIM == h


def spread(x, heads):
    rows, cols = x.shape
    zero = jnp.zeros_like(x)
    return jnp.concatenate([jnp.where(head_lanes(rows, cols, h), x, zero) for h in range(heads)], 0)


def gather_heads(x, heads):
    rows, cols = x.shape[0] // heads, x.shape[1]
    out = x[:rows]
    for h in range(1, heads):
        out = jnp.where(head_lanes(rows, cols, h), x[h * rows : (h + 1) * rows], out)
    return out


def whole(shape):
    return pl.BlockSpec(shape, lambda *_: (0,) * len(shape))


def shape_of(shape, dtype):
    return jax.ShapeDtypeStruct(shape, dtype)


def params(limit):
    return pltpu.CompilerParams(vmem_limit_bytes=limit * MIB)


def cost(flops, moved, special=0):
    return pl.CostEstimate(flops=int(flops), bytes_accessed=int(moved), transcendentals=int(special))


def project_kernel(tok_ref, mod_ref, w_ref, bias_ref, in_ref, q_ref, k_ref, v_ref):
    normed, _ = normalize(tok_ref[0].astype(F32))
    low = (normed * (1.0 + mod_ref[0, 1:2]) + mod_ref[0, 0:1]).astype(BF)
    in_ref[...] = low
    q_ref[...] = (dot(low, w_ref[0]) + bias_ref[0:1].astype(F32)).astype(BF)
    k_ref[...] = dot(low, w_ref[1]).astype(BF)
    v_ref[...] = (dot(low, w_ref[2]) + bias_ref[1:2].astype(F32)).astype(BF)


def project(tok, modulation, w3, bias, lat, block=512):
    _, seq, width = tok.shape
    cols = w3.shape[2]
    rows = lambda n: pl.BlockSpec((block, n), lambda i: (i, 0))
    return pl.pallas_call(
        project_kernel,
        out_shape=[shape_of((seq, width), BF)] + [shape_of((seq, cols), BF)] * 3,
        grid=(seq // block,),
        in_specs=[
            pl.BlockSpec((1, block, width), lambda i: (lat, i, 0)),
            pl.BlockSpec((1,) + modulation.shape[1:], lambda i: (lat, 0, 0)),
            whole(w3.shape),
            whole(bias.shape),
        ],
        out_specs=[rows(width), rows(cols), rows(cols), rows(cols)],
        compiler_params=params(40),
        cost_estimate=cost(6 * seq * width * cols, 4 * seq * width + 6 * seq * cols + 6 * width * cols),
        name="project",
    )(tok, modulation, w3, bias)


def attend_kernel(q_ref, k_ref, v_ref, mixed_ref, total_ref):
    rows, cols = q_ref.shape
    q, k, v = q_ref[...] * BF(SCALE), k_ref[...], v_ref[...]
    out = None
    for h in range(cols // HEAD_DIM):
        mine = head_lanes(rows, cols, h)
        scores = dot(jnp.where(mine, q, jnp.zeros_like(q)), k, COLS)
        largest = jnp.max(scores, axis=1, keepdims=True)
        powers = jnp.exp(scores - largest)
        total = jnp.sum(powers, axis=1, keepdims=True)
        part = dot((powers * (1.0 / total)).astype(BF), v)
        out = part if out is None else jnp.where(mine, part, out)
        log_total = jnp.broadcast_to(largest + jnp.log(total), (rows, 128))
        total_ref[0, :, h * rows : (h + 1) * rows] = log_total.T[:1]
    mixed_ref[...] = out.astype(BF)


def attend(q, k, v, block):
    seq, cols = q.shape
    heads = cols // HEAD_DIM
    rows = pl.BlockSpec((block, cols), lambda i: (i, 0))
    return pl.pallas_call(
        attend_kernel,
        out_shape=(
            shape_of((seq, cols), BF),
            shape_of((seq // block, 1, heads * block), F32),
        ),
        grid=(seq // block,),
        in_specs=[rows, whole((seq, cols)), whole((seq, cols))],
        out_specs=(rows, pl.BlockSpec((1, 1, heads * block), lambda i: (i, 0, 0))),
        compiler_params=params(40),
        cost_estimate=cost(16 * seq * seq * cols, 8 * seq * cols, seq * seq * heads),
        name="attend_forward",
    )(q, k, v)


def feed_kernel(
    order_ref, m0, m1, m2, m3, p0, p1, p2, p3, pb_ref, tok_ref, cot_ref, mod_ref, up_ref, ub_ref, down_ref,
    in_ref, hid_ref, pre_ref, gm_ref, upd_ref, send_u, keep_u, send_g, keep_g, gub_ref, gdb_ref,
):
    i = pl.program_id(0)
    row = lambda j: mod_ref[0, j : j + 1]
    update = pb_ref[...].astype(F32)
    for m, p in ((m0, p0), (m1, p1), (m2, p2), (m3, p3)):
        update = update + dot(m[...], p[...])
    upd_ref[...] = update
    normed, _ = normalize(tok_ref[0].astype(F32) + row(2) * update)
    low = (normed * (1.0 + row(4)) + row(3)).astype(BF)
    in_ref[...] = low
    act, slope = gelu_pair(dot(low, up_ref[...]) + ub_ref[...].astype(F32))
    hidden = act.astype(BF)
    hid_ref[...] = hidden
    grad_mlp = (row(5) * cot_ref[0].astype(F32)).astype(BF)
    gm_ref[...] = grad_mlp
    grad_pre = (dot(grad_mlp, down_ref[...], COLS) * slope).astype(BF)
    pre_ref[...] = grad_pre
    out_g = dot(grad_pre, up_ref[...], COLS)
    out_u = dot(hidden, down_ref[...])

    @pl.when(i < 2)
    def _():
        send_g[...] = out_g
        send_u[...] = out_u

    @pl.when(i >= 2)
    def _():
        keep_g[...] = out_g
        keep_u[...] = out_u

    @pl.when(i == 0)
    def _():
        gub_ref[...] = jnp.zeros_like(gub_ref)
        gdb_ref[...] = jnp.zeros_like(gdb_ref)

    gub_ref[...] += jnp.sum(grad_pre.astype(F32), axis=0, keepdims=True)
    gdb_ref[...] += jnp.sum(grad_mlp.astype(F32), axis=0, keepdims=True)


def feed(order, mixed, proj, proj_bias, tok, cot, modulation, up, up_bias, down, lat):
    _, seq, width = tok.shape
    block = seq // 4
    ff = up.shape[1]
    cols = mixed[0].shape[1]
    at = lambda n: pl.BlockSpec((block, n), lambda i, o: (o[i], 0))
    at3 = pl.BlockSpec((1, block, width), lambda i, o: (lat, o[i], 0))
    send = pl.BlockSpec((block, width), lambda i, o: (jnp.minimum(i, 1), 0))
    keep = pl.BlockSpec((block, width), lambda i, o: (jnp.maximum(i - 2, 0), 0))
    half = shape_of((2 * block, width), F32)
    flops = 2 * seq * width * (width + 4 * ff)
    return pl.pallas_call(
        feed_kernel,
        out_shape=[
            shape_of((seq, width), BF),
            shape_of((seq, ff), BF),
            shape_of((seq, ff), BF),
            shape_of((seq, width), BF),
            shape_of((block, width), F32),
            half,
            half,
            half,
            half,
            shape_of((1, ff), F32),
            shape_of((1, width), F32),
        ],
        grid_spec=pltpu.PrefetchScalarGridSpec(
            num_scalar_prefetch=1,
            grid=(4,),
            in_specs=[at(cols)] * 4
            + [whole((cols, width))] * 4
            + [whole((1, width)), at3, at3]
            + [pl.BlockSpec((1,) + modulation.shape[1:], lambda i, o: (lat, 0, 0))]
            + [whole(up.shape), whole((1, ff)), whole(down.shape)],
            out_specs=[at(width), at(ff), at(ff), at(width), whole((block, width))]
            + [send, keep, send, keep, whole((1, ff)), whole((1, width))],
        ),
        compiler_params=params(56),
        cost_estimate=cost(flops, 40 * MIB, seq * ff),
        name="feed",
    )(order, *mixed, *proj, proj_bias, tok, cot, modulation, up, up_bias, down)


def place_rows(pos_ref, send_ref, keep_ref, first, values, tiles):
    rows = send_ref.shape[0] * 2 // tiles
    for t in range(values.shape[0] // rows):
        pos = pos_ref[first + t]
        part = values[t * rows : (t + 1) * rows]

        @pl.when(pos < tiles // 2)
        def _():
            send_ref[pl.ds(pl.multiple_of(pos * rows, rows), rows), :] = part.astype(BF)

        @pl.when(pos >= tiles // 2)
        def _():
            keep_ref[pl.ds(pl.multiple_of((pos - tiles // 2) * rows, rows), rows), :] = part


def weight_kernel(tiles, terms, pos_ref, *refs):
    i = pl.program_id(0)
    block = refs[0].shape[1]
    rows = refs[-1].shape[0] * 2 // tiles
    for j in range(len(terms)):
        send_ref, keep_ref = refs[-2 * len(terms) + 2 * j], refs[-2 * len(terms) + 2 * j + 1]
        total = None
        for left, right in terms[j]:
            part = dot(refs[left][...], refs[right][...], ROWS)
            total = part if total is None else total + part
        place_rows(pos_ref.at[j], send_ref, keep_ref, i * (block // rows), total, tiles)


def weight_grads(pos, arrays, lefts, terms, widths, name, steps=4):
    tiles = pos.shape[1]
    seq, depth = arrays[lefts[0]].shape
    block = depth // steps
    specs = [
        pl.BlockSpec((seq, block), lambda i, o: (0, i)) if j in lefts else whole(a.shape)
        for j, a in enumerate(arrays)
    ]
    outs, out_specs = [], []
    for width in widths:
        outs += [shape_of((depth // 2, width), BF), shape_of((depth // 2, width), F32)]
        out_specs += [whole((depth // 2, width))] * 2
    flops = sum(2 * seq * depth * w * len(t) for w, t in zip(widths, terms))
    moved = sum(a.size * 2 for a in arrays) + sum(depth * w * 3 for w in widths)
    return pl.pallas_call(
        functools.partial(weight_kernel, tiles, terms),
        out_shape=outs,
        grid_spec=pltpu.PrefetchScalarGridSpec(
            num_scalar_prefetch=1, grid=(steps,), in_specs=specs, out_specs=out_specs
        ),
        compiler_params=params(56),
        cost_estimate=cost(flops, moved),
        name=name,
    )(pos, *arrays)


def proj_grad_kernel(tiles, quarter, order_ref, pos_ref, *refs):
    mixed, pieces, (send_ref, keep_ref) = refs[:2], refs[2:10], refs[10:]
    total = None
    for lat in range(2):
        for j in range(4):
            rows = pl.ds(pl.multiple_of(order_ref[j] * quarter, quarter), quarter)
            part = dot(mixed[lat][rows, :], pieces[4 * lat + j][...], ROWS)
            total = part if total is None else total + part
    place_rows(pos_ref, send_ref, keep_ref, 0, total.T, tiles)


def proj_grad(order, pos, mixed, pieces):
    tiles = pos.shape[0]
    quarter, width = pieces[0][0].shape
    cols = mixed[0].shape[1]
    args = list(mixed) + [p for four in pieces for p in four]
    return pl.pallas_call(
        functools.partial(proj_grad_kernel, tiles, quarter),
        out_shape=[shape_of((width // 2, cols), BF), shape_of((width // 2, cols), F32)],
        grid_spec=pltpu.PrefetchScalarGridSpec(
            num_scalar_prefetch=2,
            grid=(1,),
            in_specs=[whole(a.shape) for a in args],
            out_specs=[whole((width // 2, cols))] * 2,
        ),
        compiler_params=params(40),
        cost_estimate=cost(16 * quarter * width * cols, 8 * MIB),
        name="proj_grad",
    )(order, pos, *args)


def back_kernel(
    near_ref, order_ref, u0, u1, u2, u3, p_ref, q_ref, k_ref, v_ref, total_ref, w_ref, tok_ref,
    low_ref, send_ref, keep_ref, bias_ref, stat_ref, dk_acc, dv_acc,
):
    i = pl.program_id(0)
    rows, cols = q_ref.shape
    heads = cols // HEAD_DIM

    @pl.when(i == 0)
    def _():
        dk_acc[...] = jnp.zeros_like(dk_acc)
        dv_acc[...] = jnp.zeros_like(dv_acc)
        stat_ref[...] = jnp.zeros_like(stat_ref)

    @pl.when(i < 4)
    def _():
        update = u3[...]
        for j, piece in ((2, u2), (1, u1), (0, u0)):
            update = jnp.where(i == j, piece[...], update)
        grad = dot(update, p_ref[...], COLS).astype(BF)
        q = spread(q_ref[...] * BF(SCALE), heads)
        g = spread(grad, heads)
        k, v = k_ref[...], v_ref[...]
        probs = jnp.exp(dot(k, q, COLS) - total_ref[0])
        grad_probs = dot(v, g, COLS)
        inner = jnp.sum(probs * grad_probs, axis=0, keepdims=True)
        scores = (probs * (grad_probs - inner)).astype(BF)
        dv_acc[...] += dot(probs.astype(BF), g)
        dk_acc[...] += dot(scores, q)
        dq = gather_heads(dot(scores, k, ROWS), heads) * SCALE
        low_ref[0, pl.ds(pl.multiple_of(near_ref[i] * rows, rows), rows), :] = dq.astype(BF)

    @pl.when(i == 3)
    def _():
        low_ref[1] = dk_acc[...].astype(BF)
        low_ref[2] = dv_acc[...].astype(BF)
        for j in range(3):
            bias_ref[j : j + 1] = jnp.sum(low_ref[j].astype(F32), axis=0, keepdims=True)

    @pl.when(i >= 4)
    def _():
        here = pl.ds(pl.multiple_of(order_ref[jnp.maximum(i - 4, 0)] * rows, rows), rows)
        out = None
        for j in range(3):
            part = dot(low_ref[j, here, :], w_ref[j], COLS)
            out = part if out is None else out + part
        normed, _ = normalize(tok_ref[0].astype(F32))
        stat_ref[0:1] += jnp.sum(out, axis=0, keepdims=True)
        stat_ref[1:2] += jnp.sum(out * normed, axis=0, keepdims=True)

        @pl.when(i < 6)
        def _():
            send_ref[...] = out

        @pl.when(i >= 6)
        def _():
            keep_ref[...] = out


def attend_back(near, order, pieces, proj, q, k, v, total, w3, tok, lat):
    seq, cols = q.shape
    width = proj.shape[1]
    block = seq // 4
    heads = cols // HEAD_DIM
    first = lambda i, n, o: n[jnp.minimum(i, 3)]
    later = lambda i, n, o: o[jnp.maximum(i - 4, 0)]
    half = shape_of((2 * block, width), F32)
    flops = 20 * seq * seq * cols + 8 * seq * width * cols
    return pl.pallas_call(
        back_kernel,
        out_shape=[shape_of((3, seq, cols), BF), half, half, shape_of((8, cols), F32), shape_of((8, width), F32)],
        grid_spec=pltpu.PrefetchScalarGridSpec(
            num_scalar_prefetch=2,
            grid=(8,),
            in_specs=[whole((block, width))] * 4
            + [whole(proj.shape), pl.BlockSpec((block, cols), lambda *a: (first(*a), 0))]
            + [whole((seq, cols))] * 2
            + [pl.BlockSpec((1, 1, heads * block), lambda *a: (first(*a), 0, 0))]
            + [whole(w3.shape), pl.BlockSpec((1, block, width), lambda *a: (lat, later(*a), 0))],
            out_specs=[
                whole((3, seq, cols)),
                pl.BlockSpec((block, width), lambda i, n, o: (jnp.clip(i - 4, 0, 1), 0)),
                pl.BlockSpec((block, width), lambda i, n, o: (jnp.clip(i - 6, 0, 1), 0)),
                whole((8, cols)),
                whole((8, width)),
            ],
            scratch_shapes=[pltpu.VMEM((seq, cols), F32)] * 2,
        ),
        compiler_params=params(58),
        cost_estimate=cost(flops, 16 * MIB, seq * seq * heads),
        name="attend_backward",
    )(near, order, *pieces, proj, q, k, v, total, w3, tok)


def token_scatter(send, keep):
    rows = keep.shape[0] // 2
    kept = keep + swap(send, "tensor", 1)
    return kept[rows:] + swap(kept[:rows].astype(BF), "tensor", 2).astype(F32)


def pieces_of(own):
    far = swap(own, "tensor", 2)
    return own, far, swap(own, "tensor", 1), swap(far, "tensor", 1)


def dp_bits(size):
    return [1 << i for i in range(size.bit_length() - 1)]


def row_places(index, size, bits):
    away = jnp.arange(size, dtype=jnp.int32) ^ index
    place = jnp.zeros((size,), jnp.int32)
    for bit in bits:
        place = 2 * place + 1 - (away // bit) % 2
    return place


def dp_scatter(send, keep, bits):
    for bit in bits:
        kept = keep + swap(send, "dp", bit).astype(F32)
        half = kept.shape[0] // 2
        send, keep = kept[:half].astype(BF), kept[half:]
    return kept


def shards(
    tokens,
    condition,
    modulation_weight,
    modulation_bias,
    qkv_weight,
    qv_bias,
    proj_weight,
    proj_bias,
    up_weight,
    up_bias,
    down_weight,
    down_bias,
    cotangent,
):
    seq, lats, width = tokens.shape
    place = lax.axis_index("tensor")
    index = lax.axis_index("dp")
    size = lax.axis_size("dp")
    quarter = seq // 4
    mod_cols = modulation_weight.shape[1] // 4
    span = range(lats)
    order = jnp.array(SEND_FIRST, jnp.int32) ^ place
    near = jnp.array(NEAR_FIRST, jnp.int32) ^ place
    bits = dp_bits(size)
    other_bits = [bits[1], bits[0]] + bits[2:]
    places, other_places = row_places(index, size, bits), row_places(index, size, other_bits)
    proj = pieces_of(proj_weight)
    cond = condition.astype(F32)
    silu_low = jax.nn.silu(cond).astype(BF)
    modulation = (dot(silu_low, modulation_weight) + modulation_bias.astype(F32)).reshape(
        lats, 6, width
    )
    w3 = jnp.transpose(qkv_weight, (1, 0, 2))
    heads = w3.shape[2]
    tok = jnp.transpose(tokens, (1, 0, 2))
    cot = jnp.transpose(cotangent, (1, 0, 2))
    here = lambda value: lax.dynamic_slice_in_dim(value, place * quarter, quarter, 0)
    row = lambda l, i: modulation[l, i : i + 1]

    projected = [project(tok, modulation, w3, qv_bias, l) for l in span]
    mixed, log_total = zip(*[attend(*projected[l][1:], quarter) for l in span])
    mixed_all = [pieces_of(m) for m in mixed]

    fed = [
        feed(
            order, mixed_all[l], proj, proj_bias[None], tok, cot, modulation, up_weight,
            up_bias[None], down_weight, l,
        )
        for l in span
    ]
    mlp_in, hidden, grad_pre, grad_mlp, update = [[f[j] for f in fed] for j in range(5)]
    grad_mlp_in = [token_scatter(f[7], f[8]) for f in fed]
    mlp_sum = [token_scatter(f[5], f[6]) for f in fed]
    arrays = mlp_in + grad_pre + grad_mlp + hidden
    up_send, up_keep, down_send, down_keep = weight_grads(
        jnp.stack([places, other_places]),
        arrays,
        (0, 1, 4, 5),
        (((0, 2), (1, 3)), ((4, 6), (5, 7))),
        (hidden[0].shape[1],) * 2,
        "feed_grads",
    )
    up_shard = dp_scatter(up_send, up_keep, bits)
    down_shard = dp_scatter(down_send, down_keep, other_bits).T

    grad_stream, grad_update, stats, outs = [], [], [], []
    for l in span:
        stream = here(tok[l]).astype(F32) + row(l, 2) * update[l]
        normed, inverse = normalize(stream)
        cot_here = here(cot[l]).astype(F32)
        g = cot_here + norm_back(grad_mlp_in[l] * (1.0 + row(l, 4)), normed, inverse)
        grad_stream.append(g)
        grad_update.append(pieces_of((row(l, 2) * g).astype(BF)))
        mlp_update = mlp_sum[l] + down_bias.astype(F32)
        outs.append((stream + row(l, 5) * mlp_update).astype(BF))
        total = lambda v: jnp.sum(v, axis=0)
        stats.append(
            [
                total(g * update[l]),
                total(grad_mlp_in[l]),
                total(grad_mlp_in[l] * normed),
                total(cot_here * mlp_update),
            ]
        )

    proj_send, proj_keep = proj_grad(near, places, mixed, grad_update)
    proj_shard = dp_scatter(proj_send, proj_keep, bits).T
    backs = [
        attend_back(
            near, order, grad_update[l], proj_weight, *projected[l][1:], log_total[l], w3, tok, l
        )
        for l in span
    ]
    lows = [b[0] for b in backs]
    attend_in = [p[0] for p in projected]
    arrays = attend_in + [low[j] for low in lows for j in range(3)]
    sent = weight_grads(
        jnp.stack([other_places] * 3),
        arrays,
        (0, 1),
        tuple(((0, 2 + j), (1, 5 + j)) for j in range(3)),
        (heads,) * 3,
        "qkv_grads",
    )
    qkv_shard = dp_scatter(
        jnp.concatenate(sent[0::2], 1), jnp.concatenate(sent[1::2], 1), other_bits
    ).reshape(-1, 3, heads)

    grad_tokens, mod_part = [], []
    for l in span:
        grad_in = token_scatter(backs[l][1], backs[l][2])
        normed, inverse = normalize(here(tok[l]).astype(F32))
        grad_tokens.append(
            grad_stream[l] + norm_back(grad_in * (1.0 + row(l, 1)), normed, inverse)
        )
        mod_part.append(jnp.stack([backs[l][4][0], backs[l][4][1]] + stats[l]))

    mod = jnp.stack(mod_part).reshape(lats, -1)
    mod = mod + swap(mod, "tensor", 1)
    mod = mod + swap(mod, "tensor", 2)
    grad_modulation = mod.astype(BF)
    own_cols = lax.dynamic_slice_in_dim(grad_modulation, place * mod_cols, mod_cols, 1)
    own_weight = lax.dynamic_slice_in_dim(modulation_weight, place * mod_cols, mod_cols, 1)
    grad_silu = dot(own_cols, own_weight, COLS)
    grad_silu = grad_silu + swap(grad_silu, "tensor", 1)
    grad_silu = grad_silu + swap(grad_silu, "tensor", 2)
    grad_condition = jax.vjp(jax.nn.silu, cond)[1](grad_silu)[0]

    qkv_sum = backs[0][3] + backs[1][3]
    update_sum = sum(jnp.sum(p, axis=0, dtype=F32) for l in span for p in grad_update[l])
    biases = jnp.concatenate(
        [(fed[0][9] + fed[1][9])[0], (fed[0][10] + fed[1][10])[0], update_sum, qkv_sum[0], qkv_sum[2]]
    )
    gathered = jnp.concatenate([silu_low.astype(F32), own_cols.astype(F32)], 1)
    for bit in bits:
        other = swap(jnp.concatenate([gathered.reshape(-1), biases]), "dp", bit)
        theirs = other[: gathered.size].reshape(gathered.shape)
        biases = biases + other[gathered.size :]
        low = (index // bit) % 2 == 0
        gathered = jnp.concatenate(
            [jnp.where(low, gathered, theirs), jnp.where(low, theirs, gathered)], 0
        )
    all_silu = gathered[:, :width].astype(BF)
    all_cols = gathered[:, width:].astype(BF)
    mod_rows = width // size
    my_silu = lax.dynamic_slice_in_dim(all_silu, index * mod_rows, mod_rows, 1)
    mod_shard = dot(my_silu, all_cols, ROWS)
    mod_bias_sum = jnp.sum(all_cols, axis=0, dtype=F32)
    ff = up_weight.shape[1]
    ends = [ff, ff + width, ff + 2 * width, ff + 2 * width + heads]
    up_bias_sum, down_bias_sum, proj_bias_sum, q_sum, v_sum = jnp.split(biases, ends)
    return (
        jnp.stack(outs, 1),
        jnp.stack(grad_tokens, 1),
        grad_condition,
        mod_shard,
        mod_bias_sum,
        qkv_shard,
        jnp.stack([q_sum, v_sum]),
        proj_shard,
        proj_bias_sum,
        up_shard,
        up_bias_sum,
        down_shard,
        down_bias_sum,
    )


def solution(mesh):
    in_specs = (
        P(None, "dp", None),
        P("dp", None),
        P(),
        P(),
        P(None, None, "tensor"),
        P(None, "tensor"),
        P("tensor", None),
        P(),
        P(None, "tensor"),
        P("tensor"),
        P("tensor", None),
        P(),
        P(None, "dp", None),
    )
    out_specs = (
        P("tensor", "dp", None),
        P("tensor", "dp", None),
        P("dp", None),
        P("dp", "tensor"),
        P("tensor"),
        P("dp", None, "tensor"),
        P(None, "tensor"),
        P("tensor", "dp"),
        P(),
        P("dp", "tensor"),
        P("tensor"),
        P("tensor", "dp"),
        P(),
    )
    return jax.shard_map(shards, mesh=mesh, in_specs=in_specs, out_specs=out_specs, check_vma=False)
```

```python
import functools

import jax
import jax.numpy as jnp
from jax import lax
from jax.experimental import pallas as pl
from jax.experimental.pallas import tpu as pltpu
from jax.sharding import PartitionSpec as P

HEAD_DIM = 64
EPS = 1e-06
BF = jnp.bfloat16
F32 = jnp.float32
ROWS = ((0,), (0,))
COLS = ((1,), (1,))
MIB = 1 << 20
SCALE = HEAD_DIM**-0.5
SEND_FIRST = (3, 1, 2, 0)
NEAR_FIRST = (0, 2, 1, 3)
LIMITS = {
    "project": 24,
    "feed": 36,
    "feed_down": 20,
    "up_grad": 28,
    "down_grad": 28,
    "qkv_grad": 28,
    "attend_forward": 20,
    "attend_backward": 28,
    "attend_backward_end": 32,
}


def dot(left, right, dims=((1,), (0,))):
    return lax.dot_general(left, right, (dims, ((), ())), preferred_element_type=F32)


def swap(value, axis, bit):
    pairs = [(i, i ^ bit) for i in range(lax.axis_size(axis))]
    return lax.ppermute(value, axis, pairs)


def normalize(values):
    centre = values - jnp.mean(values, axis=-1, keepdims=True)
    inverse = lax.rsqrt(jnp.mean(centre * centre, axis=-1, keepdims=True) + EPS)
    return centre * inverse, inverse


def norm_back(grad, normed, inverse):
    return inverse * (
        grad
        - jnp.mean(grad, axis=-1, keepdims=True)
        - normed * jnp.mean(grad * normed, axis=-1, keepdims=True)
    )


def gelu_pair(v):
    root = 0.7978845608028654
    square = v * v
    inner = jnp.tanh(v * (root + (root * 0.044715) * square))
    half = 0.5 + 0.5 * inner
    slope = half + (0.5 * v) * (1.0 - inner * inner) * (root + (3 * root * 0.044715) * square)
    return v * half, slope


def head_lanes(rows, cols, h):
    return lax.broadcasted_iota(jnp.int32, (rows, cols), 1) // HEAD_DIM == h


def spread(x, heads):
    rows, cols = x.shape
    zero = jnp.zeros_like(x)
    return jnp.concatenate([jnp.where(head_lanes(rows, cols, h), x, zero) for h in range(heads)], 0)


def gather_heads(x, heads):
    rows, cols = x.shape[0] // heads, x.shape[1]
    out = x[:rows]
    for h in range(1, heads):
        out = jnp.where(head_lanes(rows, cols, h), x[h * rows : (h + 1) * rows], out)
    return out


def whole(shape):
    return pl.BlockSpec(shape, lambda *_: (0,) * len(shape))


def shape_of(shape, dtype):
    return jax.ShapeDtypeStruct(shape, dtype)


def cost(expected):
    return pl.CostEstimate(flops=int(expected * 1.15e10), bytes_accessed=0, transcendentals=0)


ANY = pl.BlockSpec(memory_space=pl.ANY)


def call(kernel, name, scalars, grid, ins, in_specs, outs, out_specs, expected, after=(), scratch=()):
    skip = len(after)

    def body(*refs):
        first = len(scalars)
        kernel(*refs[:first], *refs[first + skip :])

    return pl.pallas_call(
        body,
        out_shape=[shape_of(*o) for o in outs],
        grid_spec=pltpu.PrefetchScalarGridSpec(
            num_scalar_prefetch=len(scalars),
            grid=grid,
            in_specs=[ANY] * skip + in_specs,
            out_specs=out_specs,
            scratch_shapes=list(scratch),
        ),
        compiler_params=pltpu.CompilerParams(vmem_limit_bytes=LIMITS.get(name, 16) * MIB),
        cost_estimate=cost(expected),
        name=name,
    )(*scalars, *after, *ins)


def modulate_kernel(cond_ref, w_ref, bias_ref, out_ref):
    out_ref[...] = dot(cond_ref[...], w_ref[...]) + bias_ref[...].astype(F32)


def modulate(cond, weight, bias, first, count, after=()):
    lats, width = cond.shape
    return call(
        modulate_kernel, "modulate", [], (count,),
        [cond, weight, bias],
        [
            whole(cond.shape),
            pl.BlockSpec((width, width), lambda i: (0, first + i)),
            pl.BlockSpec((1, width), lambda i: (0, first + i)),
        ],
        [((lats, count * width), F32)],
        [pl.BlockSpec((lats, width), lambda i: (0, i))],
        count / 2, after,
    )[0]


def project_kernel(lat, tok_ref, mod_ref, w_ref, bias_ref, in_ref, q_ref, k_ref, v_ref):
    width = tok_ref.shape[2]
    row = lambda j: mod_ref[lat : lat + 1, j * width : (j + 1) * width]
    normed, _ = normalize(tok_ref[0].astype(F32))
    low = (normed * (1.0 + row(1)) + row(0)).astype(BF)
    in_ref[...] = low
    q_ref[...] = (dot(low, w_ref[0]) + bias_ref[0:1].astype(F32)).astype(BF)
    k_ref[...] = dot(low, w_ref[1]).astype(BF)
    v_ref[...] = (dot(low, w_ref[2]) + bias_ref[1:2].astype(F32)).astype(BF)


def project(tok, mod, w3, bias, lat, after=(), block=512):
    _, seq, width = tok.shape
    cols = w3.shape[2]
    rows = lambda n: pl.BlockSpec((block, n), lambda i: (i, 0))
    return call(
        functools.partial(project_kernel, lat), "project", [], (seq // block,),
        [tok, mod, w3, bias],
        [pl.BlockSpec((1, block, width), lambda i: (lat, i, 0))] + [whole(a.shape) for a in (mod, w3, bias)],
        [((seq, width), BF)] + [((seq, cols), BF)] * 3,
        [rows(width), rows(cols), rows(cols), rows(cols)],
        3, after,
    )


def attend_kernel(q_ref, k_ref, v_ref, mixed_ref, total_ref):
    rows, cols = q_ref.shape
    q, k, v = q_ref[...] * BF(SCALE), k_ref[...], v_ref[...]
    out = None
    for h in range(cols // HEAD_DIM):
        mine = head_lanes(rows, cols, h)
        scores = dot(jnp.where(mine, q, jnp.zeros_like(q)), k, COLS)
        largest = jnp.max(scores, axis=1, keepdims=True)
        powers = jnp.exp(scores - largest)
        total = jnp.sum(powers, axis=1, keepdims=True)
        part = dot((powers * (1.0 / total)).astype(BF), v)
        out = part if out is None else jnp.where(mine, part, out)
        log_total = jnp.broadcast_to(largest + jnp.log(total), (rows, 128))
        total_ref[0, :, h * rows : (h + 1) * rows] = log_total.T[:1]
    mixed_ref[...] = out.astype(BF)


def attend(q, k, v, block):
    seq, cols = q.shape
    heads = cols // HEAD_DIM
    rows = pl.BlockSpec((block, cols), lambda i: (i, 0))
    return call(
        attend_kernel, "attend_forward", [], (seq // block,),
        [q, k, v],
        [rows, whole((seq, cols)), whole((seq, cols))],
        [((seq, cols), BF), ((seq // block, 1, heads * block), F32)],
        [rows, pl.BlockSpec((1, 1, heads * block), lambda i: (i, 0, 0))],
        8,
    )


def halves(block, width):
    return [
        pl.BlockSpec((block, width), lambda i, *_: (jnp.minimum(i, 1), 0)),
        whole((block, width)),
        whole((block, width)),
    ]


def place_quarter(step, value, send_ref, far_ref, own_ref):
    @pl.when(step < 2)
    def _():
        send_ref[...] = value

    @pl.when(step == 2)
    def _():
        far_ref[...] = value

    @pl.when(step == 3)
    def _():
        own_ref[...] = value


def feed_kernel(
    lat, order_ref, m0, m1, m2, m3, p0, p1, p2, p3, pb_ref, tok_ref, cot_ref, mod_ref, up_ref, ub_ref, down_ref,
    in_ref, hid_ref, pre_ref, gm_ref, upd_ref, send_ref, far_ref, own_ref, gub_ref, gdb_ref,
):
    i = pl.program_id(0)
    width = tok_ref.shape[2]
    row = lambda j: mod_ref[lat : lat + 1, j * width : (j + 1) * width]
    update = pb_ref[...].astype(F32)
    for m, p in ((m0, p0), (m1, p1), (m2, p2), (m3, p3)):
        update = update + dot(m[...], p[...])
    upd_ref[...] = update
    normed, _ = normalize(tok_ref[0].astype(F32) + row(0) * update)
    low = (normed * (1.0 + row(2)) + row(1)).astype(BF)
    in_ref[...] = low
    act, slope = gelu_pair(dot(low, up_ref[...]) + ub_ref[...].astype(F32))
    hid_ref[...] = act.astype(BF)
    grad_mlp = (row(3) * cot_ref[0].astype(F32)).astype(BF)
    gm_ref[...] = grad_mlp
    grad_pre = (dot(grad_mlp, down_ref[...], COLS) * slope).astype(BF)
    pre_ref[...] = grad_pre
    place_quarter(i, dot(grad_pre, up_ref[...], COLS), send_ref, far_ref, own_ref)

    @pl.when(i == 0)
    def _():
        gub_ref[...] = jnp.zeros_like(gub_ref)
        gdb_ref[...] = jnp.zeros_like(gdb_ref)

    gub_ref[...] += jnp.sum(grad_pre.astype(F32), axis=0, keepdims=True)
    gdb_ref[...] += jnp.sum(grad_mlp.astype(F32), axis=0, keepdims=True)


def feed(order, mixed, proj, proj_bias, tok, cot, mod, up, up_bias, down, lat, after=()):
    _, seq, width = tok.shape
    block = seq // 4
    ff = up.shape[1]
    cols = mixed[0].shape[1]
    at = lambda n: pl.BlockSpec((block, n), lambda i, o: (o[i], 0))
    at3 = pl.BlockSpec((1, block, width), lambda i, o: (lat, o[i], 0))
    quarter = ((block, width), F32)
    return call(
        functools.partial(feed_kernel, lat), "feed", [order], (4,),
        [*mixed, *proj, proj_bias, tok, cot, mod, up, up_bias, down],
        [at(cols)] * 4
        + [whole((cols, width))] * 4
        + [whole((1, width)), at3, at3, whole(mod.shape)]
        + [whole(up.shape), whole((1, ff)), whole(down.shape)],
        [((seq, width), BF), ((seq, ff), BF), ((seq, ff), BF), ((seq, width), BF), quarter]
        + [((2 * block, width), F32), quarter, quarter, ((1, ff), F32), ((1, width), F32)],
        [at(width), at(ff), at(ff), at(width), whole((block, width))]
        + halves(block, width)
        + [whole((1, ff)), whole((1, width))],
        18, after,
    )


def down_kernel(order_ref, hid_ref, down_ref, send_ref, far_ref, own_ref):
    out = dot(hid_ref[...], down_ref[...])
    place_quarter(pl.program_id(0), out, send_ref, far_ref, own_ref)


def feed_down(order, hidden, down, after=()):
    seq, ff = hidden.shape
    width = down.shape[1]
    block = seq // 4
    quarter = ((block, width), F32)
    return call(
        down_kernel, "feed_down", [order], (4,),
        [hidden, down],
        [pl.BlockSpec((block, ff), lambda i, o: (o[i], 0)), whole(down.shape)],
        [((2 * block, width), F32), quarter, quarter],
        halves(block, width),
        5, after,
    )


def own_rows(lat, rows, width):
    return pl.BlockSpec((1, rows, width), lambda i, o: (lat, o[0], 0))


def second(rows, width):
    return pl.BlockSpec((rows, width), lambda i, o: (1, 0))


def stats_of(ref, values):
    ref[...] = jnp.zeros_like(ref)
    for j, value in enumerate(values):
        ref[j : j + 1] = jnp.sum(value, axis=0, keepdims=True)


def middle_kernel(lat, place_ref, own, near, far, upd_ref, tok_ref, cot_ref, mod_ref, g_ref, low_ref, stat_ref):
    width = upd_ref.shape[1]
    row = lambda j: mod_ref[lat : lat + 1, j * width : (j + 1) * width]
    grad_in = own[...] + near[...] + far[...].astype(F32)
    update = upd_ref[...]
    normed, inverse = normalize(tok_ref[0].astype(F32) + row(0) * update)
    grad = cot_ref[0].astype(F32) + norm_back(grad_in * (1.0 + row(2)), normed, inverse)
    g_ref[...] = grad
    low_ref[...] = (row(0) * grad).astype(BF)
    stats_of(stat_ref, (grad * update, grad_in, grad_in * normed))


def middle(place, own, near, far, update, tok, cot, mod, lat, after=()):
    rows, width = own.shape
    mine = whole((rows, width))
    return call(
        functools.partial(middle_kernel, lat), "middle", [place], (1,),
        [own, near, far, update, tok, cot, mod],
        [mine, second(rows, width), mine, mine]
        + [own_rows(lat, rows, width)] * 2
        + [whole(mod.shape)],
        [((rows, width), F32), ((rows, width), BF), ((8, width), F32)],
        [mine, mine, whole((8, width))],
        2, after,
    )


def finish_kernel(lat, place_ref, own, near, far, upd_ref, tok_ref, cot_ref, mod_ref, bias_ref, out_ref, stat_ref):
    width = upd_ref.shape[1]
    row = lambda j: mod_ref[lat : lat + 1, j * width : (j + 1) * width]
    update = own[...] + near[...] + far[...].astype(F32) + bias_ref[...].astype(F32)
    stream = tok_ref[0].astype(F32) + row(0) * upd_ref[...]
    out_ref[...] = (stream + row(3) * update).astype(BF)
    stats_of(stat_ref, (cot_ref[0].astype(F32) * update,))


def finish(place, own, near, far, update, tok, cot, mod, bias, lat, after=()):
    rows, width = own.shape
    mine = whole((rows, width))
    return call(
        functools.partial(finish_kernel, lat), "finish", [place], (1,),
        [own, near, far, update, tok, cot, mod, bias],
        [mine, second(rows, width), mine, mine]
        + [own_rows(lat, rows, width)] * 2
        + [whole(mod.shape), whole((1, width))],
        [((rows, width), BF), ((8, width), F32)],
        [mine, whole((8, width))],
        2, after,
    )


def last_kernel(lat, place_ref, own, near, far, g_ref, tok_ref, mod_ref, out_ref):
    width = g_ref.shape[1]
    grad_in = own[...] + near[...] + far[...].astype(F32)
    normed, inverse = normalize(tok_ref[0].astype(F32))
    scale = 1.0 + mod_ref[lat : lat + 1, width : 2 * width]
    out_ref[...] = g_ref[...] + norm_back(grad_in * scale, normed, inverse)


def last(place, own, near, far, grad, tok, mod, lat, after=()):
    rows, width = own.shape
    mine = whole((rows, width))
    return call(
        functools.partial(last_kernel, lat), "grad_tokens", [place], (1,),
        [own, near, far, grad, tok, mod],
        [mine, second(rows, width), mine, mine, own_rows(lat, rows, width), whole(mod.shape)],
        [((rows, width), F32)],
        [mine],
        2, after,
    )[0]


def place_rows(pos_ref, send_ref, keep_ref, first, values, tiles):
    rows = send_ref.shape[0] * 2 // tiles
    for t in range(values.shape[0] // rows):
        pos = pos_ref[first + t]
        part = values[t * rows : (t + 1) * rows]

        @pl.when(pos < tiles // 2)
        def _():
            send_ref[pl.ds(pl.multiple_of(pos * rows, rows), rows), :] = part.astype(BF)

        @pl.when(pos >= tiles // 2)
        def _():
            keep_ref[pl.ds(pl.multiple_of((pos - tiles // 2) * rows, rows), rows), :] = part


def weight_kernel(tiles, lats, pos_ref, *refs):
    send_ref, keep_ref = refs[-2:]
    rows = send_ref.shape[0] * 2 // tiles
    total = None
    for l in range(lats):
        right = refs[lats + l]
        value = right[...] if len(right.shape) == 2 else jnp.concatenate([right[j] for j in range(3)], 1)
        part = dot(refs[l][...], value, ROWS)
        total = part if total is None else total + part
    first = pl.program_id(0) * (refs[0].shape[1] // rows)
    place_rows(pos_ref, send_ref, keep_ref, first, total, tiles)


def weight_grad(pos, lefts, rights, name, after=(), steps=4):
    tiles = pos.shape[0]
    seq, depth = lefts[0].shape
    shape = rights[0].shape
    width = shape[1] if len(shape) == 2 else shape[0] * shape[2]
    block = depth // steps
    half = (depth // 2, width)
    return call(
        functools.partial(weight_kernel, tiles, len(lefts)), name, [pos], (steps,),
        [*lefts, *rights],
        [pl.BlockSpec((seq, block), lambda i, o: (0, i))] * len(lefts) + [whole(shape)] * len(rights),
        [(half, BF), (half, F32)],
        [whole(half)] * 2,
        width / 128, after,
    )


def proj_grad_kernel(tiles, quarter, lats, order_ref, pos_ref, *refs):
    mixed, pieces, (send_ref, keep_ref) = refs[:lats], refs[lats:-2], refs[-2:]
    total = None
    for lat in range(lats):
        for j in range(4):
            rows = pl.ds(pl.multiple_of(order_ref[j] * quarter, quarter), quarter)
            part = dot(mixed[lat][rows, :], pieces[4 * lat + j][...], ROWS)
            total = part if total is None else total + part
    place_rows(pos_ref, send_ref, keep_ref, 0, total.T, tiles)


def proj_grad(order, pos, mixed, pieces, after=()):
    tiles = pos.shape[0]
    quarter, width = pieces[0][0].shape
    cols = mixed[0].shape[1]
    args = list(mixed) + [p for four in pieces for p in four]
    half = (width // 2, cols)
    return call(
        functools.partial(proj_grad_kernel, tiles, quarter, len(mixed)), "proj_grad", [order, pos], (1,),
        args,
        [whole(a.shape) for a in args],
        [(half, BF), (half, F32)],
        [whole(half)] * 2,
        4, after,
    )


def back_step(i, near_ref, pieces, p_ref, q_ref, k_ref, v_ref, total_ref, low_ref, bias_ref, dk_acc, dv_acc):
    rows, cols = q_ref.shape
    heads = cols // HEAD_DIM

    @pl.when(i == 0)
    def _():
        dk_acc[...] = jnp.zeros_like(dk_acc)
        dv_acc[...] = jnp.zeros_like(dv_acc)

    @pl.when(i < 4)
    def _():
        update = pieces[3][...]
        for j in (2, 1, 0):
            update = jnp.where(i == j, pieces[j][...], update)
        grad = dot(update, p_ref[...], COLS).astype(BF)
        q = spread(q_ref[...] * BF(SCALE), heads)
        g = spread(grad, heads)
        k, v = k_ref[...], v_ref[...]
        probs = jnp.exp(dot(k, q, COLS) - total_ref[0])
        grad_probs = dot(v, g, COLS)
        inner = jnp.sum(probs * grad_probs, axis=0, keepdims=True)
        scores = (probs * (grad_probs - inner)).astype(BF)
        dv_acc[...] += dot(probs.astype(BF), g)
        dk_acc[...] += dot(scores, q)
        dq = gather_heads(dot(scores, k, ROWS), heads) * SCALE
        low_ref[0, pl.ds(pl.multiple_of(near_ref[i] * rows, rows), rows), :] = dq.astype(BF)

    @pl.when(i == 3)
    def _():
        low_ref[1] = dk_acc[...].astype(BF)
        low_ref[2] = dv_acc[...].astype(BF)
        bias_ref[...] = jnp.zeros_like(bias_ref)
        for j in range(3):
            bias_ref[j : j + 1] = jnp.sum(low_ref[j].astype(F32), axis=0, keepdims=True)


def back_kernel(near_ref, u0, u1, u2, u3, p_ref, q_ref, k_ref, v_ref, total_ref, low_ref, bias_ref, dk_acc, dv_acc):
    back_step(
        pl.program_id(0), near_ref, (u0, u1, u2, u3), p_ref, q_ref, k_ref, v_ref, total_ref, low_ref, bias_ref,
        dk_acc, dv_acc,
    )


def back_end_kernel(
    lat, near_ref, order_ref, u0, u1, u2, u3, p_ref, q_ref, k_ref, v_ref, total_ref, other_ref, w_ref, tok_ref,
    low_ref, bias_ref, send_ref, far_ref, own_ref, stat_ref, dk_acc, dv_acc,
):
    i = pl.program_id(0)
    rows = q_ref.shape[0]
    back_step(
        i, near_ref, (u0, u1, u2, u3), p_ref, q_ref, k_ref, v_ref, total_ref, low_ref, bias_ref, dk_acc, dv_acc
    )

    @pl.when(i == 0)
    def _():
        stat_ref[...] = jnp.zeros_like(stat_ref)

    @pl.when(i >= 4)
    def _():
        here = pl.ds(pl.multiple_of(order_ref[jnp.maximum(i - 4, 0)] * rows, rows), rows)
        out = None
        for j in range(3):
            both = jnp.concatenate([other_ref[j, here, :], low_ref[j, here, :]], 1)
            part = dot(both, w_ref[j], COLS)
            out = part if out is None else out + part
        normed, _ = normalize(tok_ref[0].astype(F32))
        stat_ref[0:1] += jnp.sum(out, axis=0, keepdims=True)
        stat_ref[1:2] += jnp.sum(out * normed, axis=0, keepdims=True)
        place_quarter(i - 4, out, send_ref, far_ref, own_ref)


def attend_back(near, order, pieces, proj, q, k, v, total, part, lat, end=None, after=()):
    seq, cols = q.shape
    cols = cols // 2
    width = proj.shape[1]
    block = seq // 4
    heads = cols // HEAD_DIM
    first = lambda i, n, *_: n[jnp.minimum(i, 3)]
    later = lambda i, n, o: o[jnp.maximum(i - 4, 0)]
    keys = pl.BlockSpec((seq, cols), lambda *_: (0, part))
    ins = [*pieces, proj, q, k, v, total]
    in_specs = [whole((block, width))] * 4 + [
        pl.BlockSpec((cols, width), lambda *_: (part, 0)),
        pl.BlockSpec((block, cols), lambda *a: (first(*a), part)),
        keys,
        keys,
        pl.BlockSpec((1, 1, heads * block), lambda *a: (first(*a), 0, part)),
    ]
    outs = [((3, seq, cols), BF), ((8, cols), F32)]
    out_specs = [whole((3, seq, cols)), whole((8, cols))]
    scratch = [pltpu.VMEM((seq, cols), F32)] * 2
    if end is None:
        return call(
            back_kernel, "attend_backward", [near], (4,), ins, in_specs, outs, out_specs, 10, after, scratch
        )
    other, w3, tok = end
    quarter = ((block, width), F32)
    return call(
        functools.partial(back_end_kernel, lat), "attend_backward_end", [near, order], (8,),
        ins + [other, w3, tok],
        in_specs
        + [whole(other.shape), whole(w3.shape)]
        + [pl.BlockSpec((1, block, width), lambda *a: (lat, later(*a), 0))],
        outs + [((2 * block, width), F32), quarter, quarter, ((8, width), F32)],
        out_specs
        + [
            pl.BlockSpec((block, width), lambda i, *_: (jnp.clip(i - 4, 0, 1), 0)),
            whole((block, width)),
            whole((block, width)),
            whole((8, width)),
        ],
        17, after, scratch,
    )


def tie(value, *others):
    return lax.optimization_barrier((value, *others))[0]


def far_kernel(far_ref, near_ref, out_ref):
    out_ref[...] = (far_ref[...] + near_ref[...]).astype(BF)


def far_sum(far, near, after=()):
    rows, width = far.shape
    block = pl.BlockSpec((rows, width), lambda i: (0, 0))
    return call(
        far_kernel, "far_sum", [], (1,), [far, near], [block, block], [((rows, width), BF)], [block], 1, after
    )[0]


def fold_kernel(*refs):
    count = len(refs) // 4
    for j in range(count):
        keep, got, send, kept = refs[2 * j], refs[2 * j + 1], refs[2 * count + 2 * j], refs[2 * count + 2 * j + 1]
        half = kept.shape[0]
        send[...] = (keep[:half] + got[:half].astype(F32)).astype(BF)
        kept[...] = keep[half:] + got[half:].astype(F32)


def fold(pairs, after=()):
    ins = [a for pair in pairs for a in pair]
    outs = []
    for keep, _ in pairs:
        half = (keep.shape[0] // 2, keep.shape[1])
        outs += [(half, BF), (half, F32)]
    got = call(
        fold_kernel, "fold", [], (1,), ins, [whole(a.shape) for a in ins], outs, [whole(o[0]) for o in outs], 2, after
    )
    return [(got[2 * j], got[2 * j + 1]) for j in range(len(pairs))]


def close_kernel(turn, keep_ref, got_ref, out_ref):
    out = keep_ref[...] + got_ref[...].astype(F32)
    out_ref[...] = out.T if turn else out


def close(keep, got, turn=False, after=()):
    shape = keep.shape[::-1] if turn else keep.shape
    return call(
        functools.partial(close_kernel, turn), "close", [], (1,),
        [keep, got], [whole(keep.shape)] * 2, [(shape, F32)], [whole(shape)], 1, after,
    )[0]


def end_sum(keep, got, bits, turn=False, after=()):
    for bit in bits:
        ((send, keep),) = fold([(keep, got)])
        got = swap(send, "dp", bit)
    return close(keep, got, turn, after)


def pieces_of(own, far):
    return own, far, swap(own, "tensor", 1), swap(far, "tensor", 1)


def dp_bits(size):
    return [1 << i for i in range(size.bit_length() - 1)]


def row_places(index, size, bits):
    away = jnp.arange(size, dtype=jnp.int32) ^ index
    place = jnp.zeros((size,), jnp.int32)
    for bit in bits:
        place = 2 * place + 1 - (away // bit) % 2
    return place


def shards(
    tokens,
    condition,
    modulation_weight,
    modulation_bias,
    qkv_weight,
    qv_bias,
    proj_weight,
    proj_bias,
    up_weight,
    up_bias,
    down_weight,
    down_bias,
    cotangent,
):
    seq, lats, width = tokens.shape
    place = lax.axis_index("tensor")
    index = lax.axis_index("dp")
    size = lax.axis_size("dp")
    quarter = seq // 4
    mod_cols = modulation_weight.shape[1] // 4
    order = jnp.array(SEND_FIRST, jnp.int32) ^ place
    near = jnp.array(NEAR_FIRST, jnp.int32) ^ place
    here = place[None]
    bits = dp_bits(size)
    other_bits = [bits[1], bits[0]] + bits[2:]
    places, other_places = row_places(index, size, bits), row_places(index, size, other_bits)
    to_dp = lambda value, bit: swap(value, "dp", bit)
    core = lambda value: swap(value, "tensor", 1)
    chip = lambda value: swap(value, "tensor", 2)

    proj_far = chip(proj_weight)
    cond = condition.astype(F32)
    silu_low = jax.nn.silu(cond).astype(BF)
    mod_bias = modulation_bias[None]
    mod_one = modulate(silu_low, modulation_weight, mod_bias, 0, 2)
    w3 = jnp.transpose(qkv_weight, (1, 0, 2))
    heads = w3.shape[2]
    tok = jnp.transpose(tokens, (1, 0, 2))

    in0, *qkv0 = project(tok, mod_one, w3, qv_bias, 0)
    mixed0, total0 = attend(*qkv0, quarter)
    mixed_far0 = chip(mixed0)
    in1, *qkv1 = project(tok, mod_one, w3, qv_bias, 1, [mixed0])
    mixed1, total1 = attend(*qkv1, quarter)
    mixed_far1 = chip(mixed1)
    cot = jnp.transpose(tie(cotangent, mixed1), (1, 0, 2))
    mod_two = modulate(silu_low, modulation_weight, mod_bias, 2, 4, [mixed1])
    proj = pieces_of(proj_weight, tie(proj_far, mixed1))
    gathered0 = pieces_of(mixed0, tie(mixed_far0, mixed1))

    feed_args = (proj, proj_bias[None], tok, cot, mod_two, up_weight, up_bias[None], down_weight)
    low0, hid0, pre0, gm0, upd0, send0, far0, own0, ub0, db0 = feed(order, gathered0, *feed_args, 0)
    near0 = core(send0)
    gathered1 = pieces_of(mixed1, tie(mixed_far1, own0))
    down0 = feed_down(order, hid0, down_weight)
    sum0 = far_sum(far0, tie(near0, down0[1]))
    grad_far0 = chip(sum0)
    low1, hid1, pre1, gm1, upd1, send1, far1, own1, ub1, db1 = feed(
        order, gathered1, *feed_args, 1, [sum0]
    )
    near1 = core(send1)
    mid_args = (tok, cot, mod_two)
    g0, u0, stat0 = middle(here, own0, near0, tie(grad_far0, own1), upd0, *mid_args, 0, [own1])
    u_far0 = chip(u0)
    down1 = feed_down(order, hid1, down_weight, [u0])
    sum1 = far_sum(far1, tie(near1, down1[1]))
    grad_far1 = chip(sum1)
    up_send, up_keep = weight_grad(places, [low0, low1], [pre0, pre1], "up_grad", [sum1])
    up_got = to_dp(up_send, bits[0])
    pieces0 = pieces_of(u0, tie(u_far0, up_keep))
    down_send, down_keep = weight_grad(other_places, [gm0, gm1], [hid0, hid1], "down_grad", [up_keep])
    down_got = to_dp(down_send, other_bits[0])
    g1, u1, stat1 = middle(here, own1, near1, tie(grad_far1, down_keep), upd1, *mid_args, 1, [down_keep])
    u_far1 = chip(u1)

    half0 = attend_back(near, order, pieces0, proj_weight, *qkv0, total0, 0, 0, None, [u1])
    mlp_near0, mlp_near1 = core(tie(down0[0], u1)), core(tie(down1[0], u1))
    mlp_sum0 = far_sum(down0[1], tie(mlp_near0, half0[1]))
    mlp_sum1 = far_sum(down1[1], tie(mlp_near1, half0[1]))
    mlp_far0, mlp_far1 = chip(mlp_sum0), chip(mlp_sum1)
    rest0 = attend_back(
        near, order, pieces0, proj_weight, *qkv0, total0, 1, 0, (half0[0], w3, tok), [mlp_sum0, mlp_sum1]
    )
    in_near0 = core(rest0[2])
    pieces1 = pieces_of(u1, tie(u_far1, rest0[1]))
    (up_send, up_keep), (down_send, down_keep) = fold(
        [(up_keep, tie(up_got, rest0[1])), (down_keep, tie(down_got, rest0[1]))]
    )
    up_got, down_got = to_dp(up_send, bits[1]), to_dp(down_send, other_bits[1])
    in_sum0 = far_sum(rest0[3], tie(in_near0, up_keep))
    in_far0 = chip(in_sum0)
    proj_send, proj_keep = proj_grad(
        near, other_places, [mixed0, mixed1], [pieces0, pieces1], [in_sum0]
    )
    proj_got = to_dp(proj_send, other_bits[0])
    half1 = attend_back(near, order, pieces1, proj_weight, *qkv1, total1, 0, 1, None, [proj_keep])
    first_send, first_keep = weight_grad(places, [in0, in1], [half0[0], half1[0]], "qkv_grad", [half1[1]])
    first_got = to_dp(first_send, bits[0])
    after = first_keep
    (up_send, up_keep), (down_send, down_keep), (proj_send, proj_keep) = fold(
        [
            (up_keep, tie(up_got, after)),
            (down_keep, tie(down_got, after)),
            (proj_keep, tie(proj_got, after)),
        ]
    )
    up_got, down_got = to_dp(up_send, bits[2]), to_dp(down_send, other_bits[2])
    proj_got = to_dp(proj_send, other_bits[1])
    out0, gate0 = finish(
        here, down0[2], mlp_near0, tie(mlp_far0, after), upd0, *mid_args, down_bias[None], 0, [up_keep]
    )
    out1, gate1 = finish(
        here, down1[2], mlp_near1, tie(mlp_far1, after), upd1, *mid_args, down_bias[None], 1, [up_keep]
    )
    rest1 = attend_back(
        near, order, pieces1, proj_weight, *qkv1, total1, 1, 1, (half1[0], w3, tok), [gate0, gate1]
    )

    in_near1 = core(rest1[2])
    second_send, second_keep = weight_grad(
        other_places, [in0, in1], [rest0[0], rest1[0]], "qkv_grad", [rest1[1]]
    )
    second_got = to_dp(second_send, other_bits[0])
    in_sum1 = far_sum(rest1[3], tie(in_near1, second_keep))
    in_far1 = chip(in_sum1)
    mod = jnp.concatenate(
        [
            jnp.concatenate([rest[5][:2], stat[:3], gate[:1]]).reshape(1, -1)
            for rest, stat, gate in ((rest0, stat0, gate0), (rest1, stat1, gate1))
        ]
    )
    mod = tie(mod, in_sum1)
    mod = mod + core(mod)
    mod = mod + chip(mod)
    after = second_keep
    (first_send, first_keep), (proj_send, proj_keep) = fold(
        [(first_keep, tie(first_got, after)), (proj_keep, tie(proj_got, after))], [in_sum1]
    )
    first_got, proj_got = to_dp(first_send, bits[1]), to_dp(proj_send, other_bits[2])
    up_shard = end_sum(up_keep, tie(up_got, first_keep), bits[3:])
    down_shard = end_sum(down_keep, tie(down_got, first_keep), bits[3:], True)
    grad_tokens0 = last(here, rest0[4], in_near0, tie(in_far0, first_keep), g0, tok, mod_one, 0)
    grad_modulation = mod.astype(BF)
    own_cols = lax.dynamic_slice_in_dim(grad_modulation, place * mod_cols, mod_cols, 1)
    own_weight = lax.dynamic_slice_in_dim(modulation_weight, place * mod_cols, mod_cols, 1)
    grad_silu = dot(own_cols, own_weight, COLS)
    grad_silu = grad_silu + core(grad_silu)
    grad_silu = grad_silu + chip(grad_silu)
    grad_condition = jax.vjp(jax.nn.silu, cond)[1](grad_silu)[0]

    (second_send, second_keep), (first_send, first_keep) = fold(
        [(second_keep, second_got), (first_keep, first_got)], [grad_tokens0]
    )
    second_got, first_got = to_dp(second_send, other_bits[1]), to_dp(first_send, bits[2])
    grad_tokens1 = last(here, rest1[4], in_near1, in_far1, g1, tok, mod_one, 1, [second_keep])
    proj_shard = end_sum(proj_keep, tie(proj_got, second_keep), bits[3:], True)
    ((second_send, second_keep),) = fold([(second_keep, second_got)], [grad_tokens1])
    second_got = to_dp(second_send, other_bits[2])
    qkv_shard = jnp.concatenate(
        [
            part.reshape(part.shape[0], 3, -1)
            for part in (end_sum(first_keep, first_got, bits[3:]), end_sum(second_keep, second_got, bits[3:]))
        ],
        2,
    )

    q_sums = jnp.concatenate([half0[1] + half1[1], rest0[1] + rest1[1]], 1)
    update_sum = sum(jnp.sum(p, axis=0, dtype=F32) for p in pieces0 + pieces1)
    biases = jnp.concatenate([(ub0 + ub1)[0], (db0 + db1)[0], update_sum, q_sums[0], q_sums[2]])
    gathered = jnp.concatenate([silu_low.astype(F32), own_cols.astype(F32)], 1)
    for bit in bits:
        other = swap(jnp.concatenate([gathered.reshape(-1), biases]), "dp", bit)
        theirs = other[: gathered.size].reshape(gathered.shape)
        biases = biases + other[gathered.size :]
        low = (index // bit) % 2 == 0
        gathered = jnp.concatenate(
            [jnp.where(low, gathered, theirs), jnp.where(low, theirs, gathered)], 0
        )
    all_silu = gathered[:, :width].astype(BF)
    all_cols = gathered[:, width:].astype(BF)
    mod_rows = width // size
    my_silu = lax.dynamic_slice_in_dim(all_silu, index * mod_rows, mod_rows, 1)
    mod_shard = dot(my_silu, all_cols, ROWS)
    mod_bias_sum = jnp.sum(all_cols, axis=0, dtype=F32)
    ff = up_weight.shape[1]
    ends = [ff, ff + width, ff + 2 * width, ff + 2 * width + heads]
    up_bias_sum, down_bias_sum, proj_bias_sum, q_sum, v_sum = jnp.split(biases, ends)
    return (
        jnp.stack([out0, out1], 1),
        jnp.stack([grad_tokens0, grad_tokens1], 1),
        grad_condition,
        mod_shard,
        mod_bias_sum,
        qkv_shard,
        jnp.stack([q_sum, v_sum]),
        proj_shard,
        proj_bias_sum,
        up_shard,
        up_bias_sum,
        down_shard,
        down_bias_sum,
    )


def solution(mesh):
    in_specs = (
        P(None, "dp", None),
        P("dp", None),
        P(),
        P(),
        P(None, None, "tensor"),
        P(None, "tensor"),
        P("tensor", None),
        P(),
        P(None, "tensor"),
        P("tensor"),
        P("tensor", None),
        P(),
        P(None, "dp", None),
    )
    out_specs = (
        P("tensor", "dp", None),
        P("tensor", "dp", None),
        P("dp", None),
        P("dp", "tensor"),
        P("tensor"),
        P("dp", None, "tensor"),
        P(None, "tensor"),
        P("tensor", "dp"),
        P(),
        P("dp", "tensor"),
        P("tensor"),
        P("tensor", "dp"),
        P(),
    )
    return jax.shard_map(shards, mesh=mesh, in_specs=in_specs, out_specs=out_specs, check_vma=False)
```

```python
import functools

import jax
import jax.numpy as jnp
from jax import lax
from jax.experimental import pallas as pl
from jax.experimental.pallas import tpu as pltpu
from jax.sharding import PartitionSpec as P

HEAD_DIM = 64
EPS = 1e-06
BF = jnp.bfloat16
F32 = jnp.float32
ROWS = ((0,), (0,))
COLS = ((1,), (1,))
MIB = 1 << 20
SCALE = HEAD_DIM**-0.5
SEND_FIRST = (3, 1, 2, 0)
NEAR_FIRST = (0, 2, 1, 3)
LIMITS = {
    "modulate": 60,
    "project": 14,
    "attend_forward": 10,
    "feed": 24,
    "feed_down": 14,
    "far_sum": 8,
    "middle": 20,
    "up_grad": 24,
    "down_grad": 24,
    "qkv_grad": 16,
    "proj_grad": 24,
    "fold": 24,
    "attend_backward": 16,
    "attend_backward_end": 24,
    "finish": 32,
    "grad_tokens": 32,
}


def dot(left, right, dims=((1,), (0,))):
    return lax.dot_general(left, right, (dims, ((), ())), preferred_element_type=F32)


def swap(value, axis, bit):
    pairs = [(i, i ^ bit) for i in range(lax.axis_size(axis))]
    return lax.ppermute(value, axis, pairs)


def normalize(values):
    centre = values - jnp.mean(values, axis=-1, keepdims=True)
    inverse = lax.rsqrt(jnp.mean(centre * centre, axis=-1, keepdims=True) + EPS)
    return centre * inverse, inverse


def norm_back(grad, normed, inverse):
    return inverse * (
        grad
        - jnp.mean(grad, axis=-1, keepdims=True)
        - normed * jnp.mean(grad * normed, axis=-1, keepdims=True)
    )


def gelu_pair(v):
    root = 0.7978845608028654
    square = v * v
    inner = jnp.tanh(v * (root + (root * 0.044715) * square))
    half = 0.5 + 0.5 * inner
    slope = half + (0.5 * v) * (1.0 - inner * inner) * (root + (3 * root * 0.044715) * square)
    return v * half, slope


def head_lanes(rows, cols, h):
    return lax.broadcasted_iota(jnp.int32, (rows, cols), 1) // HEAD_DIM == h


def spread(x, heads):
    rows, cols = x.shape
    zero = jnp.zeros_like(x)
    return jnp.concatenate([jnp.where(head_lanes(rows, cols, h), x, zero) for h in range(heads)], 0)


def gather_heads(x, heads):
    rows, cols = x.shape[0] // heads, x.shape[1]
    out = x[:rows]
    for h in range(1, heads):
        out = jnp.where(head_lanes(rows, cols, h), x[h * rows : (h + 1) * rows], out)
    return out


def whole(shape):
    return pl.BlockSpec(shape, lambda *_: (0,) * len(shape))


def shape_of(shape, dtype):
    return jax.ShapeDtypeStruct(shape, dtype)


def cost(expected):
    return pl.CostEstimate(flops=int(expected * 1.15e10), bytes_accessed=0, transcendentals=0)


ANY = pl.BlockSpec(memory_space=pl.ANY)


def call(kernel, name, scalars, grid, ins, in_specs, outs, out_specs, expected, after=(), scratch=()):
    skip = len(after)

    def body(*refs):
        first = len(scalars)
        kernel(*refs[:first], *refs[first + skip :])

    return pl.pallas_call(
        body,
        out_shape=[shape_of(*o) for o in outs],
        grid_spec=pltpu.PrefetchScalarGridSpec(
            num_scalar_prefetch=len(scalars),
            grid=grid,
            in_specs=[ANY] * skip + in_specs,
            out_specs=out_specs,
            scratch_shapes=list(scratch),
        ),
        compiler_params=pltpu.CompilerParams(vmem_limit_bytes=LIMITS.get(name, 16) * MIB),
        cost_estimate=cost(expected),
        name=name,
    )(*scalars, *after, *ins)


def modulate_kernel(cond_ref, w_ref, bias_ref, out_ref):
    out_ref[...] = dot(cond_ref[...], w_ref[...]) + bias_ref[...].astype(F32)


def modulate(cond, weight, bias, first, count, after=()):
    lats, width = cond.shape
    return call(
        modulate_kernel, "modulate", [], (count,),
        [cond, weight, bias],
        [
            whole(cond.shape),
            pl.BlockSpec((width, width), lambda i: (0, first + i)),
            pl.BlockSpec((1, width), lambda i: (0, first + i)),
        ],
        [((lats, count * width), F32)],
        [pl.BlockSpec((lats, width), lambda i: (0, i))],
        count / 2, after,
    )[0]


def project_kernel(lat, tok_ref, mod_ref, w_ref, bias_ref, in_ref, q_ref, k_ref, v_ref):
    width = tok_ref.shape[2]
    row = lambda j: mod_ref[lat : lat + 1, j * width : (j + 1) * width]
    normed, _ = normalize(tok_ref[0].astype(F32))
    low = (normed * (1.0 + row(1)) + row(0)).astype(BF)
    in_ref[...] = low
    q_ref[...] = (dot(low, w_ref[0]) + bias_ref[0:1].astype(F32)).astype(BF)
    k_ref[...] = dot(low, w_ref[1]).astype(BF)
    v_ref[...] = (dot(low, w_ref[2]) + bias_ref[1:2].astype(F32)).astype(BF)


def project(tok, mod, w3, bias, lat, after=(), block=512):
    _, seq, width = tok.shape
    cols = w3.shape[2]
    rows = lambda n: pl.BlockSpec((block, n), lambda i: (i, 0))
    return call(
        functools.partial(project_kernel, lat), "project", [], (seq // block,),
        [tok, mod, w3, bias],
        [pl.BlockSpec((1, block, width), lambda i: (lat, i, 0))] + [whole(a.shape) for a in (mod, w3, bias)],
        [((seq, width), BF)] + [((seq, cols), BF)] * 3,
        [rows(width), rows(cols), rows(cols), rows(cols)],
        3, after,
    )


def attend_kernel(q_ref, k_ref, v_ref, mixed_ref, total_ref):
    rows, cols = q_ref.shape
    q, k, v = q_ref[...] * BF(SCALE), k_ref[...], v_ref[...]
    out = None
    for h in range(cols // HEAD_DIM):
        mine = head_lanes(rows, cols, h)
        scores = dot(jnp.where(mine, q, jnp.zeros_like(q)), k, COLS)
        largest = jnp.max(scores, axis=1, keepdims=True)
        powers = jnp.exp(scores - largest)
        total = jnp.sum(powers, axis=1, keepdims=True)
        part = dot((powers * (1.0 / total)).astype(BF), v)
        out = part if out is None else jnp.where(mine, part, out)
        log_total = jnp.broadcast_to(largest + jnp.log(total), (rows, 128))
        total_ref[0, :, h * rows : (h + 1) * rows] = log_total.T[:1]
    mixed_ref[...] = out.astype(BF)


def attend(q, k, v, block, after=()):
    seq, cols = q.shape
    heads = cols // HEAD_DIM
    rows = pl.BlockSpec((block, cols), lambda i: (i, 0))
    return call(
        attend_kernel, "attend_forward", [], (seq // block,),
        [q, k, v],
        [rows, whole((seq, cols)), whole((seq, cols))],
        [((seq, cols), BF), ((seq // block, 1, heads * block), F32)],
        [rows, pl.BlockSpec((1, 1, heads * block), lambda i: (i, 0, 0))],
        8, after,
    )


def halves(block, width):
    return [
        pl.BlockSpec((block, width), lambda i, *_: (jnp.minimum(i, 1), 0)),
        whole((block, width)),
        whole((block, width)),
    ]


def place_quarter(step, value, send_ref, far_ref, own_ref):
    @pl.when(step < 2)
    def _():
        send_ref[...] = value

    @pl.when(step == 2)
    def _():
        far_ref[...] = value

    @pl.when(step == 3)
    def _():
        own_ref[...] = value


def feed_kernel(
    lat, order_ref, m0, m1, m2, m3, p0, p1, p2, p3, pb_ref, tok_ref, cot_ref, mod_ref, up_ref, ub_ref, down_ref,
    in_ref, hid_ref, pre_ref, gm_ref, upd_ref, tok_out, cot_out, send_ref, far_ref, own_ref, gub_ref, gdb_ref,
):
    i = pl.program_id(0)
    width = tok_ref.shape[2]
    row = lambda j: mod_ref[lat : lat + 1, j * width : (j + 1) * width]
    update = pb_ref[...].astype(F32)
    for m, p in ((m0, p0), (m1, p1), (m2, p2), (m3, p3)):
        update = update + dot(m[...], p[...])
    normed, _ = normalize(tok_ref[0].astype(F32) + row(0) * update)
    low = (normed * (1.0 + row(2)) + row(1)).astype(BF)
    in_ref[...] = low
    act, slope = gelu_pair(dot(low, up_ref[...]) + ub_ref[...].astype(F32))
    hid_ref[...] = act.astype(BF)
    grad_mlp = (row(3) * cot_ref[0].astype(F32)).astype(BF)
    gm_ref[...] = grad_mlp
    grad_pre = (dot(grad_mlp, down_ref[...], COLS) * slope).astype(BF)
    pre_ref[...] = grad_pre
    place_quarter(i, dot(grad_pre, up_ref[...], COLS), send_ref, far_ref, own_ref)

    @pl.when(i == 3)
    def _():
        upd_ref[...] = update
        tok_out[...] = tok_ref[0]
        cot_out[...] = cot_ref[0]

    @pl.when(i == 0)
    def _():
        gub_ref[...] = jnp.zeros_like(gub_ref)
        gdb_ref[...] = jnp.zeros_like(gdb_ref)

    gub_ref[...] += jnp.sum(grad_pre.astype(F32), axis=0, keepdims=True)
    gdb_ref[...] += jnp.sum(grad_mlp.astype(F32), axis=0, keepdims=True)


def feed(order, mixed, proj, proj_bias, tok, cot, mod, up, up_bias, down, lat, after=()):
    _, seq, width = tok.shape
    block = seq // 4
    ff = up.shape[1]
    cols = mixed[0].shape[1]
    at = lambda n: pl.BlockSpec((block, n), lambda i, o: (o[i], 0))
    at3 = pl.BlockSpec((1, block, width), lambda i, o: (lat, o[i], 0))
    quarter = ((block, width), F32)
    return call(
        functools.partial(feed_kernel, lat), "feed", [order], (4,),
        [*mixed, *proj, proj_bias, tok, cot, mod, up, up_bias, down],
        [at(cols)] * 4
        + [whole((cols, width))] * 4
        + [whole((1, width)), at3, at3, whole(mod.shape)]
        + [whole(up.shape), whole((1, ff)), whole(down.shape)],
        [((seq, width), BF), ((seq, ff), BF), ((seq, ff), BF), ((seq, width), BF), quarter]
        + [((block, width), BF)] * 2
        + [((2 * block, width), F32), quarter, quarter, ((1, ff), F32), ((1, width), F32)],
        [at(width), at(ff), at(ff), at(width)]
        + [whole((block, width))] * 3
        + halves(block, width)
        + [whole((1, ff)), whole((1, width))],
        18, after,
    )


def down_kernel(order_ref, hid_ref, down_ref, send_ref, far_ref, own_ref):
    out = dot(hid_ref[...], down_ref[...])
    place_quarter(pl.program_id(0), out, send_ref, far_ref, own_ref)


def feed_down(order, hidden, down, after=()):
    seq, ff = hidden.shape
    width = down.shape[1]
    block = seq // 4
    quarter = ((block, width), F32)
    return call(
        down_kernel, "feed_down", [order], (4,),
        [hidden, down],
        [pl.BlockSpec((block, ff), lambda i, o: (o[i], 0)), whole(down.shape)],
        [((2 * block, width), F32), quarter, quarter],
        halves(block, width),
        5, after,
    )


def second(rows, width):
    return pl.BlockSpec((rows, width), lambda i: (1, 0))


def stats_of(ref, values):
    ref[...] = jnp.zeros_like(ref)
    for j, value in enumerate(values):
        ref[j : j + 1] = jnp.sum(value, axis=0, keepdims=True)


def middle_kernel(lat, own, near, far, upd_ref, tok_ref, cot_ref, mod_ref, g_ref, low_ref, stat_ref):
    width = upd_ref.shape[1]
    row = lambda j: mod_ref[lat : lat + 1, j * width : (j + 1) * width]
    grad_in = own[...] + near[...] + far[...].astype(F32)
    update = upd_ref[...]
    normed, inverse = normalize(tok_ref[...].astype(F32) + row(0) * update)
    grad = cot_ref[...].astype(F32) + norm_back(grad_in * (1.0 + row(2)), normed, inverse)
    g_ref[...] = grad
    low = (row(0) * grad).astype(BF)
    low_ref[...] = low
    stats_of(stat_ref, (grad * update, grad_in, grad_in * normed, low.astype(F32)))


def middle(own, near, far, update, tok, cot, mod, lat, after=()):
    rows, width = own.shape
    mine = whole((rows, width))
    return call(
        functools.partial(middle_kernel, lat), "middle", [], (1,),
        [own, near, far, update, tok, cot, mod],
        [mine, second(rows, width)] + [mine] * 4 + [whole(mod.shape)],
        [((rows, width), F32), ((rows, width), BF), ((8, width), F32)],
        [mine, mine, whole((8, width))],
        2, after,
    )


def finish_kernel(*refs):
    mod_ref, bias_ref, out_ref, stat_ref = refs[-4:]
    width = mod_ref.shape[1] // 4
    stat_ref[...] = jnp.zeros_like(stat_ref)
    for lat in range(2):
        own, near, far, upd, tok, cot = refs[6 * lat : 6 * lat + 6]
        row = lambda j: mod_ref[lat : lat + 1, j * width : (j + 1) * width]
        update = own[...] + near[...] + far[...].astype(F32) + bias_ref[...].astype(F32)
        stream = tok[...].astype(F32) + row(0) * upd[...]
        out_ref[:, lat, :] = (stream + row(3) * update).astype(BF)
        total = jnp.sum(cot[...].astype(F32) * update, axis=0, keepdims=True)
        stat_ref[lat : lat + 1] = total


def finish(first, other, mod, bias, after=()):
    rows, width = first[0].shape
    mine = whole((rows, width))
    one = [mine, second(rows, width)] + [mine] * 4
    return call(
        finish_kernel, "finish", [], (1,),
        [*first, *other, mod, bias],
        one + one + [whole(mod.shape), whole((1, width))],
        [((rows, 2, width), BF), ((8, width), F32)],
        [whole((rows, 2, width)), whole((8, width))],
        4, after,
    )


def last_kernel(*refs):
    mod_ref, out_ref = refs[-2:]
    width = mod_ref.shape[1] // 2
    for lat in range(2):
        own, near, far, g_ref, tok = refs[5 * lat : 5 * lat + 5]
        grad_in = own[...] + near[...] + far[...].astype(F32)
        normed, inverse = normalize(tok[...].astype(F32))
        scale = 1.0 + mod_ref[lat : lat + 1, width : 2 * width]
        out_ref[:, lat, :] = g_ref[...] + norm_back(grad_in * scale, normed, inverse)


def last(first, other, mod, after=()):
    rows, width = first[0].shape
    mine = whole((rows, width))
    one = [mine, second(rows, width)] + [mine] * 3
    return call(
        last_kernel, "grad_tokens", [], (1,),
        [*first, *other, mod],
        one + one + [whole(mod.shape)],
        [((rows, 2, width), F32)],
        [whole((rows, 2, width))],
        4, after,
    )[0]


def pack_kernel(rest0, mid0, rest1, mid1, gate, out_ref):
    out_ref[...] = jnp.zeros_like(out_ref)
    for lat, (rest, mid) in enumerate(((rest0, mid0), (rest1, mid1))):
        out_ref[8 * lat : 8 * lat + 2] = rest[0:2]
        out_ref[8 * lat + 2 : 8 * lat + 5] = mid[0:3]
        out_ref[8 * lat + 5 : 8 * lat + 6] = gate[lat : lat + 1]
        out_ref[8 * lat + 6 : 8 * lat + 7] = mid[3:4]


def pack(arrays, after=()):
    width = arrays[0].shape[1]
    return call(
        pack_kernel, "pack", [], (1,), arrays, [whole(a.shape) for a in arrays],
        [((16, width), F32)], [whole((16, width))], 1, after,
    )[0]


def message_kernel(place_ref, mine, theirs, silu, ub0, ub1, db0, db1, half0, rest0, half1, rest1, out_ref, low_ref):
    width = mine.shape[1]
    total = mine[...] + theirs[...]
    low_ref[...] = total.astype(BF).astype(F32)
    out_ref[...] = jnp.zeros_like(out_ref)
    unit = width // 2
    for lat in range(2):
        out_ref[lat : lat + 1, :width] = silu[lat : lat + 1, :].astype(F32)
        for t in range(3):
            at = 3 * place_ref[0] + t
            cols = pl.ds(pl.multiple_of(lax.rem(at, 2) * unit, unit), unit)
            out_ref[lat : lat + 1, width + t * unit : width + (t + 1) * unit] = low_ref[
                pl.ds(8 * lat + lax.div(at, 2), 1), cols
            ]
    ff = ub0.shape[1]
    heads = half0.shape[1]
    out_ref[2:3, :ff] = ub0[...] + ub1[...]
    out_ref[2:3, ff : ff + width] = db0[...] + db1[...]
    at = ff + width
    for j in (0, 2):
        for one, other in ((half0, half1), (rest0, rest1)):
            out_ref[2:3, at : at + heads] = one[j : j + 1] + other[j : j + 1]
            at += heads
    out_ref[3:4, :width] = total[6:7] + total[14:15]


def message(place, arrays, after=()):
    width = arrays[0].shape[1]
    ff, heads = arrays[3].shape[1], arrays[7].shape[1]
    shape = (4, max(width + 3 * (width // 2), ff + width + 4 * heads))
    return call(
        message_kernel, "message", [place], (1,), arrays, [whole(a.shape) for a in arrays],
        [(shape, F32), ((16, width), F32)], [whole(shape), whole((16, width))], 1, after,
    )


def join_kernel(mine, theirs, out_ref):
    rows = mine.shape[0] - 2
    out_ref[:rows] = mine[:rows]
    out_ref[rows : 2 * rows] = theirs[:rows]
    out_ref[2 * rows :] = mine[rows:] + theirs[rows:]


def join(mine, theirs, after=()):
    shape = (2 * mine.shape[0] - 2, mine.shape[1])
    return call(
        join_kernel, "join", [], (1,), [mine, theirs], [whole(mine.shape)] * 2,
        [(shape, F32)], [whole(shape)], 1, after,
    )[0]


def condition_kernel(low_ref, w_ref, cond_ref, out_ref, acc):
    j = pl.program_id(0)

    @pl.when(j == 0)
    def _():
        acc[...] = jnp.zeros_like(acc)

    rows = jnp.concatenate([low_ref[pl.ds(j, 1), :], low_ref[pl.ds(8 + j, 1), :]], 0)
    acc[...] += dot(rows.astype(BF), w_ref[...], COLS)

    @pl.when(j == pl.num_programs(0) - 1)
    def _():
        cond = cond_ref[...].astype(F32)
        sig = 1.0 / (1.0 + jnp.exp(-cond))
        out_ref[...] = acc[...] * (sig * (1.0 + cond * (1.0 - sig)))


def condition_grad(low, weight, cond, after=()):
    lats, width = cond.shape
    return call(
        condition_kernel, "condition_grad", [], (6,), [low, weight, cond],
        [whole(low.shape), pl.BlockSpec((width, width), lambda i: (0, i)), whole(cond.shape)],
        [((lats, width), F32)], [whole((lats, width))], 5, after, [pltpu.VMEM((lats, width), F32)],
    )[0]


def place_rows(pos_ref, send_ref, keep_ref, first, values, tiles):
    rows = send_ref.shape[0] * 2 // tiles
    for t in range(values.shape[0] // rows):
        pos = pos_ref[first + t]
        part = values[t * rows : (t + 1) * rows]

        @pl.when(pos < tiles // 2)
        def _():
            send_ref[pl.ds(pl.multiple_of(pos * rows, rows), rows), :] = part.astype(BF)

        @pl.when(pos >= tiles // 2)
        def _():
            keep_ref[pl.ds(pl.multiple_of((pos - tiles // 2) * rows, rows), rows), :] = part


def weight_kernel(tiles, lats, pos_ref, *refs):
    send_ref, keep_ref = refs[-2:]
    rows = send_ref.shape[0] * 2 // tiles
    total = None
    for l in range(lats):
        right = refs[lats + l]
        value = right[...] if len(right.shape) == 2 else jnp.concatenate([right[j] for j in range(3)], 1)
        part = dot(refs[l][...], value, ROWS)
        total = part if total is None else total + part
    first = pl.program_id(0) * (refs[0].shape[1] // rows)
    place_rows(pos_ref, send_ref, keep_ref, first, total, tiles)


def weight_grad(pos, lefts, rights, name, after=(), steps=4):
    tiles = pos.shape[0]
    seq, depth = lefts[0].shape
    shape = rights[0].shape
    width = shape[1] if len(shape) == 2 else shape[0] * shape[2]
    block = depth // steps
    half = (depth // 2, width)
    return call(
        functools.partial(weight_kernel, tiles, len(lefts)), name, [pos], (steps,),
        [*lefts, *rights],
        [pl.BlockSpec((seq, block), lambda i, o: (0, i))] * len(lefts) + [whole(shape)] * len(rights),
        [(half, BF), (half, F32)],
        [whole(half)] * 2,
        width / 128, after,
    )


def proj_grad_kernel(tiles, quarter, lats, order_ref, pos_ref, *refs):
    mixed, pieces, (send_ref, keep_ref) = refs[:lats], refs[lats:-2], refs[-2:]
    total = None
    for lat in range(lats):
        for j in range(4):
            rows = pl.ds(pl.multiple_of(order_ref[j] * quarter, quarter), quarter)
            part = dot(mixed[lat][rows, :], pieces[4 * lat + j][...], ROWS)
            total = part if total is None else total + part
    place_rows(pos_ref, send_ref, keep_ref, 0, total.T, tiles)


def proj_grad(order, pos, mixed, pieces, after=()):
    tiles = pos.shape[0]
    quarter, width = pieces[0][0].shape
    cols = mixed[0].shape[1]
    args = list(mixed) + [p for four in pieces for p in four]
    half = (width // 2, cols)
    return call(
        functools.partial(proj_grad_kernel, tiles, quarter, len(mixed)), "proj_grad", [order, pos], (1,),
        args,
        [whole(a.shape) for a in args],
        [(half, BF), (half, F32)],
        [whole(half)] * 2,
        4, after,
    )


def back_step(i, near_ref, pieces, p_ref, q_ref, k_ref, v_ref, total_ref, low_ref, bias_ref, dk_acc, dv_acc):
    rows, cols = q_ref.shape
    heads = cols // HEAD_DIM

    @pl.when(i == 0)
    def _():
        dk_acc[...] = jnp.zeros_like(dk_acc)
        dv_acc[...] = jnp.zeros_like(dv_acc)

    @pl.when(i < 4)
    def _():
        update = pieces[3][...]
        for j in (2, 1, 0):
            update = jnp.where(i == j, pieces[j][...], update)
        grad = dot(update, p_ref[...], COLS).astype(BF)
        q = spread(q_ref[...] * BF(SCALE), heads)
        g = spread(grad, heads)
        k, v = k_ref[...], v_ref[...]
        probs = jnp.exp(dot(k, q, COLS) - total_ref[0])
        grad_probs = dot(v, g, COLS)
        inner = jnp.sum(probs * grad_probs, axis=0, keepdims=True)
        scores = (probs * (grad_probs - inner)).astype(BF)
        dv_acc[...] += dot(probs.astype(BF), g)
        dk_acc[...] += dot(scores, q)
        dq = gather_heads(dot(scores, k, ROWS), heads) * SCALE
        low_ref[0, pl.ds(pl.multiple_of(near_ref[i] * rows, rows), rows), :] = dq.astype(BF)

    @pl.when(i == 3)
    def _():
        low_ref[1] = dk_acc[...].astype(BF)
        low_ref[2] = dv_acc[...].astype(BF)
        bias_ref[...] = jnp.zeros_like(bias_ref)
        for j in range(3):
            bias_ref[j : j + 1] = jnp.sum(low_ref[j].astype(F32), axis=0, keepdims=True)


def back_kernel(near_ref, u0, u1, u2, u3, p_ref, q_ref, k_ref, v_ref, total_ref, low_ref, bias_ref, dk_acc, dv_acc):
    back_step(
        pl.program_id(0), near_ref, (u0, u1, u2, u3), p_ref, q_ref, k_ref, v_ref, total_ref, low_ref, bias_ref,
        dk_acc, dv_acc,
    )


def back_end_kernel(
    lat, near_ref, order_ref, u0, u1, u2, u3, p_ref, q_ref, k_ref, v_ref, total_ref, other_ref, w_ref, tok_ref,
    low_ref, bias_ref, send_ref, far_ref, own_ref, stat_ref, dk_acc, dv_acc,
):
    i = pl.program_id(0)
    rows = q_ref.shape[0]
    back_step(
        i, near_ref, (u0, u1, u2, u3), p_ref, q_ref, k_ref, v_ref, total_ref, low_ref, bias_ref, dk_acc, dv_acc
    )

    @pl.when(i == 0)
    def _():
        stat_ref[...] = jnp.zeros_like(stat_ref)

    @pl.when(i >= 4)
    def _():
        here = pl.ds(pl.multiple_of(order_ref[jnp.maximum(i - 4, 0)] * rows, rows), rows)
        out = None
        for j in range(3):
            both = jnp.concatenate([other_ref[j, here, :], low_ref[j, here, :]], 1)
            part = dot(both, w_ref[j], COLS)
            out = part if out is None else out + part
        normed, _ = normalize(tok_ref[0].astype(F32))
        stat_ref[0:1] += jnp.sum(out, axis=0, keepdims=True)
        stat_ref[1:2] += jnp.sum(out * normed, axis=0, keepdims=True)
        place_quarter(i - 4, out, send_ref, far_ref, own_ref)


def attend_back(near, order, pieces, proj, q, k, v, total, part, lat, end=None, after=()):
    seq, cols = q.shape
    cols = cols // 2
    width = proj.shape[1]
    block = seq // 4
    heads = cols // HEAD_DIM
    first = lambda i, n, *_: n[jnp.minimum(i, 3)]
    later = lambda i, n, o: o[jnp.maximum(i - 4, 0)]
    keys = pl.BlockSpec((seq, cols), lambda *_: (0, part))
    ins = [*pieces, proj, q, k, v, total]
    in_specs = [whole((block, width))] * 4 + [
        pl.BlockSpec((cols, width), lambda *_: (part, 0)),
        pl.BlockSpec((block, cols), lambda *a: (first(*a), part)),
        keys,
        keys,
        pl.BlockSpec((1, 1, heads * block), lambda *a: (first(*a), 0, part)),
    ]
    outs = [((3, seq, cols), BF), ((8, cols), F32)]
    out_specs = [whole((3, seq, cols)), whole((8, cols))]
    scratch = [pltpu.VMEM((seq, cols), F32)] * 2
    if end is None:
        return call(
            back_kernel, "attend_backward", [near], (4,), ins, in_specs, outs, out_specs, 10, after, scratch
        )
    other, w3, tok = end
    quarter = ((block, width), F32)
    return call(
        functools.partial(back_end_kernel, lat), "attend_backward_end", [near, order], (8,),
        ins + [other, w3, tok],
        in_specs
        + [whole(other.shape), whole(w3.shape)]
        + [pl.BlockSpec((1, block, width), lambda *a: (lat, later(*a), 0))],
        outs + [((2 * block, width), F32), quarter, quarter, ((8, width), F32)],
        out_specs
        + [
            pl.BlockSpec((block, width), lambda i, *_: (jnp.clip(i - 4, 0, 1), 0)),
            whole((block, width)),
            whole((block, width)),
            whole((8, width)),
        ],
        17, after, scratch,
    )


def tie(value, *others):
    return lax.optimization_barrier((value, *others))[0]


def far_kernel(far_ref, near_ref, out_ref):
    out_ref[...] = (far_ref[...] + near_ref[...]).astype(BF)


def far_sum(far, near, after=()):
    rows, width = far.shape
    block = pl.BlockSpec((rows, width), lambda i: (0, 0))
    return call(
        far_kernel, "far_sum", [], (1,), [far, near], [block, block], [((rows, width), BF)], [block], 1, after
    )[0]


def fold_kernel(*refs):
    count = len(refs) // 4
    for j in range(count):
        keep, got, send, kept = refs[2 * j], refs[2 * j + 1], refs[2 * count + 2 * j], refs[2 * count + 2 * j + 1]
        half = kept.shape[0]
        send[...] = (keep[:half] + got[:half].astype(F32)).astype(BF)
        kept[...] = keep[half:] + got[half:].astype(F32)


def fold(pairs, after=()):
    ins = [a for pair in pairs for a in pair]
    outs = []
    for keep, _ in pairs:
        half = (keep.shape[0] // 2, keep.shape[1])
        outs += [(half, BF), (half, F32)]
    got = call(
        fold_kernel, "fold", [], (1,), ins, [whole(a.shape) for a in ins], outs, [whole(o[0]) for o in outs], 2, after
    )
    return [(got[2 * j], got[2 * j + 1]) for j in range(len(pairs))]


def close_kernel(turn, keep_ref, got_ref, out_ref):
    out = keep_ref[...] + got_ref[...].astype(F32)
    out_ref[...] = out.T if turn else out


def close(keep, got, turn=False, after=()):
    shape = keep.shape[::-1] if turn else keep.shape
    return call(
        functools.partial(close_kernel, turn), "close", [], (1,),
        [keep, got], [whole(keep.shape)] * 2, [(shape, F32)], [whole(shape)], 1, after,
    )[0]


def end_sum(keep, got, bits, turn=False, after=()):
    for bit in bits:
        ((send, keep),) = fold([(keep, got)])
        got = swap(send, "dp", bit)
    return close(keep, got, turn, after)


def pieces_of(own, far):
    return own, far, swap(own, "tensor", 1), swap(far, "tensor", 1)


def dp_bits(size):
    return [1 << i for i in range(size.bit_length() - 1)]


def row_places(index, size, bits):
    away = jnp.arange(size, dtype=jnp.int32) ^ index
    place = jnp.zeros((size,), jnp.int32)
    for bit in bits:
        place = 2 * place + 1 - (away // bit) % 2
    return place


def shards(
    tokens,
    condition,
    modulation_weight,
    modulation_bias,
    qkv_weight,
    qv_bias,
    proj_weight,
    proj_bias,
    up_weight,
    up_bias,
    down_weight,
    down_bias,
    cotangent,
):
    seq, lats, width = tokens.shape
    place = lax.axis_index("tensor")
    index = lax.axis_index("dp")
    size = lax.axis_size("dp")
    quarter = seq // 4
    mod_cols = modulation_weight.shape[1] // 4
    order = jnp.array(SEND_FIRST, jnp.int32) ^ place
    near = jnp.array(NEAR_FIRST, jnp.int32) ^ place
    here = place[None]
    bits = dp_bits(size)
    other_bits = [bits[1], bits[0]] + bits[2:]
    places, other_places = row_places(index, size, bits), row_places(index, size, other_bits)
    to_dp = lambda value, bit: swap(value, "dp", bit)
    core = lambda value: swap(value, "tensor", 1)
    chip = lambda value: swap(value, "tensor", 2)

    proj_far = chip(proj_weight)
    cond = condition.astype(F32)
    silu_low = jax.nn.silu(cond).astype(BF)
    mod_bias = modulation_bias[None]
    mod_one = modulate(silu_low, modulation_weight, mod_bias, 0, 2)
    w3 = jnp.transpose(qkv_weight, (1, 0, 2))
    heads = w3.shape[2]
    tok = jnp.transpose(tokens, (1, 0, 2))

    in0, *qkv0 = project(tok, mod_one, w3, qv_bias, 0)
    mixed0, total0 = attend(*qkv0, quarter, [proj_far])
    mixed_far0 = chip(mixed0)
    in1, *qkv1 = project(tok, mod_one, w3, qv_bias, 1, [mixed0])
    mixed1, total1 = attend(*qkv1, quarter)
    mixed_far1 = chip(mixed1)
    cot = jnp.transpose(tie(cotangent, mixed1), (1, 0, 2))
    mod_two = modulate(silu_low, modulation_weight, mod_bias, 2, 4, [mixed1])
    proj = pieces_of(proj_weight, tie(proj_far, mixed1))
    gathered0 = pieces_of(mixed0, tie(mixed_far0, mixed1))

    feed_args = (proj, proj_bias[None], tok, cot, mod_two, up_weight, up_bias[None], down_weight)
    low0, hid0, pre0, gm0, upd0, tok0, cot0, send0, far0, own0, ub0, db0 = feed(order, gathered0, *feed_args, 0)
    near0 = core(send0)
    gathered1 = pieces_of(mixed1, tie(mixed_far1, own0))
    down0 = feed_down(order, hid0, down_weight)
    sum0 = far_sum(far0, tie(near0, down0[1]))
    grad_far0 = chip(sum0)
    low1, hid1, pre1, gm1, upd1, tok1, cot1, send1, far1, own1, ub1, db1 = feed(
        order, gathered1, *feed_args, 1, [sum0]
    )
    near1 = core(send1)
    g0, u0, stat0 = middle(own0, near0, tie(grad_far0, own1), upd0, tok0, cot0, mod_two, 0, [own1])
    u_far0 = chip(u0)
    down1 = feed_down(order, hid1, down_weight, [u0])
    sum1 = far_sum(far1, tie(near1, down1[1]))
    grad_far1 = chip(sum1)
    up_send, up_keep = weight_grad(places, [low0, low1], [pre0, pre1], "up_grad", [sum1])
    up_got = to_dp(up_send, bits[0])
    pieces0 = pieces_of(u0, tie(u_far0, up_keep))
    down_send, down_keep = weight_grad(other_places, [gm0, gm1], [hid0, hid1], "down_grad", [up_keep])
    down_got = to_dp(down_send, other_bits[0])
    g1, u1, stat1 = middle(own1, near1, tie(grad_far1, down_keep), upd1, tok1, cot1, mod_two, 1, [down_keep])
    u_far1 = chip(u1)

    half0 = attend_back(near, order, pieces0, proj_weight, *qkv0, total0, 0, 0, None, [u1])
    mlp_near0, mlp_near1 = core(tie(down0[0], u1)), core(tie(down1[0], u1))
    mlp_sum0 = far_sum(down0[1], tie(mlp_near0, half0[1]))
    mlp_sum1 = far_sum(down1[1], tie(mlp_near1, half0[1]))
    mlp_far0, mlp_far1 = chip(mlp_sum0), chip(mlp_sum1)
    ((up_send, up_keep),) = fold([(up_keep, tie(up_got, half0[1]))])
    up_got = to_dp(up_send, bits[1])
    rest0 = attend_back(
        near, order, pieces0, proj_weight, *qkv0, total0, 1, 0, (half0[0], w3, tok), [mlp_sum0, mlp_sum1, up_keep]
    )
    in_near0 = core(rest0[2])
    pieces1 = pieces_of(u1, tie(u_far1, rest0[1]))
    (up_send, up_keep), (down_send, down_keep) = fold(
        [(up_keep, tie(up_got, rest0[1])), (down_keep, tie(down_got, rest0[1]))]
    )
    up_got, down_got = to_dp(up_send, bits[2]), to_dp(down_send, other_bits[1])
    in_sum0 = far_sum(rest0[3], tie(in_near0, up_keep))
    in_far0 = chip(in_sum0)
    proj_send, proj_keep = proj_grad(
        near, other_places, [mixed0, mixed1], [pieces0, pieces1], [in_sum0]
    )
    proj_got = to_dp(proj_send, other_bits[0])
    half1 = attend_back(near, order, pieces1, proj_weight, *qkv1, total1, 0, 1, None, [proj_keep])
    (down_send, down_keep), (proj_send, proj_keep) = fold(
        [(down_keep, tie(down_got, half1[1])), (proj_keep, tie(proj_got, half1[1]))]
    )
    down_got, proj_got = to_dp(down_send, other_bits[2]), to_dp(proj_send, other_bits[1])
    first_send, first_keep = weight_grad(
        places, [in0, in1], [half0[0], half1[0]], "qkv_grad", [half1[1], proj_keep]
    )
    first_got = to_dp(first_send, bits[0])
    output, gate = finish(
        (down0[2], mlp_near0, tie(mlp_far0, first_keep), upd0, tok0, cot0),
        (down1[2], mlp_near1, tie(mlp_far1, first_keep), upd1, tok1, cot1),
        mod_two, down_bias[None], [first_keep],
    )
    up_shard = end_sum(up_keep, tie(up_got, gate), bits[3:])
    (first_send, first_keep), (proj_send, proj_keep) = fold(
        [(first_keep, tie(first_got, gate)), (proj_keep, tie(proj_got, gate))], [up_shard]
    )
    first_got, proj_got = to_dp(first_send, bits[1]), to_dp(proj_send, other_bits[2])
    rest1 = attend_back(
        near, order, pieces1, proj_weight, *qkv1, total1, 1, 1, (half1[0], w3, tok), [first_keep]
    )

    in_near1 = core(rest1[2])
    mod = pack([rest0[5], stat0, rest1[5], stat1, gate])
    mod_near = core(mod)
    second_send, second_keep = weight_grad(
        other_places, [in0, in1], [rest0[0], rest1[0]], "qkv_grad", [mod]
    )
    second_got = to_dp(second_send, other_bits[0])
    mod = mod + tie(mod_near, second_keep)
    mod_far = chip(mod)
    in_sum1 = far_sum(rest1[3], tie(in_near1, mod))
    in_far1 = chip(in_sum1)
    ((first_send, first_keep),) = fold([(first_keep, tie(first_got, in_sum1))])
    first_got = to_dp(first_send, bits[2])
    note, low_mod = message(
        here,
        [mod, tie(mod_far, first_keep), silu_low, ub0, ub1, db0, db1, half0[1], rest0[1], half1[1], rest1[1]],
    )
    note_got = to_dp(note, bits[0])
    grad_condition = condition_grad(low_mod, modulation_weight, condition, [note])
    down_shard = end_sum(down_keep, tie(down_got, note), other_bits[3:], True)
    note = join(note, tie(note_got, grad_condition))
    note_got = to_dp(note, bits[1])
    ((second_send, second_keep),) = fold([(second_keep, tie(second_got, note))])
    second_got = to_dp(second_send, other_bits[1])
    proj_shard = end_sum(proj_keep, tie(proj_got, second_keep), other_bits[3:], True)
    note = join(note, tie(note_got, second_keep))
    note_got = to_dp(note, bits[2])
    grad_tokens = last(
        (rest0[4], in_near0, tie(in_far0, note), g0, tok0), (rest1[4], in_near1, tie(in_far1, note), g1, tok1), mod_one
    )
    first_shard = end_sum(first_keep, tie(first_got, note), bits[3:])
    ((second_send, second_keep),) = fold([(second_keep, tie(second_got, note))], [grad_tokens])
    second_got = to_dp(second_send, other_bits[2])
    note = join(note, tie(note_got, second_keep))
    for bit in bits[3:]:
        note = join(note, to_dp(note, bit))
    second_shard = end_sum(second_keep, second_got, bits[3:])
    qkv_shard = jnp.concatenate(
        [part.reshape(part.shape[0], 3, -1) for part in (first_shard, second_shard)], 2
    )
    rows = note.shape[0] - 2
    all_silu = note[:rows, :width].astype(BF)
    all_cols = note[:rows, width : width + mod_cols].astype(BF)
    mod_rows = width // size
    my_silu = lax.dynamic_slice_in_dim(all_silu, index * mod_rows, mod_rows, 1)
    mod_shard = dot(my_silu, all_cols, ROWS)
    mod_bias_sum = jnp.sum(all_cols, axis=0, dtype=F32)
    ff = up_weight.shape[1]
    up_bias_sum, down_bias_sum, qv_sum = jnp.split(note[rows, : ff + width + 2 * heads], [ff, ff + width])
    return (
        output,
        grad_tokens,
        grad_condition,
        mod_shard,
        mod_bias_sum,
        qkv_shard,
        qv_sum.reshape(2, heads),
        proj_shard,
        note[rows + 1, :width],
        up_shard,
        up_bias_sum,
        down_shard,
        down_bias_sum,
    )


def solution(mesh):
    in_specs = (
        P(None, "dp", None),
        P("dp", None),
        P(),
        P(),
        P(None, None, "tensor"),
        P(None, "tensor"),
        P("tensor", None),
        P(),
        P(None, "tensor"),
        P("tensor"),
        P("tensor", None),
        P(),
        P(None, "dp", None),
    )
    out_specs = (
        P("tensor", "dp", None),
        P("tensor", "dp", None),
        P("dp", None),
        P("dp", "tensor"),
        P("tensor"),
        P("dp", None, "tensor"),
        P(None, "tensor"),
        P("tensor", "dp"),
        P(),
        P("dp", "tensor"),
        P("tensor"),
        P("tensor", "dp"),
        P(),
    )
    return jax.shard_map(shards, mesh=mesh, in_specs=in_specs, out_specs=out_specs, check_vma=False)
```

```python
import functools

import jax
import jax.numpy as jnp
from jax import lax
from jax.experimental import pallas as pl
from jax.experimental.pallas import tpu as pltpu
from jax.sharding import PartitionSpec as P

HEAD_DIM = 64
EPS = 1e-06
BF = jnp.bfloat16
F32 = jnp.float32
ROWS = ((0,), (0,))
COLS = ((1,), (1,))
MIB = 1 << 20
SCALE = HEAD_DIM**-0.5
SEND_FIRST = (3, 1, 2, 0)
NEAR_FIRST = (0, 2, 1, 3)
LIMITS = {
    "modulate": 54,
    "prepare": 30,
    "attend_forward": 24,
    "feed": 24,
    "feed_down": 14,
    "far_sum": 8,
    "middle": 20,
    "up_grad": 32,
    "down_grad": 32,
    "qkv_grad": 24,
    "proj_grad": 24,
    "fold": 24,
    "attend_backward": 16,
    "attend_backward_end": 24,
    "finish": 32,
    "grad_tokens": 60,
}


def dot(left, right, dims=((1,), (0,))):
    return lax.dot_general(left, right, (dims, ((), ())), preferred_element_type=F32)


def swap(value, axis, bit):
    pairs = [(i, i ^ bit) for i in range(lax.axis_size(axis))]
    return lax.ppermute(value, axis, pairs)


def normalize(values):
    centre = values - jnp.mean(values, axis=-1, keepdims=True)
    inverse = lax.rsqrt(jnp.mean(centre * centre, axis=-1, keepdims=True) + EPS)
    return centre * inverse, inverse


def norm_back(grad, normed, inverse):
    return inverse * (
        grad
        - jnp.mean(grad, axis=-1, keepdims=True)
        - normed * jnp.mean(grad * normed, axis=-1, keepdims=True)
    )


def gelu_pair(v):
    root = 0.7978845608028654
    square = v * v
    inner = jnp.tanh(v * (root + (root * 0.044715) * square))
    half = 0.5 + 0.5 * inner
    slope = half + (0.5 * v) * (1.0 - inner * inner) * (root + (3 * root * 0.044715) * square)
    return v * half, slope


def head_lanes(rows, cols, h):
    return lax.broadcasted_iota(jnp.int32, (rows, cols), 1) // HEAD_DIM == h


def spread(x, heads):
    rows, cols = x.shape
    zero = jnp.zeros_like(x)
    return jnp.concatenate([jnp.where(head_lanes(rows, cols, h), x, zero) for h in range(heads)], 0)


def whole(shape):
    return pl.BlockSpec(shape, lambda *_: (0,) * len(shape))


def shape_of(shape, dtype):
    return jax.ShapeDtypeStruct(shape, dtype)


def cost(expected):
    return pl.CostEstimate(flops=int(expected * 1.15e10), bytes_accessed=0, transcendentals=0)


ANY = pl.BlockSpec(memory_space=pl.ANY)
HBM = "hbm"


def call(kernel, name, scalars, grid, ins, in_specs, outs, out_specs, expected, after=(), scratch=()):
    skip = len(after)

    def body(*refs):
        first = len(scalars)
        kernel(*refs[:first], *refs[first + skip :])

    return pl.pallas_call(
        body,
        out_shape=[pltpu.HBM(*o[:2]) if len(o) > 2 else shape_of(*o) for o in outs],
        grid_spec=pltpu.PrefetchScalarGridSpec(
            num_scalar_prefetch=len(scalars),
            grid=grid,
            in_specs=[ANY] * skip + in_specs,
            out_specs=out_specs,
            scratch_shapes=list(scratch),
        ),
        compiler_params=pltpu.CompilerParams(vmem_limit_bytes=LIMITS.get(name, 16) * MIB),
        cost_estimate=cost(expected),
        name=name,
    )(*scalars, *after, *ins)


def modulate_kernel(cond_ref, w_ref, bias_ref, out_ref):
    out_ref[...] = dot(cond_ref[...], w_ref[...]) + bias_ref[...].astype(F32)[None]


def modulate(cond, weight, bias, first, count, after=()):
    lats, width = cond.shape
    return call(
        modulate_kernel, "modulate", [], (count,),
        [cond, weight, bias],
        [
            whole(cond.shape),
            pl.BlockSpec((width, width), lambda i: (0, first + i)),
            pl.BlockSpec((width,), lambda i: (first + i,)),
        ],
        [((lats, count * width), F32)],
        [pl.BlockSpec((lats, width), lambda i: (0, i))],
        count / 2, after,
    )[0]


def prepare_kernel(tok_ref, mod_ref, w_ref, bias_ref, tok_out, *outs):
    rows, lats, width = tok_ref.shape
    chunk = min(rows, 128)
    both = tok_ref[...].reshape(rows * lats, width)
    here = lax.broadcasted_iota(jnp.int32, (chunk, lats * chunk), 0)
    there = lax.broadcasted_iota(jnp.int32, (chunk, lats * chunk), 1)
    for lat in range(lats):
        pick = jnp.where(there == lats * here + lat, 1.0, 0.0).astype(BF)
        step = lats * chunk
        x = jnp.concatenate([dot(pick, both[j * step : (j + 1) * step]) for j in range(rows // chunk)], 0)
        tok_out[lat] = x.astype(BF)
        row = lambda j: mod_ref[lat : lat + 1, j * width : (j + 1) * width]
        normed, _ = normalize(x)
        low = (normed * (1.0 + row(1)) + row(0)).astype(BF)
        in_ref, q_ref, k_ref, v_ref = outs[4 * lat : 4 * lat + 4]
        in_ref[...] = low
        q_ref[...] = (dot(low, w_ref[0]) + bias_ref[0:1].astype(F32)).astype(BF)
        k_ref[...] = dot(low, w_ref[1]).astype(BF)
        v_ref[...] = (dot(low, w_ref[2]) + bias_ref[1:2].astype(F32)).astype(BF)


def prepare(tokens, mod, w3, bias, after=(), block=256):
    seq, lats, width = tokens.shape
    cols = w3.shape[2]
    rows = lambda n: pl.BlockSpec((block, n), lambda i: (i, 0))
    one = [((seq, width), BF, HBM)] + [((seq, cols), BF, HBM)] * 3
    got = call(
        prepare_kernel, "prepare", [], (seq // block,),
        [tokens, mod, w3, bias],
        [pl.BlockSpec((block, lats, width), lambda i: (i, 0, 0))] + [whole(a.shape) for a in (mod, w3, bias)],
        [((lats, seq, width), BF, HBM)] + one * lats,
        [pl.BlockSpec((lats, block, width), lambda i: (0, i, 0))]
        + [rows(width), rows(cols), rows(cols), rows(cols)] * lats,
        10, after,
    )
    return got[0], got[1:5], got[5:9]


def attend_kernel(q_ref, k_ref, v_ref, mixed_ref, total_ref):
    rows, cols = q_ref.shape
    heads = cols // HEAD_DIM
    value = v_ref[...].T
    scores = dot(k_ref[...], spread(q_ref[...] * BF(SCALE), heads), COLS)
    largest = jnp.max(scores, axis=0, keepdims=True)
    powers = jnp.exp(scores - largest)
    total = jnp.sum(powers, axis=0, keepdims=True)
    probs = (powers * (1.0 / total)).astype(BF)
    out = [
        dot(value[h * HEAD_DIM : (h + 1) * HEAD_DIM], probs[:, h * rows : (h + 1) * rows]) for h in range(heads)
    ]
    mixed_ref[...] = jnp.concatenate(out, 0).T.astype(BF)
    total_ref[0] = largest + jnp.log(total)


def attend(q, k, v, block, after=()):
    seq, cols = q.shape
    heads = cols // HEAD_DIM
    rows = pl.BlockSpec((block, cols), lambda i: (i, 0))
    return call(
        attend_kernel, "attend_forward", [], (seq // block,),
        [q, k, v],
        [rows, whole((seq, cols)), whole((seq, cols))],
        [((seq, cols), BF), ((seq // block, 1, heads * block), F32)],
        [rows, pl.BlockSpec((1, 1, heads * block), lambda i: (i, 0, 0))],
        8, after,
    )


def halves(block, width):
    return [
        pl.BlockSpec((block, width), lambda i, *_: (jnp.minimum(i, 1), 0)),
        whole((block, width)),
        whole((block, width)),
    ]


def place_quarter(step, value, send_ref, far_ref, own_ref):
    @pl.when(step < 2)
    def _():
        send_ref[...] = value

    @pl.when(step == 2)
    def _():
        far_ref[...] = value

    @pl.when(step == 3)
    def _():
        own_ref[...] = value


def feed_kernel(
    lat, order_ref, m0, m1, m2, m3, p0, p1, p2, p3, pb_ref, tok_ref, cot_ref, mod_ref, up_ref, ub_ref, down_ref,
    in_ref, hid_ref, pre_ref, gm_ref, upd_ref, tok_out, cot_out, send_ref, far_ref, own_ref, gub_ref, gdb_ref,
):
    i = pl.program_id(0)
    width = tok_ref.shape[2]
    row = lambda j: mod_ref[lat : lat + 1, j * width : (j + 1) * width]
    update = pb_ref[...].astype(F32)[None]
    for m, p in ((m0, p0), (m1, p1), (m2, p2), (m3, p3)):
        update = update + dot(m[...], p[...])
    normed, _ = normalize(tok_ref[0].astype(F32) + row(0) * update)
    low = (normed * (1.0 + row(2)) + row(1)).astype(BF)
    in_ref[...] = low
    act, slope = gelu_pair(dot(low, up_ref[...]) + ub_ref[...].astype(F32)[None])
    hid_ref[...] = act.astype(BF)
    grad_mlp = (row(3) * cot_ref[0].astype(F32)).astype(BF)
    gm_ref[...] = grad_mlp
    grad_pre = (dot(grad_mlp, down_ref[...], COLS) * slope).astype(BF)
    pre_ref[...] = grad_pre
    place_quarter(i, dot(grad_pre, up_ref[...], COLS), send_ref, far_ref, own_ref)

    @pl.when(i == 3)
    def _():
        upd_ref[...] = update
        tok_out[...] = tok_ref[0]
        cot_out[...] = cot_ref[0]

    @pl.when(i == 0)
    def _():
        gub_ref[...] = jnp.zeros_like(gub_ref)
        gdb_ref[...] = jnp.zeros_like(gdb_ref)

    gub_ref[...] += jnp.sum(grad_pre.astype(F32), axis=0, keepdims=True)
    gdb_ref[...] += jnp.sum(grad_mlp.astype(F32), axis=0, keepdims=True)


def feed(order, mixed, proj, proj_bias, tok, cot, mod, up, up_bias, down, lat, after=()):
    _, seq, width = tok.shape
    block = seq // 4
    ff = up.shape[1]
    cols = mixed[0].shape[1]
    at = lambda n: pl.BlockSpec((block, n), lambda i, o: (o[i], 0))
    at3 = pl.BlockSpec((1, block, width), lambda i, o: (lat, o[i], 0))
    quarter = ((block, width), F32)
    return call(
        functools.partial(feed_kernel, lat), "feed", [order], (4,),
        [*mixed, *proj, proj_bias, tok, cot, mod, up, up_bias, down],
        [at(cols)] * 4
        + [whole((cols, width))] * 4
        + [whole((width,)), at3, at3, whole(mod.shape)]
        + [whole(up.shape), whole((ff,)), whole(down.shape)],
        [((seq, width), BF), ((seq, ff), BF), ((seq, ff), BF), ((seq, width), BF), quarter]
        + [((block, width), BF)] * 2
        + [((2 * block, width), F32), quarter, quarter, ((1, ff), F32), ((1, width), F32)],
        [at(width), at(ff), at(ff), at(width)]
        + [whole((block, width))] * 3
        + halves(block, width)
        + [whole((1, ff)), whole((1, width))],
        18, after,
    )


def down_kernel(order_ref, hid_ref, down_ref, send_ref, far_ref, own_ref):
    out = dot(hid_ref[...], down_ref[...])
    place_quarter(pl.program_id(0), out, send_ref, far_ref, own_ref)


def feed_down(order, hidden, down, after=()):
    seq, ff = hidden.shape
    width = down.shape[1]
    block = seq // 4
    quarter = ((block, width), F32)
    return call(
        down_kernel, "feed_down", [order], (4,),
        [hidden, down],
        [pl.BlockSpec((block, ff), lambda i, o: (o[i], 0)), whole(down.shape)],
        [((2 * block, width), F32), quarter, quarter],
        halves(block, width),
        5, after,
    )


def row_blocks(rows, width, skip=0, steps=1):
    return pl.BlockSpec((rows // steps, width), lambda i: (skip * steps + i, 0))


def add_stats(ref, values, first=0):
    @pl.when(pl.program_id(0) == 0)
    def _():
        ref[first : first + len(values)] = jnp.zeros((len(values), ref.shape[1]), F32)

    for j, value in enumerate(values):
        ref[first + j : first + j + 1] += jnp.sum(value, axis=0, keepdims=True)


def middle_kernel(lat, own, near, far, upd_ref, tok_ref, cot_ref, mod_ref, g_ref, low_ref, stat_ref):
    width = upd_ref.shape[1]
    row = lambda j: mod_ref[lat : lat + 1, j * width : (j + 1) * width]
    grad_in = own[...] + near[...] + far[...].astype(F32)
    update = upd_ref[...]
    normed, inverse = normalize(tok_ref[...].astype(F32) + row(0) * update)
    grad = cot_ref[...].astype(F32) + norm_back(grad_in * (1.0 + row(2)), normed, inverse)
    g_ref[...] = grad
    low = (row(0) * grad).astype(BF)
    low_ref[...] = low
    add_stats(stat_ref, (grad * update, grad_in, grad_in * normed, low.astype(F32)))


def middle(own, near, far, update, tok, cot, mod, lat, after=()):
    rows, width = own.shape
    mine = row_blocks(rows, width)
    return call(
        functools.partial(middle_kernel, lat), "middle", [], (1,),
        [own, near, far, update, tok, cot, mod],
        [mine, row_blocks(rows, width, 1)] + [mine] * 4 + [whole(mod.shape)],
        [((rows, width), F32), ((rows, width), BF), ((4, width), F32)],
        [mine, mine, whole((4, width))],
        2, after,
    )


def finish_kernel(*refs):
    mod_ref, bias_ref, out_ref, stat_ref = refs[-4:]
    width = mod_ref.shape[1] // 4
    for lat in range(2):
        own, near, far, upd, tok, cot = refs[6 * lat : 6 * lat + 6]
        row = lambda j: mod_ref[lat : lat + 1, j * width : (j + 1) * width]
        update = own[...] + near[...] + far[...].astype(F32) + bias_ref[...].astype(F32)[None]
        stream = tok[...].astype(F32) + row(0) * upd[...]
        out_ref[:, lat, :] = (stream + row(3) * update).astype(BF)
        add_stats(stat_ref, (cot[...].astype(F32) * update,), lat)


def finish(first, other, mod, bias, after=()):
    rows, width = first[0].shape
    mine = row_blocks(rows, width)
    one = lambda lat: [mine, row_blocks(rows, width, 1), row_blocks(rows, width, lat)] + [mine] * 3
    return call(
        finish_kernel, "finish", [], (1,),
        [*first, *other, mod, bias],
        one(0) + one(1) + [whole(mod.shape), whole((width,))],
        [((rows, 2, width), BF), ((2, width), F32)],
        [whole((rows, 2, width)), whole((2, width))],
        4, after,
    )


def last_kernel(lat, *refs):
    own, near, far, g_ref, tok, mod_ref = refs[:6]
    out_ref = refs[-1]
    width = mod_ref.shape[1] // 2
    grad_in = own[...] + near[...] + far[...].astype(F32)
    normed, inverse = normalize(tok[...].astype(F32))
    scale = 1.0 + mod_ref[lat : lat + 1, width : 2 * width]
    out = g_ref[...] + norm_back(grad_in * scale, normed, inverse)
    if lat == 0:
        out_ref[...] = out
    else:
        out_ref[:, 0, :] = refs[6][...]
        out_ref[:, 1, :] = out


def last(arrays, mod, lat, other=None, after=()):
    rows, width = arrays[0].shape
    steps = 1 if lat == 0 else 4
    mine = row_blocks(rows, width, 0, steps)
    both = [] if other is None else [other]
    shape, block = (
        ((rows, width), mine) if lat == 0
        else ((rows, 2, width), pl.BlockSpec((rows // steps, 2, width), lambda i: (i, 0, 0)))
    )
    return call(
        functools.partial(last_kernel, lat), "grad_tokens", [], (steps,),
        [*arrays, mod, *both],
        [mine, row_blocks(rows, width, 1, steps)] + [mine] * 3 + [whole(mod.shape)] + [mine] * len(both),
        [(shape, F32) if lat == 0 else (shape, F32, HBM)],
        [block],
        3, after,
    )[0]


def pack_kernel(rest0, mid0, rest1, mid1, gate, out_ref):
    out_ref[...] = jnp.zeros_like(out_ref)
    for lat, (rest, mid) in enumerate(((rest0, mid0), (rest1, mid1))):
        out_ref[8 * lat : 8 * lat + 2] = rest[0:2]
        out_ref[8 * lat + 2 : 8 * lat + 5] = mid[0:3]
        out_ref[8 * lat + 5 : 8 * lat + 6] = gate[lat : lat + 1]
        out_ref[8 * lat + 6 : 8 * lat + 7] = mid[3:4]


def pack(arrays, after=()):
    width = arrays[0].shape[1]
    return call(
        pack_kernel, "pack", [], (1,), arrays, [whole(a.shape) for a in arrays],
        [((16, width), F32)], [whole((16, width))], 1, after,
    )[0]


def message_kernel(place_ref, mine, theirs, silu, ub0, ub1, db0, db1, half0, rest0, half1, rest1, out_ref, low_ref):
    width = mine.shape[1]
    total = mine[...] + theirs[...]
    low_ref[...] = total.astype(BF).astype(F32)
    out_ref[...] = jnp.zeros_like(out_ref)
    unit = width // 2
    for lat in range(2):
        out_ref[lat : lat + 1, :width] = silu[lat : lat + 1, :].astype(F32)
        for t in range(3):
            at = 3 * place_ref[0] + t
            cols = pl.ds(pl.multiple_of(lax.rem(at, 2) * unit, unit), unit)
            out_ref[lat : lat + 1, width + t * unit : width + (t + 1) * unit] = low_ref[
                pl.ds(8 * lat + lax.div(at, 2), 1), cols
            ]
    ff = ub0.shape[1]
    heads = half0.shape[1]
    out_ref[2:3, :ff] = ub0[...] + ub1[...]
    out_ref[2:3, ff : ff + width] = db0[...] + db1[...]
    at = ff + width
    for j in (0, 2):
        for one, other in ((half0, half1), (rest0, rest1)):
            out_ref[2:3, at : at + heads] = one[j : j + 1] + other[j : j + 1]
            at += heads
    out_ref[3:4, :width] = total[6:7] + total[14:15]


def message(place, arrays, after=()):
    width = arrays[0].shape[1]
    ff, heads = arrays[3].shape[1], arrays[7].shape[1]
    shape = (4, max(width + 3 * (width // 2), ff + width + 4 * heads))
    return call(
        message_kernel, "message", [place], (1,), arrays, [whole(a.shape) for a in arrays],
        [(shape, F32), ((16, width), F32)], [whole(shape), whole((16, width))], 1, after,
    )


def join_kernel(mine, theirs, out_ref):
    rows = mine.shape[0] - 2
    out_ref[:rows] = mine[:rows]
    out_ref[rows : 2 * rows] = theirs[:rows]
    out_ref[2 * rows :] = mine[rows:] + theirs[rows:]


def join(mine, theirs, after=()):
    shape = (2 * mine.shape[0] - 2, mine.shape[1])
    return call(
        join_kernel, "join", [], (1,), [mine, theirs], [whole(mine.shape)] * 2,
        [(shape, F32)], [whole(shape)], 1, after,
    )[0]


def condition_kernel(low_ref, w_ref, cond_ref, out_ref, acc):
    j = pl.program_id(0)

    @pl.when(j == 0)
    def _():
        acc[...] = jnp.zeros_like(acc)

    rows = jnp.concatenate([low_ref[pl.ds(j, 1), :], low_ref[pl.ds(8 + j, 1), :]], 0)
    acc[...] += dot(rows.astype(BF), w_ref[...], COLS)

    @pl.when(j == pl.num_programs(0) - 1)
    def _():
        cond = cond_ref[...].astype(F32)
        sig = 1.0 / (1.0 + jnp.exp(-cond))
        out_ref[...] = acc[...] * (sig * (1.0 + cond * (1.0 - sig)))


def condition_grad(low, weight, cond, after=()):
    lats, width = cond.shape
    return call(
        condition_kernel, "condition_grad", [], (6,), [low, weight, cond],
        [whole(low.shape), pl.BlockSpec((width, width), lambda i: (0, i)), whole(cond.shape)],
        [((lats, width), F32)], [whole((lats, width))], 5, after, [pltpu.VMEM((lats, width), F32)],
    )[0]


def place_rows(pos_ref, send_ref, keep_ref, first, values, tiles):
    rows = send_ref.shape[0] * 2 // tiles
    for t in range(values.shape[0] // rows):
        pos = pos_ref[first + t]
        part = values[t * rows : (t + 1) * rows]

        @pl.when(pos < tiles // 2)
        def _():
            send_ref[pl.ds(pl.multiple_of(pos * rows, rows), rows), :] = part.astype(BF)

        @pl.when(pos >= tiles // 2)
        def _():
            keep_ref[pl.ds(pl.multiple_of((pos - tiles // 2) * rows, rows), rows), :] = part


def weight_kernel(tiles, lats, pos_ref, *refs):
    send_ref, keep_ref = refs[-2:]
    rows = send_ref.shape[0] * 2 // tiles
    total = None
    for l in range(lats):
        right = refs[lats + l]
        value = right[...] if len(right.shape) == 2 else jnp.concatenate([right[j] for j in range(3)], 1)
        part = dot(refs[l][...], value, ROWS)
        total = part if total is None else total + part
    first = pl.program_id(0) * (refs[0].shape[1] // rows)
    place_rows(pos_ref, send_ref, keep_ref, first, total, tiles)


def weight_grad(pos, lefts, rights, name, after=(), steps=1):
    tiles = pos.shape[0]
    seq, depth = lefts[0].shape
    shape = rights[0].shape
    width = shape[1] if len(shape) == 2 else shape[0] * shape[2]
    block = depth // steps
    half = (depth // 2, width)
    return call(
        functools.partial(weight_kernel, tiles, len(lefts)), name, [pos], (steps,),
        [*lefts, *rights],
        [pl.BlockSpec((seq, block), lambda i, o: (0, i))] * len(lefts) + [whole(shape)] * len(rights),
        [(half, BF), (half, F32)],
        [whole(half)] * 2,
        width / 128, after,
    )


def proj_grad_kernel(tiles, quarter, lats, order_ref, pos_ref, *refs):
    mixed, pieces, (send_ref, keep_ref) = refs[:lats], refs[lats:-2], refs[-2:]
    total = None
    for lat in range(lats):
        for j in range(4):
            rows = pl.ds(pl.multiple_of(order_ref[j] * quarter, quarter), quarter)
            part = dot(mixed[lat][rows, :], pieces[4 * lat + j][...], ROWS)
            total = part if total is None else total + part
    place_rows(pos_ref, send_ref, keep_ref, 0, total.T, tiles)


def proj_grad(order, pos, mixed, pieces, after=()):
    tiles = pos.shape[0]
    quarter, width = pieces[0][0].shape
    cols = mixed[0].shape[1]
    args = list(mixed) + [p for four in pieces for p in four]
    half = (width // 2, cols)
    return call(
        functools.partial(proj_grad_kernel, tiles, quarter, len(mixed)), "proj_grad", [order, pos], (1,),
        args,
        [whole(a.shape) for a in args],
        [(half, BF), (half, F32)],
        [whole(half)] * 2,
        4, after,
    )


def back_step(i, near_ref, pieces, p_ref, q_ref, k_ref, v_ref, total_ref, low_ref, bias_ref, dk_acc, dv_acc):
    rows, cols = q_ref.shape
    heads = cols // HEAD_DIM

    @pl.when(i == 0)
    def _():
        dk_acc[...] = jnp.zeros_like(dk_acc)
        dv_acc[...] = jnp.zeros_like(dv_acc)

    @pl.when(i < 4)
    def _():
        update = pieces[3][...]
        for j in (2, 1, 0):
            update = jnp.where(i == j, pieces[j][...], update)
        grad = dot(update, p_ref[...], COLS).astype(BF)
        q = spread(q_ref[...] * BF(SCALE), heads)
        g = spread(grad, heads)
        k, v = k_ref[...], v_ref[...]
        probs = jnp.exp(dot(k, q, COLS) - total_ref[0])
        grad_probs = dot(v, g, COLS)
        inner = jnp.sum(probs * grad_probs, axis=0, keepdims=True)
        scores = (probs * (grad_probs - inner)).astype(BF)
        dv_acc[...] += dot(g, probs.astype(BF), ((0,), (1,)))
        dk_acc[...] += dot(q, scores, ((0,), (1,)))
        every = dot(k, scores, ROWS)
        dq = jnp.concatenate(
            [every[h * HEAD_DIM : (h + 1) * HEAD_DIM, h * rows : (h + 1) * rows] for h in range(heads)], 0
        )
        low_ref[0, pl.ds(pl.multiple_of(near_ref[i] * rows, rows), rows), :] = (dq * SCALE).T.astype(BF)

    @pl.when(i == 3)
    def _():
        low_ref[1] = dk_acc[...].T.astype(BF)
        low_ref[2] = dv_acc[...].T.astype(BF)
        bias_ref[...] = jnp.zeros_like(bias_ref)
        for j in range(3):
            bias_ref[j : j + 1] = jnp.sum(low_ref[j].astype(F32), axis=0, keepdims=True)


def back_kernel(near_ref, u0, u1, u2, u3, p_ref, q_ref, k_ref, v_ref, total_ref, low_ref, bias_ref, dk_acc, dv_acc):
    back_step(
        pl.program_id(0), near_ref, (u0, u1, u2, u3), p_ref, q_ref, k_ref, v_ref, total_ref, low_ref, bias_ref,
        dk_acc, dv_acc,
    )


def back_end_kernel(
    lat, near_ref, order_ref, u0, u1, u2, u3, p_ref, q_ref, k_ref, v_ref, total_ref, other_ref, w_ref, tok_ref,
    low_ref, bias_ref, send_ref, far_ref, own_ref, stat_ref, dk_acc, dv_acc,
):
    i = pl.program_id(0)
    rows = q_ref.shape[0]
    back_step(
        i, near_ref, (u0, u1, u2, u3), p_ref, q_ref, k_ref, v_ref, total_ref, low_ref, bias_ref, dk_acc, dv_acc
    )

    @pl.when(i == 0)
    def _():
        stat_ref[...] = jnp.zeros_like(stat_ref)

    @pl.when(i >= 4)
    def _():
        here = pl.ds(pl.multiple_of(order_ref[jnp.maximum(i - 4, 0)] * rows, rows), rows)
        out = None
        for j in range(3):
            both = jnp.concatenate([other_ref[j, here, :], low_ref[j, here, :]], 1)
            part = dot(both, w_ref[j], COLS)
            out = part if out is None else out + part
        normed, _ = normalize(tok_ref[0].astype(F32))
        stat_ref[0:1] += jnp.sum(out, axis=0, keepdims=True)
        stat_ref[1:2] += jnp.sum(out * normed, axis=0, keepdims=True)
        place_quarter(i - 4, out, send_ref, far_ref, own_ref)


def attend_back(near, order, pieces, proj, q, k, v, total, part, lat, end=None, after=()):
    seq, cols = q.shape
    cols = cols // 2
    width = proj.shape[1]
    block = seq // 4
    heads = cols // HEAD_DIM
    first = lambda i, n, *_: n[jnp.minimum(i, 3)]
    later = lambda i, n, o: o[jnp.maximum(i - 4, 0)]
    keys = pl.BlockSpec((seq, cols), lambda *_: (0, part))
    ins = [*pieces, proj, q, k, v, total]
    in_specs = [whole((block, width))] * 4 + [
        pl.BlockSpec((cols, width), lambda *_: (part, 0)),
        pl.BlockSpec((block, cols), lambda *a: (first(*a), part)),
        keys,
        keys,
        pl.BlockSpec((1, 1, heads * block), lambda *a: (first(*a), 0, part)),
    ]
    outs = [((3, seq, cols), BF), ((8, cols), F32)]
    out_specs = [whole((3, seq, cols)), whole((8, cols))]
    scratch = [pltpu.VMEM((cols, seq), F32)] * 2
    if end is None:
        return call(
            back_kernel, "attend_backward", [near], (4,), ins, in_specs, outs, out_specs, 10, after, scratch
        )
    other, w3, tok = end
    quarter = ((block, width), F32)
    return call(
        functools.partial(back_end_kernel, lat), "attend_backward_end", [near, order], (8,),
        ins + [other, w3, tok],
        in_specs
        + [whole(other.shape), whole(w3.shape)]
        + [pl.BlockSpec((1, block, width), lambda *a: (lat, later(*a), 0))],
        outs + [((2 * block, width), F32), quarter, quarter, ((8, width), F32)],
        out_specs
        + [
            pl.BlockSpec((block, width), lambda i, *_: (jnp.clip(i - 4, 0, 1), 0)),
            whole((block, width)),
            whole((block, width)),
            whole((8, width)),
        ],
        17, after, scratch,
    )


def tie(value, *others):
    return lax.optimization_barrier((value, *others))[0]


def far_kernel(*refs):
    out_ref = refs[-1]
    for j in range(len(refs) // 2):
        rows = refs[2 * j].shape[0]
        out_ref[j * rows : (j + 1) * rows] = (refs[2 * j][...] + refs[2 * j + 1][...]).astype(BF)


def far_sum(pairs, after=()):
    rows, width = pairs[0][0].shape
    ins = [a for pair in pairs for a in pair]
    shape = (rows * len(pairs), width)
    block = pl.BlockSpec((rows, width), lambda i: (0, 0))
    return call(
        far_kernel, "far_sum", [], (1,), ins, [block] * len(ins), [(shape, BF)], [whole(shape)], 1, after
    )[0]


def fold_kernel(*refs):
    count = len(refs) // 4
    for j in range(count):
        keep, got, send, kept = refs[2 * j], refs[2 * j + 1], refs[2 * count + 2 * j], refs[2 * count + 2 * j + 1]
        half = kept.shape[0]
        send[...] = (keep[:half] + got[:half].astype(F32)).astype(BF)
        kept[...] = keep[half:] + got[half:].astype(F32)


def fold(pairs, after=()):
    ins = [a for pair in pairs for a in pair]
    outs = []
    for keep, _ in pairs:
        half = (keep.shape[0] // 2, keep.shape[1])
        outs += [(half, BF), (half, F32)]
    got = call(
        fold_kernel, "fold", [], (1,), ins, [whole(a.shape) for a in ins], outs, [whole(o[0]) for o in outs], 2, after
    )
    return [(got[2 * j], got[2 * j + 1]) for j in range(len(pairs))]


def close_kernel(turn, keep_ref, got_ref, out_ref):
    out = keep_ref[...] + got_ref[...].astype(F32)
    out_ref[...] = out.T if turn else out


def close(keep, got, turn=False, after=()):
    shape = keep.shape[::-1] if turn else keep.shape
    return call(
        functools.partial(close_kernel, turn), "close", [], (1,),
        [keep, got], [whole(keep.shape)] * 2, [(shape, F32)], [whole(shape)], 1, after,
    )[0]


def end_sum(keep, got, bits, turn=False, after=()):
    for bit in bits:
        ((send, keep),) = fold([(keep, got)])
        got = swap(send, "dp", bit)
    return close(keep, got, turn, after)


def pieces_of(own, far):
    return own, far, swap(own, "tensor", 1), swap(far, "tensor", 1)


def dp_bits(size):
    return [1 << i for i in range(size.bit_length() - 1)]


def row_places(index, size, bits):
    away = jnp.arange(size, dtype=jnp.int32) ^ index
    place = jnp.zeros((size,), jnp.int32)
    for bit in bits:
        place = 2 * place + 1 - (away // bit) % 2
    return place


def shards(
    tokens,
    condition,
    modulation_weight,
    modulation_bias,
    qkv_weight,
    qv_bias,
    proj_weight,
    proj_bias,
    up_weight,
    up_bias,
    down_weight,
    down_bias,
    cotangent,
):
    seq, lats, width = tokens.shape
    place = lax.axis_index("tensor")
    index = lax.axis_index("dp")
    size = lax.axis_size("dp")
    quarter = seq // 4
    mod_cols = modulation_weight.shape[1] // 4
    order = jnp.array(SEND_FIRST, jnp.int32) ^ place
    near = jnp.array(NEAR_FIRST, jnp.int32) ^ place
    here = place[None]
    bits = dp_bits(size)
    other_bits = [bits[1], bits[0]] + bits[2:]
    places, other_places = row_places(index, size, bits), row_places(index, size, other_bits)
    to_dp = lambda value, bit: swap(value, "dp", bit)
    core = lambda value: swap(value, "tensor", 1)
    chip = lambda value: swap(value, "tensor", 2)

    proj_far = chip(proj_weight)
    cond = condition.astype(F32)
    silu_low = jax.nn.silu(cond).astype(BF)
    mod_one = modulate(silu_low, modulation_weight, modulation_bias, 0, 2)
    w3 = jnp.transpose(qkv_weight, (1, 0, 2))
    heads = w3.shape[2]

    tok, (in0, *qkv0), (in1, *qkv1) = prepare(tokens, mod_one, w3, qv_bias)
    mixed0, total0 = attend(*qkv0, quarter, [proj_far])
    mixed_far0 = chip(mixed0)
    mixed1, total1 = attend(*qkv1, quarter, [mixed0])
    mixed_far1 = chip(mixed1)
    cot = jnp.transpose(tie(cotangent, mixed1), (1, 0, 2))
    mod_two = modulate(silu_low, modulation_weight, modulation_bias, 2, 4, [mixed1])
    proj = pieces_of(proj_weight, tie(proj_far, mixed1))
    gathered0 = pieces_of(mixed0, tie(mixed_far0, mod_two))

    feed_args = (proj, proj_bias, tok, cot, mod_two, up_weight, up_bias, down_weight)
    low0, hid0, pre0, gm0, upd0, tok0, cot0, send0, far0, own0, ub0, db0 = feed(order, gathered0, *feed_args, 0)
    near0 = core(send0)
    gathered1 = pieces_of(mixed1, tie(mixed_far1, own0))
    down0 = feed_down(order, hid0, down_weight)
    sum0 = far_sum([(far0, tie(near0, down0[1]))])
    grad_far0 = chip(sum0)
    low1, hid1, pre1, gm1, upd1, tok1, cot1, send1, far1, own1, ub1, db1 = feed(
        order, gathered1, *feed_args, 1, [sum0]
    )
    near1 = core(send1)
    g0, u0, stat0 = middle(own0, near0, tie(grad_far0, own1), upd0, tok0, cot0, mod_two, 0, [own1])
    u_far0 = chip(u0)
    down1 = feed_down(order, hid1, down_weight, [u0])
    sum1 = far_sum([(far1, tie(near1, down1[1]))])
    grad_far1 = chip(sum1)
    up_send, up_keep = weight_grad(places, [low0, low1], [pre0, pre1], "up_grad", [sum1])
    up_got = to_dp(up_send, bits[0])
    pieces0 = pieces_of(u0, tie(u_far0, up_keep))
    down_send, down_keep = weight_grad(other_places, [gm0, gm1], [hid0, hid1], "down_grad", [up_keep])
    down_got = to_dp(down_send, other_bits[0])
    g1, u1, stat1 = middle(own1, near1, tie(grad_far1, down_keep), upd1, tok1, cot1, mod_two, 1, [down_keep])
    u_far1 = chip(u1)

    half0 = attend_back(near, order, pieces0, proj_weight, *qkv0, total0, 0, 0, None, [u1])
    mlp_near0, mlp_near1 = core(tie(down0[0], u1)), core(tie(down1[0], u1))
    mlp_sum = far_sum([(down0[1], tie(mlp_near0, half0[1])), (down1[1], tie(mlp_near1, half0[1]))])
    mlp_far = chip(mlp_sum)
    ((up_send, up_keep),) = fold([(up_keep, tie(up_got, half0[1]))])
    up_got = to_dp(up_send, bits[1])
    rest0 = attend_back(
        near, order, pieces0, proj_weight, *qkv0, total0, 1, 0, (half0[0], w3, tok), [mlp_sum, up_keep]
    )
    in_near0 = core(rest0[2])
    pieces1 = pieces_of(u1, tie(u_far1, rest0[1]))
    (up_send, up_keep), (down_send, down_keep) = fold(
        [(up_keep, tie(up_got, rest0[1])), (down_keep, tie(down_got, rest0[1]))]
    )
    up_got, down_got = to_dp(up_send, bits[2]), to_dp(down_send, other_bits[1])
    in_sum0 = far_sum([(rest0[3], tie(in_near0, up_keep))])
    in_far0 = chip(in_sum0)
    proj_send, proj_keep = proj_grad(
        near, other_places, [mixed0, mixed1], [pieces0, pieces1], [in_sum0]
    )
    proj_got = to_dp(proj_send, other_bits[0])
    half1 = attend_back(near, order, pieces1, proj_weight, *qkv1, total1, 0, 1, None, [proj_keep])
    first_send, first_keep = weight_grad(places, [in0, in1], [half0[0], half1[0]], "qkv_grad", [half1[1]])
    first_got = to_dp(first_send, bits[0])
    (down_send, down_keep), (proj_send, proj_keep) = fold(
        [(down_keep, tie(down_got, first_keep)), (proj_keep, tie(proj_got, first_keep))]
    )
    down_got, proj_got = to_dp(down_send, other_bits[2]), to_dp(proj_send, other_bits[1])
    output, gate = finish(
        (down0[2], mlp_near0, tie(mlp_far, down_keep), upd0, tok0, cot0),
        (down1[2], mlp_near1, tie(mlp_far, down_keep), upd1, tok1, cot1),
        mod_two, down_bias, [down_keep],
    )
    up_shard = end_sum(up_keep, tie(up_got, gate), bits[3:])
    grad_tokens0 = last((rest0[4], in_near0, tie(in_far0, up_shard), g0, tok0), mod_one, 0)
    (first_send, first_keep), (proj_send, proj_keep) = fold(
        [(first_keep, tie(first_got, grad_tokens0)), (proj_keep, tie(proj_got, grad_tokens0))]
    )
    first_got, proj_got = to_dp(first_send, bits[1]), to_dp(proj_send, other_bits[2])
    rest1 = attend_back(
        near, order, pieces1, proj_weight, *qkv1, total1, 1, 1, (half1[0], w3, tok), [first_keep]
    )

    in_near1 = core(rest1[2])
    mod = pack([rest0[5], stat0, rest1[5], stat1, gate])
    mod_near = core(mod)
    second_send, second_keep = weight_grad(
        other_places, [in0, in1], [rest0[0], rest1[0]], "qkv_grad", [mod]
    )
    second_got = to_dp(second_send, other_bits[0])
    mod = mod + tie(mod_near, second_keep)
    mod_far = chip(mod)
    in_sum1 = far_sum([(rest1[3], tie(in_near1, mod))])
    in_far1 = chip(in_sum1)
    ((first_send, first_keep),) = fold([(first_keep, tie(first_got, in_sum1))])
    first_got = to_dp(first_send, bits[2])
    note, low_mod = message(
        here,
        [mod, tie(mod_far, first_keep), silu_low, ub0, ub1, db0, db1, half0[1], rest0[1], half1[1], rest1[1]],
    )
    note_got = to_dp(note, bits[0])
    down_shard = end_sum(down_keep, tie(down_got, note), other_bits[3:], True)
    ((second_send, second_keep),) = fold([(second_keep, tie(second_got, down_shard))])
    second_got = to_dp(second_send, other_bits[1])
    note = join(note, tie(note_got, second_keep))
    note_got = to_dp(note, bits[1])
    grad_condition = condition_grad(low_mod, modulation_weight, condition, [note])
    ((second_send, second_keep),) = fold([(second_keep, tie(second_got, grad_condition))])
    second_got = to_dp(second_send, other_bits[2])
    note = join(note, tie(note_got, second_keep))
    note_got = to_dp(note, bits[2])
    grad_tokens = last((rest1[4], in_near1, tie(in_far1, note), g1, tok1), mod_one, 1, grad_tokens0)
    proj_shard = end_sum(proj_keep, tie(proj_got, note), other_bits[3:], True)
    first_shard = end_sum(first_keep, tie(first_got, note), bits[3:])
    note = join(note, tie(note_got, grad_tokens))
    for bit in bits[3:]:
        note = join(note, to_dp(note, bit))
    second_shard = end_sum(second_keep, tie(second_got, grad_tokens), bits[3:])
    qkv_shard = jnp.concatenate(
        [part.reshape(part.shape[0], 3, -1) for part in (first_shard, second_shard)], 2
    )
    rows = note.shape[0] - 2
    all_silu = note[:rows, :width].astype(BF)
    all_cols = note[:rows, width : width + mod_cols].astype(BF)
    mod_rows = width // size
    my_silu = lax.dynamic_slice_in_dim(all_silu, index * mod_rows, mod_rows, 1)
    mod_shard = dot(my_silu, all_cols, ROWS)
    mod_bias_sum = jnp.sum(all_cols, axis=0, dtype=F32)
    ff = up_weight.shape[1]
    up_bias_sum, down_bias_sum, qv_sum = jnp.split(note[rows, : ff + width + 2 * heads], [ff, ff + width])
    return (
        output,
        grad_tokens,
        grad_condition,
        mod_shard,
        mod_bias_sum,
        qkv_shard,
        qv_sum.reshape(2, heads),
        proj_shard,
        note[rows + 1, :width],
        up_shard,
        up_bias_sum,
        down_shard,
        down_bias_sum,
    )


def solution(mesh):
    in_specs = (
        P(None, "dp", None),
        P("dp", None),
        P(),
        P(),
        P(None, None, "tensor"),
        P(None, "tensor"),
        P("tensor", None),
        P(),
        P(None, "tensor"),
        P("tensor"),
        P("tensor", None),
        P(),
        P(None, "dp", None),
    )
    out_specs = (
        P("tensor", "dp", None),
        P("tensor", "dp", None),
        P("dp", None),
        P("dp", "tensor"),
        P("tensor"),
        P("dp", None, "tensor"),
        P(None, "tensor"),
        P("tensor", "dp"),
        P(),
        P("dp", "tensor"),
        P("tensor"),
        P("tensor", "dp"),
        P(),
    )
    return jax.shard_map(shards, mesh=mesh, in_specs=in_specs, out_specs=out_specs, check_vma=False)
```

```python
import functools

import jax
import jax.numpy as jnp
from jax import lax
from jax.experimental import pallas as pl
from jax.experimental.pallas import tpu as pltpu
from jax.sharding import PartitionSpec as P

HEAD_DIM = 64
EPS = 1e-06
BF = jnp.bfloat16
F32 = jnp.float32
ROWS = ((0,), (0,))
COLS = ((1,), (1,))
MIB = 1 << 20
SCALE = HEAD_DIM**-0.5
SEND_FIRST = (3, 1, 2, 0)
NEAR_FIRST = (0, 2, 1, 3)
LIMITS = {
    "prepare": 60,
    "attend_forward": 16,
    "feed": 24,
    "feed_down": 14,
    "far_sum": 8,
    "middle": 20,
    "up_grad": 20,
    "down_grad": 20,
    "qkv_grad": 24,
    "first_grad": 40,
    "fold": 24,
    "attend_backward": 20,
    "attend_backward_end": 32,
    "finish": 32,
    "grad_tokens": 60,
}


def dot(left, right, dims=((1,), (0,))):
    return lax.dot_general(left, right, (dims, ((), ())), preferred_element_type=F32)


def swap(value, axis, bit):
    pairs = [(i, i ^ bit) for i in range(lax.axis_size(axis))]
    return lax.ppermute(value, axis, pairs)


def normalize(values):
    centre = values - jnp.mean(values, axis=-1, keepdims=True)
    inverse = lax.rsqrt(jnp.mean(centre * centre, axis=-1, keepdims=True) + EPS)
    return centre * inverse, inverse


def norm_back(grad, normed, inverse):
    return inverse * (
        grad
        - jnp.mean(grad, axis=-1, keepdims=True)
        - normed * jnp.mean(grad * normed, axis=-1, keepdims=True)
    )


def gelu_pair(v):
    root = 0.7978845608028654
    square = v * v
    inner = jnp.tanh(v * (root + (root * 0.044715) * square))
    half = 0.5 + 0.5 * inner
    slope = half + (0.5 * v) * (1.0 - inner * inner) * (root + (3 * root * 0.044715) * square)
    return v * half, slope


def head_lanes(rows, cols, h):
    return lax.broadcasted_iota(jnp.int32, (rows, cols), 1) // HEAD_DIM == h


def spread(x, heads):
    rows, cols = x.shape
    zero = jnp.zeros_like(x)
    return jnp.concatenate([jnp.where(head_lanes(rows, cols, h), x, zero) for h in range(heads)], 0)


def whole(shape):
    return pl.BlockSpec(shape, lambda *_: (0,) * len(shape))


def shape_of(shape, dtype):
    return jax.ShapeDtypeStruct(shape, dtype)


def cost(expected):
    return pl.CostEstimate(flops=int(expected * 1.15e10), bytes_accessed=0, transcendentals=0)


ANY = pl.BlockSpec(memory_space=pl.ANY)
HBM = "hbm"


def call(kernel, name, scalars, grid, ins, in_specs, outs, out_specs, expected, after=(), scratch=()):
    skip = len(after)

    def body(*refs):
        first = len(scalars)
        kernel(*refs[:first], *refs[first + skip :])

    return pl.pallas_call(
        body,
        out_shape=[pltpu.HBM(*o[:2]) if len(o) > 2 else shape_of(*o) for o in outs],
        grid_spec=pltpu.PrefetchScalarGridSpec(
            num_scalar_prefetch=len(scalars),
            grid=grid,
            in_specs=[ANY] * skip + in_specs,
            out_specs=out_specs,
            scratch_shapes=list(scratch),
        ),
        compiler_params=pltpu.CompilerParams(vmem_limit_bytes=LIMITS.get(name, 16) * MIB),
        cost_estimate=cost(expected),
        name=name,
    )(*scalars, *after, *ins)


def silu(cond):
    value = cond.astype(F32)
    return (value * (1.0 / (1.0 + jnp.exp(-value)))).astype(BF)


def modulate(cond_ref, w_ref, bias_ref):
    return dot(silu(cond_ref[...]), w_ref[...]) + bias_ref[...].astype(F32)[None]


def mod_specs(cond, width, first):
    return [
        whole(cond.shape),
        pl.BlockSpec((width, width), lambda i: (0, first(i))),
        pl.BlockSpec((width,), lambda i: (first(i),)),
    ]


def prepare_kernel(tok_ref, w_ref, bias_ref, cond_ref, s_ref, sb_ref, cond_too, t_ref, tb_ref, mod_ref, *outs):
    rows, lats, width = tok_ref.shape

    @pl.when(pl.program_id(0) == 0)
    def _():
        mod_ref[:, :width] = modulate(cond_ref, s_ref, sb_ref)
        mod_ref[:, width:] = modulate(cond_too, t_ref, tb_ref)

    chunk = min(rows, 128)
    both = tok_ref[...].reshape(rows * lats, width)
    here = lax.broadcasted_iota(jnp.int32, (chunk, lats * chunk), 0)
    there = lax.broadcasted_iota(jnp.int32, (chunk, lats * chunk), 1)
    for lat in range(lats):
        pick = jnp.where(there == lats * here + lat, 1.0, 0.0).astype(BF)
        step = lats * chunk
        x = jnp.concatenate([dot(pick, both[j * step : (j + 1) * step]) for j in range(rows // chunk)], 0)
        row = lambda j: mod_ref[lat : lat + 1, j * width : (j + 1) * width]
        normed, _ = normalize(x)
        low = (normed * (1.0 + row(1)) + row(0)).astype(BF)
        tok_out, in_ref, q_ref, k_ref, v_ref = outs[5 * lat : 5 * lat + 5]
        tok_out[...] = x.astype(BF)
        in_ref[...] = low
        q_ref[...] = (dot(low, w_ref[0]) + bias_ref[0:1].astype(F32)).astype(BF)
        k_ref[...] = dot(low, w_ref[1]).astype(BF)
        v_ref[...] = (dot(low, w_ref[2]) + bias_ref[1:2].astype(F32)).astype(BF)


def prepare(tokens, cond, mod_weight, mod_bias, w3, bias, after=(), block=256):
    seq, lats, width = tokens.shape
    cols = w3.shape[2]
    rows = lambda n: pl.BlockSpec((block, n), lambda i: (i, 0))
    one = [((seq, width), BF, HBM)] * 2 + [((seq, cols), BF)] * 3
    got = call(
        prepare_kernel, "prepare", [], (seq // block,),
        [tokens, w3, bias] + [cond, mod_weight, mod_bias] * 2,
        [pl.BlockSpec((block, lats, width), lambda i: (i, 0, 0)), whole(w3.shape), whole(bias.shape)]
        + mod_specs(cond, width, lambda i: 0)
        + mod_specs(cond, width, lambda i: 1),
        [((lats, 2 * width), F32)] + one * lats,
        [whole((lats, 2 * width))] + [rows(width), rows(width), rows(cols), rows(cols), rows(cols)] * lats,
        12, after,
    )
    return got[0], got[1:6], got[6:11]


def attend_kernel(q_ref, k_ref, v_ref, *refs):
    mixed_ref, total_ref = refs[-2:]
    rows, cols = q_ref.shape
    heads = cols // HEAD_DIM
    value = v_ref[...].T
    scores = dot(k_ref[...], spread(q_ref[...] * BF(SCALE), heads), COLS)
    largest = jnp.max(scores, axis=0, keepdims=True)
    powers = jnp.exp(scores - largest)
    total = jnp.sum(powers, axis=0, keepdims=True)
    probs = (powers * (1.0 / total)).astype(BF)
    out = [
        dot(value[h * HEAD_DIM : (h + 1) * HEAD_DIM], probs[:, h * rows : (h + 1) * rows]) for h in range(heads)
    ]
    mixed_ref[...] = jnp.concatenate(out, 0).T.astype(BF)
    total_ref[0] = largest + jnp.log(total)
    if len(refs) > 2:
        cond_ref, w_ref, bias_ref, mod_ref = refs[:4]
        mod_ref[...] = modulate(cond_ref, w_ref, bias_ref)


def attend(q, k, v, block, after=(), mod=None):
    seq, cols = q.shape
    heads = cols // HEAD_DIM
    rows = pl.BlockSpec((block, cols), lambda i: (i, 0))
    ins, in_specs, outs, out_specs = [q, k, v], [rows, whole((seq, cols)), whole((seq, cols))], [], []
    if mod is not None:
        lats, width = mod[0].shape
        ins += mod
        in_specs += mod_specs(mod[0], width, lambda i: 2 + i)
        outs, out_specs = [((lats, 4 * width), F32)], [pl.BlockSpec((lats, width), lambda i: (0, i))]
    return call(
        attend_kernel, "attend_forward", [], (seq // block,), ins, in_specs,
        outs + [((seq, cols), BF), ((seq // block, 1, heads * block), F32)],
        out_specs + [rows, pl.BlockSpec((1, 1, heads * block), lambda i: (i, 0, 0))],
        8, after,
    )


def halves(block, width):
    return [
        pl.BlockSpec((block, width), lambda i, *_: (jnp.minimum(i, 1), 0)),
        whole((block, width)),
        whole((block, width)),
    ]


def place_quarter(step, value, send_ref, far_ref, own_ref):
    @pl.when(step < 2)
    def _():
        send_ref[...] = value

    @pl.when(step == 2)
    def _():
        far_ref[...] = value

    @pl.when(step == 3)
    def _():
        own_ref[...] = value


def feed_kernel(
    lat, order_ref, m0, m1, m2, m3, p0, p1, p2, p3, pb_ref, tok_ref, cot_ref, mod_ref, up_ref, ub_ref, down_ref,
    in_ref, hid_ref, pre_ref, gm_ref, upd_ref, tok_out, cot_out, send_ref, far_ref, own_ref, gub_ref, gdb_ref,
):
    i = pl.program_id(0)
    width = tok_ref.shape[1]
    row = lambda j: mod_ref[lat : lat + 1, j * width : (j + 1) * width]
    update = pb_ref[...].astype(F32)[None]
    for m, p in ((m0, p0), (m1, p1), (m2, p2), (m3, p3)):
        update = update + dot(m[...], p[...])
    normed, _ = normalize(tok_ref[...].astype(F32) + row(0) * update)
    low = (normed * (1.0 + row(2)) + row(1)).astype(BF)
    in_ref[...] = low
    act, slope = gelu_pair(dot(low, up_ref[...]) + ub_ref[...].astype(F32)[None])
    hid_ref[...] = act.astype(BF)
    grad_mlp = (row(3) * cot_ref[0].astype(F32)).astype(BF)
    gm_ref[...] = grad_mlp
    grad_pre = (dot(grad_mlp, down_ref[...], COLS) * slope).astype(BF)
    pre_ref[...] = grad_pre
    place_quarter(i, dot(grad_pre, up_ref[...], COLS), send_ref, far_ref, own_ref)

    @pl.when(i == 3)
    def _():
        upd_ref[...] = update
        tok_out[...] = tok_ref[...]
        cot_out[...] = cot_ref[0]

    @pl.when(i == 0)
    def _():
        gub_ref[...] = jnp.zeros_like(gub_ref)
        gdb_ref[...] = jnp.zeros_like(gdb_ref)

    gub_ref[...] += jnp.sum(grad_pre.astype(F32), axis=0, keepdims=True)
    gdb_ref[...] += jnp.sum(grad_mlp.astype(F32), axis=0, keepdims=True)


def feed(order, mixed, proj, proj_bias, tok, cot, mod, up, up_bias, down, lat, after=()):
    seq, width = tok.shape
    block = seq // 4
    ff = up.shape[1]
    cols = mixed[0].shape[1]
    at = lambda n: pl.BlockSpec((block, n), lambda i, o: (o[i], 0))
    at3 = pl.BlockSpec((1, block, width), lambda i, o: (lat, o[i], 0))
    quarter = ((block, width), F32)
    return call(
        functools.partial(feed_kernel, lat), "feed", [order], (4,),
        [*mixed, *proj, proj_bias, tok, cot, mod, up, up_bias, down],
        [at(cols)] * 4
        + [whole((cols, width))] * 4
        + [whole((width,)), at(width), at3, whole(mod.shape)]
        + [whole(up.shape), whole((ff,)), whole(down.shape)],
        [((seq, width), BF), ((seq, ff), BF), ((seq, ff), BF), ((seq, width), BF), quarter]
        + [((block, width), BF)] * 2
        + [((2 * block, width), F32), quarter, quarter, ((1, ff), F32), ((1, width), F32)],
        [at(width), at(ff), at(ff), at(width)]
        + [whole((block, width))] * 3
        + halves(block, width)
        + [whole((1, ff)), whole((1, width))],
        18, after,
    )


def down_kernel(order_ref, hid_ref, down_ref, send_ref, far_ref, own_ref):
    out = dot(hid_ref[...], down_ref[...])
    place_quarter(pl.program_id(0), out, send_ref, far_ref, own_ref)


def feed_down(order, hidden, down, after=()):
    seq, ff = hidden.shape
    width = down.shape[1]
    block = seq // 4
    quarter = ((block, width), F32)
    return call(
        down_kernel, "feed_down", [order], (4,),
        [hidden, down],
        [pl.BlockSpec((block, ff), lambda i, o: (o[i], 0)), whole(down.shape)],
        [((2 * block, width), F32), quarter, quarter],
        halves(block, width),
        5, after,
    )


def row_blocks(rows, width, skip=0, steps=1):
    return pl.BlockSpec((rows // steps, width), lambda i: (skip * steps + i, 0))


def add_stats(ref, values, first=0):
    @pl.when(pl.program_id(0) == 0)
    def _():
        ref[first : first + len(values)] = jnp.zeros((len(values), ref.shape[1]), F32)

    for j, value in enumerate(values):
        ref[first + j : first + j + 1] += jnp.sum(value, axis=0, keepdims=True)


def middle_kernel(lat, own, near, far, upd_ref, tok_ref, cot_ref, mod_ref, g_ref, low_ref, stat_ref):
    width = upd_ref.shape[1]
    row = lambda j: mod_ref[lat : lat + 1, j * width : (j + 1) * width]
    grad_in = own[...] + near[...] + far[...].astype(F32)
    update = upd_ref[...]
    normed, inverse = normalize(tok_ref[...].astype(F32) + row(0) * update)
    grad = cot_ref[...].astype(F32) + norm_back(grad_in * (1.0 + row(2)), normed, inverse)
    g_ref[...] = grad
    low = (row(0) * grad).astype(BF)
    low_ref[...] = low
    add_stats(stat_ref, (grad * update, grad_in, grad_in * normed, low.astype(F32)))


def middle(own, near, far, update, tok, cot, mod, lat, after=()):
    rows, width = own.shape
    mine = row_blocks(rows, width)
    return call(
        functools.partial(middle_kernel, lat), "middle", [], (1,),
        [own, near, far, update, tok, cot, mod],
        [mine, row_blocks(rows, width, 1)] + [mine] * 4 + [whole(mod.shape)],
        [((rows, width), F32, HBM), ((rows, width), BF), ((4, width), F32)],
        [mine, mine, whole((4, width))],
        2, after,
    )


def finish_kernel(*refs):
    mod_ref, bias_ref, out_ref, stat_ref = refs[-4:]
    width = mod_ref.shape[1] // 4
    for lat in range(2):
        own, near, far, upd, tok, cot = refs[6 * lat : 6 * lat + 6]
        row = lambda j: mod_ref[lat : lat + 1, j * width : (j + 1) * width]
        update = own[...] + near[...] + far[...].astype(F32) + bias_ref[...].astype(F32)[None]
        stream = tok[...].astype(F32) + row(0) * upd[...]
        out_ref[:, lat, :] = (stream + row(3) * update).astype(BF)
        add_stats(stat_ref, (cot[...].astype(F32) * update,), lat)


def finish(first, other, mod, bias, after=()):
    rows, width = first[0].shape
    mine = row_blocks(rows, width)
    one = lambda lat: [mine, row_blocks(rows, width, 1), row_blocks(rows, width, lat)] + [mine] * 3
    return call(
        finish_kernel, "finish", [], (1,),
        [*first, *other, mod, bias],
        one(0) + one(1) + [whole(mod.shape), whole((width,))],
        [((rows, 2, width), BF), ((2, width), F32)],
        [whole((rows, 2, width)), whole((2, width))],
        4, after,
    )


def last_kernel(lat, *refs):
    own, near, far, g_ref, tok, mod_ref = refs[:6]
    out_ref = refs[-1]
    width = mod_ref.shape[1] // 2
    grad_in = own[...] + near[...] + far[...].astype(F32)
    normed, inverse = normalize(tok[...].astype(F32))
    scale = 1.0 + mod_ref[lat : lat + 1, width : 2 * width]
    out = g_ref[...] + norm_back(grad_in * scale, normed, inverse)
    if lat == 0:
        out_ref[...] = out
    else:
        out_ref[:, 0, :] = refs[6][...]
        out_ref[:, 1, :] = out


def last(arrays, mod, lat, other=None, after=()):
    rows, width = arrays[0].shape
    steps = 1 if lat == 0 else 4
    mine = row_blocks(rows, width, 0, steps)
    both = [] if other is None else [other]
    shape, block = (
        ((rows, width), mine) if lat == 0
        else ((rows, 2, width), pl.BlockSpec((rows // steps, 2, width), lambda i: (i, 0, 0)))
    )
    return call(
        functools.partial(last_kernel, lat), "grad_tokens", [], (steps,),
        [*arrays, mod, *both],
        [mine, row_blocks(rows, width, 1, steps)] + [mine] * 3 + [whole(mod.shape)] + [mine] * len(both),
        [(shape, F32) if lat == 0 else (shape, F32, HBM)],
        [block],
        3, after,
    )[0]


def pack_kernel(rest0, mid0, rest1, mid1, gate, out_ref):
    out_ref[...] = jnp.zeros_like(out_ref)
    for lat, (rest, mid) in enumerate(((rest0, mid0), (rest1, mid1))):
        out_ref[8 * lat : 8 * lat + 2] = rest[0:2]
        out_ref[8 * lat + 2 : 8 * lat + 5] = mid[0:3]
        out_ref[8 * lat + 5 : 8 * lat + 6] = gate[lat : lat + 1]
        out_ref[8 * lat + 6 : 8 * lat + 7] = mid[3:4]


def pack(arrays, after=()):
    width = arrays[0].shape[1]
    return call(
        pack_kernel, "pack", [], (1,), arrays, [whole(a.shape) for a in arrays],
        [((16, width), F32)], [whole((16, width))], 1, after,
    )[0]


def message_kernel(place_ref, mine, theirs, cond_ref, ub0, ub1, db0, db1, back0, half1, rest1, out_ref, low_ref):
    width = mine.shape[1]
    total = mine[...] + theirs[...]
    low_ref[...] = total.astype(BF).astype(F32)
    out_ref[...] = jnp.zeros_like(out_ref)
    unit = width // 2
    active = silu(cond_ref[...]).astype(F32)
    for lat in range(2):
        out_ref[lat : lat + 1, :width] = active[lat : lat + 1, :]
        for t in range(3):
            at = 3 * place_ref[0] + t
            cols = pl.ds(pl.multiple_of(lax.rem(at, 2) * unit, unit), unit)
            out_ref[lat : lat + 1, width + t * unit : width + (t + 1) * unit] = low_ref[
                pl.ds(8 * lat + lax.div(at, 2), 1), cols
            ]
    ff = ub0.shape[1]
    heads = half1.shape[1]
    out_ref[2:3, :ff] = ub0[...] + ub1[...]
    out_ref[2:3, ff : ff + width] = db0[...] + db1[...]
    at = ff + width
    for j in (0, 2):
        for t, other in enumerate((half1, rest1)):
            out_ref[2:3, at : at + heads] = back0[j : j + 1, t * heads : (t + 1) * heads] + other[j : j + 1]
            at += heads
    out_ref[3:4, :width] = total[6:7] + total[14:15]


def message(place, arrays, after=()):
    width = arrays[0].shape[1]
    ff, heads = arrays[3].shape[1], arrays[7].shape[1]
    shape = (4, max(width + 3 * (width // 2), ff + width + 2 * heads))
    return call(
        message_kernel, "message", [place], (1,), arrays, [whole(a.shape) for a in arrays],
        [(shape, F32), ((16, width), F32)], [whole(shape), whole((16, width))], 1, after,
    )


def join_kernel(mine, theirs, out_ref):
    rows = mine.shape[0] - 2
    out_ref[:rows] = mine[:rows]
    out_ref[rows : 2 * rows] = theirs[:rows]
    out_ref[2 * rows :] = mine[rows:] + theirs[rows:]


def join(mine, theirs, after=()):
    shape = (2 * mine.shape[0] - 2, mine.shape[1])
    return call(
        join_kernel, "join", [], (1,), [mine, theirs], [whole(mine.shape)] * 2,
        [(shape, F32)], [whole(shape)], 1, after,
    )[0]


def condition_kernel(low_ref, w_ref, cond_ref, out_ref, acc):
    j = pl.program_id(0)

    @pl.when(j == 0)
    def _():
        acc[...] = jnp.zeros_like(acc)

    rows = jnp.concatenate([low_ref[pl.ds(j, 1), :], low_ref[pl.ds(8 + j, 1), :]], 0)
    acc[...] += dot(rows.astype(BF), w_ref[...], COLS)

    @pl.when(j == pl.num_programs(0) - 1)
    def _():
        cond = cond_ref[...].astype(F32)
        sig = 1.0 / (1.0 + jnp.exp(-cond))
        out_ref[...] = acc[...] * (sig * (1.0 + cond * (1.0 - sig)))


def condition_grad(low, weight, cond, after=()):
    lats, width = cond.shape
    return call(
        condition_kernel, "condition_grad", [], (6,), [low, weight, cond],
        [whole(low.shape), pl.BlockSpec((width, width), lambda i: (0, i)), whole(cond.shape)],
        [((lats, width), F32)], [whole((lats, width))], 5, after, [pltpu.VMEM((lats, width), F32)],
    )[0]


def place_rows(pos_ref, send_ref, keep_ref, first, values, tiles):
    rows = send_ref.shape[0] * 2 // tiles
    for t in range(values.shape[0] // rows):
        pos = pos_ref[first + t]
        part = values[t * rows : (t + 1) * rows]

        @pl.when(pos < tiles // 2)
        def _():
            send_ref[pl.ds(pl.multiple_of(pos * rows, rows), rows), :] = part.astype(BF)

        @pl.when(pos >= tiles // 2)
        def _():
            keep_ref[pl.ds(pl.multiple_of((pos - tiles // 2) * rows, rows), rows), :] = part


def weight_kernel(tiles, lats, pos_ref, *refs):
    send_ref, keep_ref = refs[-2:]
    rows = send_ref.shape[0] * 2 // tiles
    total = None
    for l in range(lats):
        right = refs[lats + l]
        value = right[...] if len(right.shape) == 2 else jnp.concatenate([right[j] for j in range(3)], 1)
        part = dot(refs[l][...], value, ROWS)
        total = part if total is None else total + part
    first = pl.program_id(0) * (refs[0].shape[1] // rows)
    place_rows(pos_ref, send_ref, keep_ref, first, total, tiles)


def weight_grad(pos, lefts, rights, name, after=(), steps=1, parts=None):
    tiles = pos.shape[0]
    seq, depth = lefts[0].shape
    shape = rights[0].shape
    specs = [whole(shape)] * len(rights)
    if parts is not None:
        shape = shape[:-1] + (shape[-1] // parts[0][1],)
        specs = [
            pl.BlockSpec(a.shape[:-1] + (a.shape[-1] // n,), functools.partial(lambda at, *_: (0, 0, at), at))
            for a, (at, n) in zip(rights, parts)
        ]
    width = shape[1] if len(shape) == 2 else shape[0] * shape[2]
    block = depth // steps
    half = (depth // 2, width)
    return call(
        functools.partial(weight_kernel, tiles, len(lefts)), name, [pos], (steps,),
        [*lefts, *rights],
        [pl.BlockSpec((seq, block), lambda i, o: (0, i))] * len(lefts) + specs,
        [(half, BF), (half, F32)],
        [whole(half)] * 2,
        width / 128, after,
    )


def first_kernel(tiles, quarter, lats, order_ref, pos_ref, *refs):
    ins, lows, mixed, pieces = refs[:lats], refs[lats : 2 * lats], refs[2 * lats : 3 * lats], refs[3 * lats : -2]
    heads, proj = None, None
    for l in range(lats):
        part = dot(ins[l][...], jnp.concatenate([lows[l][j] for j in range(3)], 1), ROWS)
        heads = part if heads is None else heads + part
        for j in range(4):
            rows = pl.ds(pl.multiple_of(order_ref[j] * quarter, quarter), quarter)
            part = dot(pieces[4 * l + j][...], mixed[l][rows, :], ROWS)
            proj = part if proj is None else proj + part
    place_rows(pos_ref, refs[-2], refs[-1], 0, jnp.concatenate([heads, proj], 1), tiles)


def first_grad(order, pos, ins, lows, parts, mixed, pieces, after=()):
    tiles = pos.shape[0]
    quarter, width = pieces[0][0].shape
    args = [*ins, *lows, *mixed, *[p for four in pieces for p in four]]
    low_specs = [
        pl.BlockSpec(a.shape[:-1] + (a.shape[-1] // n,), functools.partial(lambda at, *_: (0, 0, at), at))
        for a, (at, n) in zip(lows, parts)
    ]
    cols = 3 * (lows[0].shape[2] // parts[0][1]) + mixed[0].shape[1]
    half = (width // 2, cols)
    return call(
        functools.partial(first_kernel, tiles, quarter, len(ins)), "first_grad", [order, pos], (1,),
        args,
        [whole(a.shape) for a in ins]
        + low_specs
        + [whole(a.shape) for a in args[2 * len(ins) :]],
        [(half, BF), (half, F32)],
        [whole(half)] * 2,
        6, after,
    )


def back_step(i, near_ref, pieces, p_ref, q_ref, k_ref, v_ref, total_ref, low_ref, bias_ref, dk_acc, dv_acc, grad_ref):
    rows, cols = q_ref.shape
    heads = cols // HEAD_DIM
    turned = dk_acc.shape[0] == cols

    @pl.when(i == 0)
    def _():
        dk_acc[...] = jnp.zeros_like(dk_acc)
        dv_acc[...] = jnp.zeros_like(dv_acc)

    for j in range(4):

        @pl.when(i == j)
        def _():
            grad_ref[...] = dot(pieces[j][...], p_ref[...], COLS).astype(BF)

    @pl.when(i < 4)
    def _():
        q = spread(q_ref[...] * BF(SCALE), heads)
        g = spread(grad_ref[...], heads)
        k, v = k_ref[...], v_ref[...]
        probs = jnp.exp(dot(k, q, COLS) - total_ref[0])
        grad_probs = dot(v, g, COLS)
        inner = jnp.sum(probs * grad_probs, axis=0, keepdims=True)
        scores = (probs * (grad_probs - inner)).astype(BF)
        probs = probs.astype(BF)
        if turned:
            dv_acc[...] += dot(g, probs, ((0,), (1,)))
            dk_acc[...] += dot(q, scores, ((0,), (1,)))
            every = dot(k, scores, ROWS)
            dq = jnp.concatenate(
                [every[h * HEAD_DIM : (h + 1) * HEAD_DIM, h * rows : (h + 1) * rows] for h in range(heads)], 0
            ).T
        else:
            dv_acc[...] += dot(probs, g)
            dk_acc[...] += dot(scores, q)
            every = dot(scores, k, ROWS)
            dq = every[:rows]
            for h in range(1, heads):
                dq = jnp.where(head_lanes(rows, cols, h), every[h * rows : (h + 1) * rows], dq)
        low_ref[0, pl.ds(pl.multiple_of(near_ref[i] * rows, rows), rows), :] = (dq * SCALE).astype(BF)

    @pl.when(i == 3)
    def _():
        low_ref[1] = (dk_acc[...].T if turned else dk_acc[...]).astype(BF)
        low_ref[2] = (dv_acc[...].T if turned else dv_acc[...]).astype(BF)
        bias_ref[...] = jnp.zeros_like(bias_ref)
        for j in range(3):
            bias_ref[j : j + 1] = jnp.sum(low_ref[j].astype(F32), axis=0, keepdims=True)


def back_kernel(near_ref, u0, u1, u2, u3, p_ref, q_ref, k_ref, v_ref, total_ref, low_ref, bias_ref, *scratch):
    back_step(
        pl.program_id(0), near_ref, (u0, u1, u2, u3), p_ref, q_ref, k_ref, v_ref, total_ref, low_ref, bias_ref,
        *scratch,
    )


def back_end_kernel(lat, others, near_ref, order_ref, u0, u1, u2, u3, p_ref, q_ref, k_ref, v_ref, total_ref, *refs):
    other_refs, (w_ref, tok_ref), refs = refs[:others], refs[others : others + 2], refs[others + 2 :]
    low_ref, bias_ref, send_ref, far_ref, own_ref, stat_ref = refs[:6]
    i = pl.program_id(0)
    rows = q_ref.shape[0]
    back_step(
        i, near_ref, (u0, u1, u2, u3), p_ref, q_ref, k_ref, v_ref, total_ref, low_ref, bias_ref, *refs[6:]
    )

    @pl.when(i == 0)
    def _():
        stat_ref[...] = jnp.zeros_like(stat_ref)

    @pl.when(i >= 4)
    def _():
        here = pl.ds(pl.multiple_of(order_ref[jnp.maximum(i - 4, 0)] * rows, rows), rows)
        out = None
        for j in range(3):
            parts = [ref[j, here, :] for ref in (*other_refs, low_ref)]
            part = dot(jnp.concatenate(parts, 1), w_ref[j], COLS)
            out = part if out is None else out + part
        normed, _ = normalize(tok_ref[...].astype(F32))
        stat_ref[0:1] += jnp.sum(out, axis=0, keepdims=True)
        stat_ref[1:2] += jnp.sum(out * normed, axis=0, keepdims=True)
        place_quarter(i - 4, out, send_ref, far_ref, own_ref)


def attend_back(near, order, pieces, proj, q, k, v, total, part, parts, lat, end=None, after=()):
    seq, cols = q.shape
    cols = cols // parts
    width = proj.shape[1]
    block = seq // 4
    heads = cols // HEAD_DIM
    first = lambda i, n, *_: n[jnp.minimum(i, 3)]
    later = lambda i, n, o: o[jnp.maximum(i - 4, 0)]
    keys = pl.BlockSpec((seq, cols), lambda *_: (0, part))
    ins = [*pieces, proj, q, k, v, total]
    in_specs = [whole((block, width))] * 4 + [
        pl.BlockSpec((cols, width), lambda *_: (part, 0)),
        pl.BlockSpec((block, cols), lambda *a: (first(*a), part)),
        keys,
        keys,
        pl.BlockSpec((1, 1, heads * block), lambda *a: (first(*a), 0, part)),
    ]
    outs = [((3, seq, cols), BF), ((8, cols), F32)]
    out_specs = [whole((3, seq, cols)), whole((8, cols))]
    sums = (seq, cols) if parts == 1 else (cols, seq)
    scratch = [pltpu.VMEM(sums, F32)] * 2 + [pltpu.VMEM((block, cols), BF)]
    if end is None:
        return call(
            back_kernel, "attend_backward", [near], (4,), ins, in_specs, outs, out_specs, 20 / parts, after, scratch
        )
    others, w3, tok = end
    quarter = ((block, width), F32)
    return call(
        functools.partial(back_end_kernel, lat, len(others)), "attend_backward_end", [near, order], (8,),
        ins + [*others, w3, tok],
        in_specs
        + [whole(other.shape) for other in others]
        + [whole(w3.shape)]
        + [pl.BlockSpec((block, width), lambda *a: (later(*a), 0))],
        outs + [((2 * block, width), F32), quarter, quarter, ((8, width), F32)],
        out_specs
        + [
            pl.BlockSpec((block, width), lambda i, *_: (jnp.clip(i - 4, 0, 1), 0)),
            whole((block, width)),
            whole((block, width)),
            whole((8, width)),
        ],
        20 / parts + 4, after, scratch,
    )


def tie(value, *others):
    return lax.optimization_barrier((value, *others))[0]


def far_kernel(*refs):
    out_ref = refs[-1]
    for j in range(len(refs) // 2):
        rows = refs[2 * j].shape[0]
        out_ref[j * rows : (j + 1) * rows] = (refs[2 * j][...] + refs[2 * j + 1][...]).astype(BF)


def far_sum(pairs, after=()):
    rows, width = pairs[0][0].shape
    ins = [a for pair in pairs for a in pair]
    shape = (rows * len(pairs), width)
    block = pl.BlockSpec((rows, width), lambda i: (0, 0))
    return call(
        far_kernel, "far_sum", [], (1,), ins, [block] * len(ins), [(shape, BF)], [whole(shape)], 1, after
    )[0]


def fold_kernel(*refs):
    count = len(refs) // 4
    for j in range(count):
        keep, got, send, kept = refs[2 * j], refs[2 * j + 1], refs[2 * count + 2 * j], refs[2 * count + 2 * j + 1]
        half = kept.shape[0]
        send[...] = (keep[:half] + got[:half].astype(F32)).astype(BF)
        kept[...] = keep[half:] + got[half:].astype(F32)


def fold(pairs, after=()):
    ins = [a for pair in pairs for a in pair]
    outs = []
    for keep, _ in pairs:
        half = (keep.shape[0] // 2, keep.shape[1])
        outs += [(half, BF), (half, F32)]
    got = call(
        fold_kernel, "fold", [], (1,), ins, [whole(a.shape) for a in ins], outs, [whole(o[0]) for o in outs], 2, after
    )
    return [(got[2 * j], got[2 * j + 1]) for j in range(len(pairs))]


def close_kernel(turn, keep_ref, got_ref, *outs):
    total = keep_ref[...] + got_ref[...].astype(F32)
    if turn < total.shape[1]:
        outs[-1][...] = total[:, turn:].T
    if turn > 0:
        outs[0][...] = total[:, :turn]


def close(keep, got, turn, after=()):
    rows, width = keep.shape
    shapes = ([(rows, turn)] if turn > 0 else []) + ([(width - turn, rows)] if turn < width else [])
    out = call(
        functools.partial(close_kernel, turn), "close", [], (1,),
        [keep, got], [whole(keep.shape)] * 2, [(a, F32) for a in shapes], [whole(a) for a in shapes], 1, after,
    )
    return out if len(out) > 1 else out[0]


def end_sum(keep, got, bits, turn, after=()):
    for bit in bits:
        ((send, keep),) = fold([(keep, got)])
        got = swap(send, "dp", bit)
    return close(keep, got, turn, after)


def pieces_of(own, far):
    return own, far, swap(own, "tensor", 1), swap(far, "tensor", 1)


def dp_bits(size):
    return [1 << i for i in range(size.bit_length() - 1)]


def row_places(index, size, bits):
    away = jnp.arange(size, dtype=jnp.int32) ^ index
    place = jnp.zeros((size,), jnp.int32)
    for bit in bits:
        place = 2 * place + 1 - (away // bit) % 2
    return place


def shards(
    tokens,
    condition,
    modulation_weight,
    modulation_bias,
    qkv_weight,
    qv_bias,
    proj_weight,
    proj_bias,
    up_weight,
    up_bias,
    down_weight,
    down_bias,
    cotangent,
):
    seq, lats, width = tokens.shape
    place = lax.axis_index("tensor")
    index = lax.axis_index("dp")
    size = lax.axis_size("dp")
    quarter = seq // 4
    mod_cols = modulation_weight.shape[1] // 4
    order = jnp.array(SEND_FIRST, jnp.int32) ^ place
    near = jnp.array(NEAR_FIRST, jnp.int32) ^ place
    here = place[None]
    bits = dp_bits(size)
    other_bits = [bits[1], bits[0]] + bits[2:]
    places, other_places = row_places(index, size, bits), row_places(index, size, other_bits)
    to_dp = lambda value, bit: swap(value, "dp", bit)
    core = lambda value: swap(value, "tensor", 1)
    chip = lambda value: swap(value, "tensor", 2)

    proj_far = chip(proj_weight)
    w3 = jnp.transpose(qkv_weight, (1, 0, 2))
    heads = w3.shape[2]

    mod_one, (tokens0, in0, *qkv0), (tokens1, in1, *qkv1) = prepare(
        tokens, condition, modulation_weight, modulation_bias, w3, qv_bias
    )
    mixed0, total0 = attend(*qkv0, quarter, [proj_far])
    mixed_far0 = chip(mixed0)
    mod_two, mixed1, total1 = attend(
        *qkv1, quarter, [mixed0], [condition, modulation_weight, modulation_bias]
    )
    mixed_far1 = chip(mixed1)
    cot = jnp.transpose(tie(cotangent, mixed1), (1, 0, 2))
    proj = pieces_of(proj_weight, tie(proj_far, mixed1))
    gathered0 = pieces_of(mixed0, tie(mixed_far0, mod_two))

    feed_args = (cot, mod_two, up_weight, up_bias, down_weight)
    low0, hid0, pre0, gm0, upd0, tok0, cot0, send0, far0, own0, ub0, db0 = feed(
        order, gathered0, proj, proj_bias, tokens0, *feed_args, 0
    )
    near0 = core(send0)
    gathered1 = pieces_of(mixed1, tie(mixed_far1, own0))
    down0 = feed_down(order, hid0, down_weight)
    sum0 = far_sum([(far0, tie(near0, down0[1]))])
    grad_far0 = chip(sum0)
    low1, hid1, pre1, gm1, upd1, tok1, cot1, send1, far1, own1, ub1, db1 = feed(
        order, gathered1, proj, proj_bias, tokens1, *feed_args, 1, [sum0]
    )
    near1 = core(send1)
    g0, u0, stat0 = middle(own0, near0, tie(grad_far0, own1), upd0, tok0, cot0, mod_two, 0, [own1])
    u_far0 = chip(u0)
    down1 = feed_down(order, hid1, down_weight, [u0])
    sum1 = far_sum([(far1, tie(near1, down1[1]))])
    grad_far1 = chip(sum1)
    up_send, up_keep = weight_grad(places, [low0, low1], [pre0, pre1], "up_grad", [sum1])
    up_got = to_dp(up_send, bits[0])
    pieces0 = pieces_of(u0, tie(u_far0, up_keep))
    down_send, down_keep = weight_grad(other_places, [gm0, gm1], [hid0, hid1], "down_grad", [up_keep])
    down_got = to_dp(down_send, other_bits[0])
    g1, u1, stat1 = middle(own1, near1, tie(grad_far1, down_keep), upd1, tok1, cot1, mod_two, 1, [down_keep])
    u_far1 = chip(u1)

    back0 = attend_back(near, order, pieces0, proj_weight, *qkv0, total0, 0, 1, 0, ((), w3, tokens0), [u1])
    mlp_near0, mlp_near1 = core(tie(down0[0], u1)), core(tie(down1[0], u1))
    mlp_sum = far_sum([(down0[1], tie(mlp_near0, back0[1])), (down1[1], tie(mlp_near1, back0[1]))])
    mlp_far = chip(mlp_sum)
    in_near0 = core(back0[2])
    pieces1 = pieces_of(u1, tie(u_far1, back0[1]))
    (up_send, up_keep), (down_send, down_keep) = fold(
        [(up_keep, tie(up_got, back0[1])), (down_keep, tie(down_got, back0[1]))], [mlp_sum]
    )
    up_got, down_got = to_dp(up_send, bits[1]), to_dp(down_send, other_bits[1])
    in_sum0 = far_sum([(back0[3], tie(in_near0, up_keep))])
    in_far0 = chip(in_sum0)
    half1 = attend_back(near, order, pieces1, proj_weight, *qkv1, total1, 0, 2, 1, None, [in_sum0])
    first_send, first_keep = first_grad(
        near, places, [in0, in1], [back0[0], half1[0]], [(0, 2), (0, 1)], [mixed0, mixed1], [pieces0, pieces1]
    )
    first_got = to_dp(first_send, bits[0])
    (up_send, up_keep), (down_send, down_keep) = fold(
        [(up_keep, tie(up_got, first_keep)), (down_keep, tie(down_got, first_keep))]
    )
    up_got, down_got = to_dp(up_send, bits[2]), to_dp(down_send, other_bits[2])
    output, gate = finish(
        (down0[2], mlp_near0, tie(mlp_far, down_keep), upd0, tok0, cot0),
        (down1[2], mlp_near1, tie(mlp_far, down_keep), upd1, tok1, cot1),
        mod_two, down_bias, [down_keep],
    )
    grad_tokens0 = last((back0[4], in_near0, tie(in_far0, gate), g0, tok0), mod_one, 0)
    ((first_send, first_keep),) = fold([(first_keep, tie(first_got, grad_tokens0))])
    first_got = to_dp(first_send, bits[1])
    rest1 = attend_back(
        near, order, pieces1, proj_weight, *qkv1, total1, 1, 2, 1, ((half1[0],), w3, tokens1), [first_keep]
    )

    in_near1 = core(rest1[2])
    mod = pack([back0[5], stat0, rest1[5], stat1, gate])
    mod_near = core(mod)
    second_send, second_keep = weight_grad(
        other_places, [in0, in1], [back0[0], rest1[0]], "qkv_grad", [mod, first_got], 1, [(1, 2), (0, 1)]
    )
    second_got = to_dp(second_send, other_bits[0])
    mod = mod + tie(mod_near, second_keep)
    mod_far = chip(mod)
    in_sum1 = far_sum([(rest1[3], tie(in_near1, mod))])
    in_far1 = chip(in_sum1)
    ((first_send, first_keep),) = fold([(first_keep, tie(first_got, in_sum1))])
    first_got = to_dp(first_send, bits[2])
    note, low_mod = message(
        here,
        [mod, tie(mod_far, first_keep), condition, ub0, ub1, db0, db1, back0[1], half1[1], rest1[1]],
    )
    note_got = to_dp(note, bits[0])
    up_shard = end_sum(up_keep, tie(up_got, note), bits[3:], up_keep.shape[1])
    down_shard = end_sum(down_keep, tie(down_got, up_shard), other_bits[3:], 0)
    ((second_send, second_keep),) = fold([(second_keep, tie(second_got, down_shard))])
    second_got = to_dp(second_send, other_bits[1])
    note = join(note, tie(note_got, second_keep))
    note_got = to_dp(note, bits[1])
    grad_condition = condition_grad(low_mod, modulation_weight, condition, [note])
    ((second_send, second_keep),) = fold([(second_keep, tie(second_got, grad_condition))])
    second_got = to_dp(second_send, other_bits[2])
    note = join(note, tie(note_got, second_keep))
    note_got = to_dp(note, bits[2])
    grad_tokens = last((rest1[4], in_near1, tie(in_far1, note), g1, tok1), mod_one, 1, grad_tokens0)
    first_shard, proj_shard = end_sum(first_keep, tie(first_got, note), bits[3:], 3 * (heads // 2))
    note = join(note, tie(note_got, grad_tokens))
    for bit in bits[3:]:
        note = join(note, to_dp(note, bit))
    second_shard = end_sum(second_keep, tie(second_got, grad_tokens), bits[3:], second_keep.shape[1])
    qkv_shard = jnp.concatenate(
        [part.reshape(part.shape[0], 3, -1) for part in (first_shard, second_shard)], 2
    )
    rows = note.shape[0] - 2
    all_silu = note[:rows, :width].astype(BF)
    all_cols = note[:rows, width : width + mod_cols].astype(BF)
    mod_rows = width // size
    my_silu = lax.dynamic_slice_in_dim(all_silu, index * mod_rows, mod_rows, 1)
    mod_shard = dot(my_silu, all_cols, ROWS)
    mod_bias_sum = jnp.sum(all_cols, axis=0, dtype=F32)
    ff = up_weight.shape[1]
    up_bias_sum, down_bias_sum, qv_sum = jnp.split(note[rows, : ff + width + 2 * heads], [ff, ff + width])
    return (
        output,
        grad_tokens,
        grad_condition,
        mod_shard,
        mod_bias_sum,
        qkv_shard,
        qv_sum.reshape(2, heads),
        proj_shard,
        note[rows + 1, :width],
        up_shard,
        up_bias_sum,
        down_shard,
        down_bias_sum,
    )


def solution(mesh):
    in_specs = (
        P(None, "dp", None),
        P("dp", None),
        P(),
        P(),
        P(None, None, "tensor"),
        P(None, "tensor"),
        P("tensor", None),
        P(),
        P(None, "tensor"),
        P("tensor"),
        P("tensor", None),
        P(),
        P(None, "dp", None),
    )
    out_specs = (
        P("tensor", "dp", None),
        P("tensor", "dp", None),
        P("dp", None),
        P("dp", "tensor"),
        P("tensor"),
        P("dp", None, "tensor"),
        P(None, "tensor"),
        P("tensor", "dp"),
        P(),
        P("dp", "tensor"),
        P("tensor"),
        P("tensor", "dp"),
        P(),
    )
    return jax.shard_map(shards, mesh=mesh, in_specs=in_specs, out_specs=out_specs, check_vma=False)
```

```python
import functools

import jax
import jax.numpy as jnp
from jax import lax
from jax.experimental import pallas as pl
from jax.experimental.pallas import tpu as pltpu
from jax.sharding import PartitionSpec as P

HEAD_DIM = 64
EPS = 1e-06
BF = jnp.bfloat16
F32 = jnp.float32
ROWS = ((0,), (0,))
COLS = ((1,), (1,))
MIB = 1 << 20
SCALE = HEAD_DIM**-0.5
SEND_FIRST = (3, 1, 2, 0)
NEAR_FIRST = (0, 2, 1, 3)
LIMITS = {
    "prepare": 60,
    "attend_forward": 16,
    "attend_modulate": 16,
    "feed": 24,
    "feed_down": 14,
    "far_sum": 8,
    "middle": 20,
    "up_grad": 20,
    "down_grad": 20,
    "qkv_grad": 24,
    "first_grad": 40,
    "fold": 24,
    "attend_backward": 20,
    "attend_backward_end": 32,
    "finish": 32,
    "grad_tokens": 60,
}


def dot(left, right, dims=((1,), (0,))):
    return lax.dot_general(left, right, (dims, ((), ())), preferred_element_type=F32)


def swap(value, axis, bit):
    pairs = [(i, i ^ bit) for i in range(lax.axis_size(axis))]
    return lax.ppermute(value, axis, pairs)


def normalize(values):
    centre = values - jnp.mean(values, axis=-1, keepdims=True)
    inverse = lax.rsqrt(jnp.mean(centre * centre, axis=-1, keepdims=True) + EPS)
    return centre * inverse, inverse


def norm_back(grad, normed, inverse):
    return inverse * (
        grad
        - jnp.mean(grad, axis=-1, keepdims=True)
        - normed * jnp.mean(grad * normed, axis=-1, keepdims=True)
    )


def gelu_pair(v):
    root = 0.7978845608028654
    square = v * v
    inner = jnp.tanh(v * (root + (root * 0.044715) * square))
    half = 0.5 + 0.5 * inner
    slope = half + (0.5 * v) * (1.0 - inner * inner) * (root + (3 * root * 0.044715) * square)
    return v * half, slope


def head_lanes(rows, cols, h):
    return lax.broadcasted_iota(jnp.int32, (rows, cols), 1) // HEAD_DIM == h


def spread(x, heads):
    rows, cols = x.shape
    zero = jnp.zeros_like(x)
    return jnp.concatenate([jnp.where(head_lanes(rows, cols, h), x, zero) for h in range(heads)], 0)


def whole(shape):
    return pl.BlockSpec(shape, lambda *_: (0,) * len(shape))


def shape_of(shape, dtype):
    return jax.ShapeDtypeStruct(shape, dtype)


def cost(expected):
    return pl.CostEstimate(flops=int(expected * 1.15e10), bytes_accessed=0, transcendentals=0)


ANY = pl.BlockSpec(memory_space=pl.ANY)
HBM = "hbm"


def call(kernel, name, scalars, grid, ins, in_specs, outs, out_specs, expected, after=(), scratch=()):
    skip = len(after)

    def body(*refs):
        first = len(scalars)
        kernel(*refs[:first], *refs[first + skip :])

    return pl.pallas_call(
        body,
        out_shape=[pltpu.HBM(*o[:2]) if len(o) > 2 else shape_of(*o) for o in outs],
        grid_spec=pltpu.PrefetchScalarGridSpec(
            num_scalar_prefetch=len(scalars),
            grid=grid,
            in_specs=[ANY] * skip + in_specs,
            out_specs=out_specs,
            scratch_shapes=list(scratch),
        ),
        compiler_params=pltpu.CompilerParams(vmem_limit_bytes=LIMITS.get(name, 16) * MIB),
        cost_estimate=cost(expected),
        name=name,
    )(*scalars, *after, *ins)


def silu(cond):
    value = cond.astype(F32)
    return (value * (1.0 / (1.0 + jnp.exp(-value)))).astype(BF)


def modulate(cond_ref, w_ref, bias_ref):
    return dot(silu(cond_ref[...]), w_ref[...]) + bias_ref[...].astype(F32)[None]


def mod_specs(cond, width, first):
    return [
        whole(cond.shape),
        pl.BlockSpec((width, width), lambda i: (0, first(i))),
        pl.BlockSpec((width,), lambda i: (first(i),)),
    ]


def prepare_kernel(tok_ref, w_ref, bias_ref, cond_ref, s_ref, sb_ref, cond_too, t_ref, tb_ref, mod_ref, *outs):
    rows, lats, width = tok_ref.shape

    @pl.when(pl.program_id(0) == 0)
    def _():
        mod_ref[:, :width] = modulate(cond_ref, s_ref, sb_ref)
        mod_ref[:, width:] = modulate(cond_too, t_ref, tb_ref)

    chunk = min(rows, 256 // lats)
    step = lats * chunk
    both = tok_ref[...].reshape(rows * lats, width)
    here = lax.broadcasted_iota(jnp.int32, (step, step), 0)
    there = lax.broadcasted_iota(jnp.int32, (step, step), 1)
    order = jnp.where(there == lats * lax.rem(here, chunk) + lax.div(here, chunk), 1.0, 0.0).astype(BF)
    split = [dot(order, both[j * step : (j + 1) * step]) for j in range(rows // chunk)]
    for lat in range(lats):
        x = jnp.concatenate([part[lat * chunk : (lat + 1) * chunk] for part in split], 0)
        tok_out, in_ref, q_ref, k_ref, v_ref = outs[5 * lat : 5 * lat + 5]
        tok_out[...] = x.astype(BF)
        row = lambda j: mod_ref[lat : lat + 1, j * width : (j + 1) * width]
        normed, _ = normalize(x)
        low = (normed * (1.0 + row(1)) + row(0)).astype(BF)
        in_ref[...] = low
        q_ref[...] = (dot(low, w_ref[0]) + bias_ref[0:1].astype(F32)).astype(BF)
        k_ref[...] = dot(low, w_ref[1]).astype(BF)
        v_ref[...] = (dot(low, w_ref[2]) + bias_ref[1:2].astype(F32)).astype(BF)


def prepare(tokens, cond, mod_weight, mod_bias, w3, bias, after=(), block=256):
    seq, lats, width = tokens.shape
    cols = w3.shape[2]
    rows = lambda n: pl.BlockSpec((block, n), lambda i: (i, 0))
    one = [((seq, width), BF, HBM)] * 2 + [((seq, cols), BF)] * 3
    got = call(
        prepare_kernel, "prepare", [], (seq // block,),
        [tokens, w3, bias] + [cond, mod_weight, mod_bias] * 2,
        [pl.BlockSpec((block, lats, width), lambda i: (i, 0, 0)), whole(w3.shape), whole(bias.shape)]
        + mod_specs(cond, width, lambda i: 0)
        + mod_specs(cond, width, lambda i: 1),
        [((lats, 2 * width), F32)] + one * lats,
        [whole((lats, 2 * width))] + [rows(width), rows(width), rows(cols), rows(cols), rows(cols)] * lats,
        12, after,
    )
    return got[0], got[1:6], got[6:11]


def attend_kernel(q_ref, k_ref, v_ref, *refs):
    mixed_ref, total_ref = refs[-2:]
    rows, cols = q_ref.shape
    heads = cols // HEAD_DIM
    value = v_ref[...].T
    scores = dot(k_ref[...], spread(q_ref[...] * BF(SCALE), heads), COLS)
    largest = jnp.max(scores, axis=0, keepdims=True)
    powers = jnp.exp(scores - largest)
    total = jnp.sum(powers, axis=0, keepdims=True)
    probs = (powers * (1.0 / total)).astype(BF)
    out = [
        dot(value[h * HEAD_DIM : (h + 1) * HEAD_DIM], probs[:, h * rows : (h + 1) * rows]) for h in range(heads)
    ]
    mixed_ref[...] = jnp.concatenate(out, 0).T.astype(BF)
    total_ref[0] = largest + jnp.log(total)
    if len(refs) > 2:
        cond_ref, w_ref, bias_ref, mod_ref = refs[:4]
        mod_ref[...] = modulate(cond_ref, w_ref, bias_ref)


def attend(q, k, v, block, after=(), mod=None):
    seq, cols = q.shape
    heads = cols // HEAD_DIM
    rows = pl.BlockSpec((block, cols), lambda i: (i, 0))
    ins, in_specs, outs, out_specs = [q, k, v], [rows, whole((seq, cols)), whole((seq, cols))], [], []
    if mod is not None:
        lats, width = mod[0].shape
        ins += mod
        in_specs += mod_specs(mod[0], width, lambda i: 2 + i)
        outs, out_specs = [((lats, 4 * width), F32)], [pl.BlockSpec((lats, width), lambda i: (0, i))]
    return call(
        attend_kernel, "attend_forward" if mod is None else "attend_modulate", [], (seq // block,), ins, in_specs,
        outs + [((seq, cols), BF), ((seq // block, 1, heads * block), F32)],
        out_specs + [rows, pl.BlockSpec((1, 1, heads * block), lambda i: (i, 0, 0))],
        8, after,
    )


def halves(block, width):
    return [
        pl.BlockSpec((block, width), lambda i, *_: (jnp.minimum(i, 1), 0)),
        whole((block, width)),
        whole((block, width)),
    ]


def place_quarter(step, value, send_ref, far_ref, own_ref):
    @pl.when(step < 2)
    def _():
        send_ref[...] = value.astype(send_ref.dtype)

    @pl.when(step == 2)
    def _():
        far_ref[...] = value

    @pl.when(step == 3)
    def _():
        own_ref[...] = value


def feed_kernel(
    lat, order_ref, m0, m1, m2, m3, p0, p1, p2, p3, pb_ref, tok_ref, cot_ref, mod_ref, up_ref, ub_ref, down_ref,
    in_ref, hid_ref, pre_ref, gm_ref, upd_ref, tok_out, cot_out, send_ref, far_ref, own_ref, gub_ref, gdb_ref,
):
    i = pl.program_id(0)
    width = tok_ref.shape[1]
    row = lambda j: mod_ref[lat : lat + 1, j * width : (j + 1) * width]
    update = pb_ref[...].astype(F32)[None]
    for m, p in ((m0, p0), (m1, p1), (m2, p2), (m3, p3)):
        update = update + dot(m[...], p[...])
    normed, _ = normalize(tok_ref[...].astype(F32) + row(0) * update)
    low = (normed * (1.0 + row(2)) + row(1)).astype(BF)
    in_ref[...] = low
    act, slope = gelu_pair(dot(low, up_ref[...]) + ub_ref[...].astype(F32)[None])
    hid_ref[...] = act.astype(BF)
    grad_mlp = (row(3) * cot_ref[0].astype(F32)).astype(BF)
    gm_ref[...] = grad_mlp
    grad_pre = (dot(grad_mlp, down_ref[...], COLS) * slope).astype(BF)
    pre_ref[...] = grad_pre
    place_quarter(i, dot(grad_pre, up_ref[...], COLS), send_ref, far_ref, own_ref)

    @pl.when(i == 3)
    def _():
        upd_ref[...] = update
        tok_out[...] = tok_ref[...]
        cot_out[...] = cot_ref[0]

    @pl.when(i == 0)
    def _():
        gub_ref[...] = jnp.zeros_like(gub_ref)
        gdb_ref[...] = jnp.zeros_like(gdb_ref)

    gub_ref[...] += jnp.sum(grad_pre.astype(F32), axis=0, keepdims=True)
    gdb_ref[...] += jnp.sum(grad_mlp.astype(F32), axis=0, keepdims=True)


def feed(order, mixed, proj, proj_bias, tok, cot, mod, up, up_bias, down, lat, after=()):
    seq, width = tok.shape
    block = seq // 4
    ff = up.shape[1]
    cols = mixed[0].shape[1]
    at = lambda n: pl.BlockSpec((block, n), lambda i, o: (o[i], 0))
    at3 = pl.BlockSpec((1, block, width), lambda i, o: (lat, o[i], 0))
    quarter = ((block, width), F32)
    return call(
        functools.partial(feed_kernel, lat), "feed", [order], (4,),
        [*mixed, *proj, proj_bias, tok, cot, mod, up, up_bias, down],
        [at(cols)] * 4
        + [whole((cols, width))] * 4
        + [whole((width,)), at(width), at3, whole(mod.shape)]
        + [whole(up.shape), whole((ff,)), whole(down.shape)],
        [((seq, width), BF), ((seq, ff), BF), ((seq, ff), BF), ((seq, width), BF), quarter]
        + [((block, width), BF)] * 2
        + [((2 * block, width), F32), quarter, quarter, ((1, ff), F32), ((1, width), F32)],
        [at(width), at(ff), at(ff), at(width)]
        + [whole((block, width))] * 3
        + halves(block, width)
        + [whole((1, ff)), whole((1, width))],
        18, after,
    )


def down_kernel(order_ref, hid_ref, down_ref, send_ref, far_ref, own_ref):
    out = dot(hid_ref[...], down_ref[...])
    place_quarter(pl.program_id(0), out, send_ref, far_ref, own_ref)


def feed_down(order, hidden, down, after=()):
    seq, ff = hidden.shape
    width = down.shape[1]
    block = seq // 4
    quarter = ((block, width), F32)
    return call(
        down_kernel, "feed_down", [order], (4,),
        [hidden, down],
        [pl.BlockSpec((block, ff), lambda i, o: (o[i], 0)), whole(down.shape)],
        [((2 * block, width), BF), quarter, quarter],
        halves(block, width),
        5, after,
    )


def row_blocks(rows, width, skip=0, steps=1):
    return pl.BlockSpec((rows // steps, width), lambda i: (skip * steps + i, 0))


def add_stats(ref, values, first=0):
    @pl.when(pl.program_id(0) == 0)
    def _():
        ref[first : first + len(values)] = jnp.zeros((len(values), ref.shape[1]), F32)

    for j, value in enumerate(values):
        ref[first + j : first + j + 1] += jnp.sum(value, axis=0, keepdims=True)


def middle_kernel(lat, own, near, far, upd_ref, tok_ref, cot_ref, mod_ref, g_ref, low_ref, stat_ref):
    width = upd_ref.shape[1]
    row = lambda j: mod_ref[lat : lat + 1, j * width : (j + 1) * width]
    grad_in = own[...] + near[...] + far[...].astype(F32)
    update = upd_ref[...]
    normed, inverse = normalize(tok_ref[...].astype(F32) + row(0) * update)
    grad = cot_ref[...].astype(F32) + norm_back(grad_in * (1.0 + row(2)), normed, inverse)
    g_ref[...] = grad
    low = (row(0) * grad).astype(BF)
    low_ref[...] = low
    add_stats(stat_ref, (grad * update, grad_in, grad_in * normed, low.astype(F32)))


def middle(own, near, far, update, tok, cot, mod, lat, after=()):
    rows, width = own.shape
    mine = row_blocks(rows, width, 0, 2)
    return call(
        functools.partial(middle_kernel, lat), "middle", [], (2,),
        [own, near, far, update, tok, cot, mod],
        [mine, row_blocks(rows, width, 1, 2)] + [mine] * 4 + [whole(mod.shape)],
        [((rows, width), F32, HBM), ((rows, width), BF), ((4, width), F32)],
        [mine, mine, whole((4, width))],
        2, after,
    )


def finish_kernel(*refs):
    mod_ref, bias_ref, out_ref, stat_ref = refs[-4:]
    width = mod_ref.shape[1] // 4
    for lat in range(2):
        own, near, far, upd, tok, cot = refs[6 * lat : 6 * lat + 6]
        row = lambda j: mod_ref[lat : lat + 1, j * width : (j + 1) * width]
        update = own[...] + near[...].astype(F32) + far[...].astype(F32) + bias_ref[...].astype(F32)[None]
        stream = tok[...].astype(F32) + row(0) * upd[...]
        out_ref[:, lat, :] = (stream + row(3) * update).astype(BF)
        add_stats(stat_ref, (cot[...].astype(F32) * update,), lat)


def finish(first, other, mod, bias, after=()):
    rows, width = first[0].shape
    mine = row_blocks(rows, width)
    one = lambda lat: [mine, row_blocks(rows, width, 1), row_blocks(rows, width, lat)] + [mine] * 3
    return call(
        finish_kernel, "finish", [], (1,),
        [*first, *other, mod, bias],
        one(0) + one(1) + [whole(mod.shape), whole((width,))],
        [((rows, 2, width), BF), ((2, width), F32)],
        [whole((rows, 2, width)), whole((2, width))],
        4, after,
    )


def last_kernel(lat, *refs):
    own, near, far, g_ref, tok, mod_ref = refs[:6]
    out_ref = refs[-1]
    width = mod_ref.shape[1] // 2
    grad_in = own[...] + near[...] + far[...].astype(F32)
    normed, inverse = normalize(tok[...].astype(F32))
    scale = 1.0 + mod_ref[lat : lat + 1, width : 2 * width]
    out = g_ref[...] + norm_back(grad_in * scale, normed, inverse)
    if lat == 0:
        out_ref[...] = out
    else:
        out_ref[:, 0, :] = refs[6][...]
        out_ref[:, 1, :] = out


def last(arrays, mod, lat, other=None, after=()):
    rows, width = arrays[0].shape
    steps = 2
    mine = row_blocks(rows, width, 0, steps)
    both = [] if other is None else [other]
    shape, block = (
        ((rows, width), mine) if lat == 0
        else ((rows, 2, width), pl.BlockSpec((rows // steps, 2, width), lambda i: (i, 0, 0)))
    )
    return call(
        functools.partial(last_kernel, lat), "grad_tokens", [], (steps,),
        [*arrays, mod, *both],
        [mine, row_blocks(rows, width, 1, steps)] + [mine] * 3 + [whole(mod.shape)] + [mine] * len(both),
        [(shape, F32) if lat == 0 else (shape, F32, HBM)],
        [block],
        3, after,
    )[0]


def pack_kernel(rest0, mid0, rest1, mid1, gate, out_ref):
    out_ref[...] = jnp.zeros_like(out_ref)
    for lat, (rest, mid) in enumerate(((rest0, mid0), (rest1, mid1))):
        out_ref[8 * lat : 8 * lat + 2] = rest[0:2]
        out_ref[8 * lat + 2 : 8 * lat + 5] = mid[0:3]
        out_ref[8 * lat + 5 : 8 * lat + 6] = gate[lat : lat + 1]
        out_ref[8 * lat + 6 : 8 * lat + 7] = mid[3:4]


def pack(arrays, after=()):
    width = arrays[0].shape[1]
    return call(
        pack_kernel, "pack", [], (1,), arrays, [whole(a.shape) for a in arrays],
        [((16, width), F32)], [whole((16, width))], 1, after,
    )[0]


def message_kernel(place_ref, mine, theirs, cond_ref, ub0, ub1, db0, db1, back0, half1, rest1, out_ref, low_ref):
    width = mine.shape[1]
    total = mine[...] + theirs[...]
    low_ref[...] = total.astype(BF).astype(F32)
    out_ref[...] = jnp.zeros_like(out_ref)
    unit = width // 2
    active = silu(cond_ref[...]).astype(F32)
    for lat in range(2):
        out_ref[lat : lat + 1, :width] = active[lat : lat + 1, :]
        for t in range(3):
            at = 3 * place_ref[0] + t
            cols = pl.ds(pl.multiple_of(lax.rem(at, 2) * unit, unit), unit)
            out_ref[lat : lat + 1, width + t * unit : width + (t + 1) * unit] = low_ref[
                pl.ds(8 * lat + lax.div(at, 2), 1), cols
            ]
    ff = ub0.shape[1]
    heads = half1.shape[1]
    out_ref[2:3, :ff] = ub0[...] + ub1[...]
    out_ref[2:3, ff : ff + width] = db0[...] + db1[...]
    at = ff + width
    for j in (0, 2):
        for t, other in enumerate((half1, rest1)):
            out_ref[2:3, at : at + heads] = back0[j : j + 1, t * heads : (t + 1) * heads] + other[j : j + 1]
            at += heads
    out_ref[3:4, :width] = total[6:7] + total[14:15]


def message(place, arrays, after=()):
    width = arrays[0].shape[1]
    ff, heads = arrays[3].shape[1], arrays[7].shape[1]
    shape = (4, max(width + 3 * (width // 2), ff + width + 2 * heads))
    return call(
        message_kernel, "message", [place], (1,), arrays, [whole(a.shape) for a in arrays],
        [(shape, F32), ((16, width), F32)], [whole(shape), whole((16, width))], 1, after,
    )


def join_kernel(mine, theirs, out_ref):
    rows = mine.shape[0] - 2
    out_ref[:rows] = mine[:rows]
    out_ref[rows : 2 * rows] = theirs[:rows]
    out_ref[2 * rows :] = mine[rows:] + theirs[rows:]


def join(mine, theirs, after=()):
    shape = (2 * mine.shape[0] - 2, mine.shape[1])
    return call(
        join_kernel, "join", [], (1,), [mine, theirs], [whole(mine.shape)] * 2,
        [(shape, F32)], [whole(shape)], 1, after,
    )[0]


def final_kernel(sizes, index_ref, mine, theirs, shard_ref, mod_ref, up_ref, down_ref, qv_ref, proj_ref):
    mod_rows, mod_cols, width, ff, heads = sizes
    rows = mine.shape[0] - 2
    here = pl.ds(pl.multiple_of(index_ref[0] * mod_rows, mod_rows), mod_rows)
    lows = jnp.concatenate([mine[:rows, width : width + mod_cols], theirs[:rows, width : width + mod_cols]], 0)
    active = jnp.concatenate([mine[:rows, here], theirs[:rows, here]], 0)
    shard_ref[...] = dot(active.astype(BF), lows.astype(BF), ROWS)
    mod_ref[...] = jnp.sum(lows, axis=0)
    sums = mine[rows : rows + 1, :] + theirs[rows : rows + 1, :]
    up_ref[...] = sums[0, :ff]
    down_ref[...] = sums[0, ff : ff + width]
    qv_ref[0:1] = sums[:, ff + width : ff + width + heads]
    qv_ref[1:2] = sums[:, ff + width + heads : ff + width + 2 * heads]
    proj_ref[...] = (mine[rows + 1 : rows + 2, :width] + theirs[rows + 1 : rows + 2, :width])[0]


def final(index, mine, theirs, *sizes):
    mod_rows, mod_cols, width, ff, heads = sizes
    shapes = [(mod_rows, mod_cols), (mod_cols,), (ff,), (width,), (2, heads), (width,)]
    return call(
        functools.partial(final_kernel, sizes), "final", [index], (1,),
        [mine, theirs], [whole(mine.shape)] * 2, [(a, F32) for a in shapes], [whole(a) for a in shapes], 2,
    )


def condition_kernel(low_ref, w_ref, cond_ref, out_ref, acc):
    j = pl.program_id(0)

    @pl.when(j == 0)
    def _():
        acc[...] = jnp.zeros_like(acc)

    rows = jnp.concatenate([low_ref[pl.ds(j, 1), :], low_ref[pl.ds(8 + j, 1), :]], 0)
    acc[...] += dot(rows.astype(BF), w_ref[...], COLS)

    @pl.when(j == pl.num_programs(0) - 1)
    def _():
        cond = cond_ref[...].astype(F32)
        sig = 1.0 / (1.0 + jnp.exp(-cond))
        out_ref[...] = acc[...] * (sig * (1.0 + cond * (1.0 - sig)))


def condition_grad(low, weight, cond, after=()):
    lats, width = cond.shape
    return call(
        condition_kernel, "condition_grad", [], (6,), [low, weight, cond],
        [whole(low.shape), pl.BlockSpec((width, width), lambda i: (0, i)), whole(cond.shape)],
        [((lats, width), F32)], [whole((lats, width))], 5, after, [pltpu.VMEM((lats, width), F32)],
    )[0]


def place_rows(pos_ref, send_ref, keep_ref, first, values, tiles):
    rows = send_ref.shape[0] * 2 // tiles
    for t in range(values.shape[0] // rows):
        pos = pos_ref[first + t]
        part = values[t * rows : (t + 1) * rows]

        @pl.when(pos < tiles // 2)
        def _():
            send_ref[pl.ds(pl.multiple_of(pos * rows, rows), rows), :] = part.astype(BF)

        @pl.when(pos >= tiles // 2)
        def _():
            keep_ref[pl.ds(pl.multiple_of((pos - tiles // 2) * rows, rows), rows), :] = part


def weight_kernel(tiles, lats, pos_ref, *refs):
    send_ref, keep_ref = refs[-2:]
    rows = send_ref.shape[0] * 2 // tiles
    total = None
    for l in range(lats):
        right = refs[lats + l]
        value = right[...] if len(right.shape) == 2 else jnp.concatenate([right[j] for j in range(3)], 1)
        part = dot(refs[l][...], value, ROWS)
        total = part if total is None else total + part
    first = pl.program_id(0) * (refs[0].shape[1] // rows)
    place_rows(pos_ref, send_ref, keep_ref, first, total, tiles)


def weight_grad(pos, lefts, rights, name, after=(), steps=1, parts=None):
    tiles = pos.shape[0]
    seq, depth = lefts[0].shape
    shape = rights[0].shape
    specs = [whole(shape)] * len(rights)
    if parts is not None:
        shape = shape[:-1] + (shape[-1] // parts[0][1],)
        specs = [
            pl.BlockSpec(a.shape[:-1] + (a.shape[-1] // n,), functools.partial(lambda at, *_: (0, 0, at), at))
            for a, (at, n) in zip(rights, parts)
        ]
    width = shape[1] if len(shape) == 2 else shape[0] * shape[2]
    block = depth // steps
    half = (depth // 2, width)
    return call(
        functools.partial(weight_kernel, tiles, len(lefts)), name, [pos], (steps,),
        [*lefts, *rights],
        [pl.BlockSpec((seq, block), lambda i, o: (0, i))] * len(lefts) + specs,
        [(half, BF), (half, F32)],
        [whole(half)] * 2,
        width / 128, after,
    )


def first_kernel(tiles, quarter, lats, order_ref, pos_ref, *refs):
    ins, lows, mixed, pieces = refs[:lats], refs[lats : 2 * lats], refs[2 * lats : 3 * lats], refs[3 * lats : -2]
    heads, proj = None, None
    for l in range(lats):
        part = dot(ins[l][...], jnp.concatenate([lows[l][j] for j in range(3)], 1), ROWS)
        heads = part if heads is None else heads + part
        for j in range(4):
            rows = pl.ds(pl.multiple_of(order_ref[j] * quarter, quarter), quarter)
            part = dot(pieces[4 * l + j][...], mixed[l][rows, :], ROWS)
            proj = part if proj is None else proj + part
    place_rows(pos_ref, refs[-2], refs[-1], 0, jnp.concatenate([heads, proj], 1), tiles)


def first_grad(order, pos, ins, lows, parts, mixed, pieces, after=()):
    tiles = pos.shape[0]
    quarter, width = pieces[0][0].shape
    args = [*ins, *lows, *mixed, *[p for four in pieces for p in four]]
    low_specs = [
        pl.BlockSpec(a.shape[:-1] + (a.shape[-1] // n,), functools.partial(lambda at, *_: (0, 0, at), at))
        for a, (at, n) in zip(lows, parts)
    ]
    cols = 3 * (lows[0].shape[2] // parts[0][1]) + mixed[0].shape[1]
    half = (width // 2, cols)
    return call(
        functools.partial(first_kernel, tiles, quarter, len(ins)), "first_grad", [order, pos], (1,),
        args,
        [whole(a.shape) for a in ins]
        + low_specs
        + [whole(a.shape) for a in args[2 * len(ins) :]],
        [(half, BF), (half, F32)],
        [whole(half)] * 2,
        6, after,
    )


def back_step(i, near_ref, pieces, p_ref, q_ref, k_ref, v_ref, total_ref, low_ref, bias_ref, dk_acc, dv_acc, grad_ref):
    rows, cols = q_ref.shape
    heads = cols // HEAD_DIM
    turned = dk_acc.shape[0] == cols

    @pl.when(i == 0)
    def _():
        dk_acc[...] = jnp.zeros_like(dk_acc)
        dv_acc[...] = jnp.zeros_like(dv_acc)

    for j in range(4):

        @pl.when(i == j)
        def _():
            grad_ref[...] = dot(pieces[j][...], p_ref[...], COLS).astype(BF)

    @pl.when(i < 4)
    def _():
        q = spread(q_ref[...] * BF(SCALE), heads)
        g = spread(grad_ref[...], heads)
        k, v = k_ref[...], v_ref[...]
        probs = jnp.exp(dot(k, q, COLS) - total_ref[0])
        grad_probs = dot(v, g, COLS)
        inner = jnp.sum(probs * grad_probs, axis=0, keepdims=True)
        scores = (probs * (grad_probs - inner)).astype(BF)
        probs = probs.astype(BF)
        if turned:
            dv_acc[...] += dot(g, probs, ((0,), (1,)))
            dk_acc[...] += dot(q, scores, ((0,), (1,)))
            every = dot(k, scores, ROWS)
            dq = jnp.concatenate(
                [every[h * HEAD_DIM : (h + 1) * HEAD_DIM, h * rows : (h + 1) * rows] for h in range(heads)], 0
            ).T
        else:
            dv_acc[...] += dot(probs, g)
            dk_acc[...] += dot(scores, q)
            every = dot(scores, k, ROWS)
            dq = every[:rows]
            for h in range(1, heads):
                dq = jnp.where(head_lanes(rows, cols, h), every[h * rows : (h + 1) * rows], dq)
        low_ref[0, pl.ds(pl.multiple_of(near_ref[i] * rows, rows), rows), :] = (dq * SCALE).astype(BF)

    @pl.when(i == 3)
    def _():
        low_ref[1] = (dk_acc[...].T if turned else dk_acc[...]).astype(BF)
        low_ref[2] = (dv_acc[...].T if turned else dv_acc[...]).astype(BF)
        bias_ref[...] = jnp.zeros_like(bias_ref)
        for j in range(3):
            bias_ref[j : j + 1] = jnp.sum(low_ref[j].astype(F32), axis=0, keepdims=True)


def back_kernel(near_ref, u0, u1, u2, u3, p_ref, q_ref, k_ref, v_ref, total_ref, low_ref, bias_ref, *scratch):
    back_step(
        pl.program_id(0), near_ref, (u0, u1, u2, u3), p_ref, q_ref, k_ref, v_ref, total_ref, low_ref, bias_ref,
        *scratch,
    )


def back_end_kernel(lat, others, near_ref, order_ref, u0, u1, u2, u3, p_ref, q_ref, k_ref, v_ref, total_ref, *refs):
    other_refs, (w_ref, tok_ref), refs = refs[:others], refs[others : others + 2], refs[others + 2 :]
    low_ref, bias_ref, send_ref, far_ref, own_ref, stat_ref = refs[:6]
    i = pl.program_id(0)
    rows = q_ref.shape[0]
    back_step(
        i, near_ref, (u0, u1, u2, u3), p_ref, q_ref, k_ref, v_ref, total_ref, low_ref, bias_ref, *refs[6:]
    )

    @pl.when(i == 0)
    def _():
        stat_ref[...] = jnp.zeros_like(stat_ref)

    @pl.when(i >= 4)
    def _():
        here = pl.ds(pl.multiple_of(order_ref[jnp.maximum(i - 4, 0)] * rows, rows), rows)
        out = None
        for j in range(3):
            parts = [ref[j, here, :] for ref in (*other_refs, low_ref)]
            part = dot(jnp.concatenate(parts, 1), w_ref[j], COLS)
            out = part if out is None else out + part
        normed, _ = normalize(tok_ref[...].astype(F32))
        stat_ref[0:1] += jnp.sum(out, axis=0, keepdims=True)
        stat_ref[1:2] += jnp.sum(out * normed, axis=0, keepdims=True)
        place_quarter(i - 4, out, send_ref, far_ref, own_ref)


def attend_back(near, order, pieces, proj, q, k, v, total, part, parts, lat, end=None, after=()):
    seq, cols = q.shape
    cols = cols // parts
    width = proj.shape[1]
    block = seq // 4
    heads = cols // HEAD_DIM
    first = lambda i, n, *_: n[jnp.minimum(i, 3)]
    later = lambda i, n, o: o[jnp.maximum(i - 4, 0)]
    keys = pl.BlockSpec((seq, cols), lambda *_: (0, part))
    ins = [*pieces, proj, q, k, v, total]
    in_specs = [whole((block, width))] * 4 + [
        pl.BlockSpec((cols, width), lambda *_: (part, 0)),
        pl.BlockSpec((block, cols), lambda *a: (first(*a), part)),
        keys,
        keys,
        pl.BlockSpec((1, 1, heads * block), lambda *a: (first(*a), 0, part)),
    ]
    outs = [((3, seq, cols), BF), ((8, cols), F32)]
    out_specs = [whole((3, seq, cols)), whole((8, cols))]
    sums = (seq, cols) if parts == 1 else (cols, seq)
    scratch = [pltpu.VMEM(sums, F32)] * 2 + [pltpu.VMEM((block, cols), BF)]
    if end is None:
        return call(
            back_kernel, "attend_backward", [near], (4,), ins, in_specs, outs, out_specs, 20 / parts, after, scratch
        )
    others, w3, tok = end
    quarter = ((block, width), F32)
    return call(
        functools.partial(back_end_kernel, lat, len(others)), "attend_backward_end", [near, order], (8,),
        ins + [*others, w3, tok],
        in_specs
        + [whole(other.shape) for other in others]
        + [whole(w3.shape)]
        + [pl.BlockSpec((block, width), lambda *a: (later(*a), 0))],
        outs + [((2 * block, width), F32), quarter, quarter, ((8, width), F32)],
        out_specs
        + [
            pl.BlockSpec((block, width), lambda i, *_: (jnp.clip(i - 4, 0, 1), 0)),
            whole((block, width)),
            whole((block, width)),
            whole((8, width)),
        ],
        20 / parts + 4, after, scratch,
    )


def tie(value, *others):
    return lax.optimization_barrier((value, *others))[0]


def far_kernel(*refs):
    out_ref = refs[-1]
    for j in range(len(refs) // 2):
        rows = refs[2 * j].shape[0]
        out_ref[j * rows : (j + 1) * rows] = (refs[2 * j][...] + refs[2 * j + 1][...].astype(F32)).astype(BF)


def far_sum(pairs, after=()):
    rows, width = pairs[0][0].shape
    ins = [a for pair in pairs for a in pair]
    shape = (rows * len(pairs), width)
    block = pl.BlockSpec((rows, width), lambda i: (0, 0))
    return call(
        far_kernel, "far_sum", [], (1,), ins, [block] * len(ins), [(shape, BF)], [whole(shape)], 1, after
    )[0]


def fold_kernel(*refs):
    count = len(refs) // 4
    for j in range(count):
        keep, got, send, kept = refs[2 * j], refs[2 * j + 1], refs[2 * count + 2 * j], refs[2 * count + 2 * j + 1]
        half = kept.shape[0]
        send[...] = (keep[:half] + got[:half].astype(F32)).astype(BF)
        kept[...] = keep[half:] + got[half:].astype(F32)


def fold(pairs, after=()):
    ins = [a for pair in pairs for a in pair]
    outs = []
    for keep, _ in pairs:
        half = (keep.shape[0] // 2, keep.shape[1])
        outs += [(half, BF), (half, F32)]
    got = call(
        fold_kernel, "fold", [], (1,), ins, [whole(a.shape) for a in ins], outs, [whole(o[0]) for o in outs], 2, after
    )
    return [(got[2 * j], got[2 * j + 1]) for j in range(len(pairs))]


def close_kernel(turns, *refs):
    outs = list(refs[2 * len(turns) :])
    for j, turn in enumerate(turns):
        total = refs[2 * j][...] + refs[2 * j + 1][...].astype(F32)
        if turn > 0:
            outs.pop(0)[...] = total[:, :turn]
        if turn < total.shape[1]:
            outs.pop(0)[...] = total[:, turn:].T


def close(pairs, turns, after=()):
    shapes = []
    for (keep, _), turn in zip(pairs, turns):
        rows, width = keep.shape
        shapes += ([(rows, turn)] if turn > 0 else []) + ([(width - turn, rows)] if turn < width else [])
    ins = [a for pair in pairs for a in pair]
    return call(
        functools.partial(close_kernel, turns), "close", [], (1,),
        ins, [whole(a.shape) for a in ins], [(a, F32) for a in shapes], [whole(a) for a in shapes], 1, after,
    )


def heads_kernel(split, one_ref, one_got, other_ref, other_got, qkv_ref, proj_ref):
    one = one_ref[...] + one_got[...].astype(F32)
    other = other_ref[...] + other_got[...].astype(F32)
    cols = split // 3
    for j in range(3):
        qkv_ref[j, :, :cols] = one[:, j * cols : (j + 1) * cols]
        qkv_ref[j, :, cols:] = other[:, j * cols : (j + 1) * cols]
    proj_ref[...] = one[:, split:].T


def close_heads(one, other, split, after=()):
    rows, width = one[0].shape
    ins = [*one, *other]
    shapes = [(3, rows, 2 * split // 3), (width - split, rows)]
    return call(
        functools.partial(heads_kernel, split), "close", [], (1,),
        ins, [whole(a.shape) for a in ins], [(a, F32) for a in shapes], [whole(a) for a in shapes], 1, after,
    )


def end_steps(keep, got, bits):
    for bit in bits:
        ((send, keep),) = fold([(keep, got)])
        got = swap(send, "dp", bit)
    return keep, got


def pieces_of(own, far):
    return own, far, swap(own, "tensor", 1), swap(far, "tensor", 1)


def dp_bits(size):
    return [1 << i for i in range(size.bit_length() - 1)]


def row_places(index, size, bits):
    away = jnp.arange(size, dtype=jnp.int32) ^ index
    place = jnp.zeros((size,), jnp.int32)
    for bit in bits:
        place = 2 * place + 1 - (away // bit) % 2
    return place


def shards(
    tokens,
    condition,
    modulation_weight,
    modulation_bias,
    qkv_weight,
    qv_bias,
    proj_weight,
    proj_bias,
    up_weight,
    up_bias,
    down_weight,
    down_bias,
    cotangent,
):
    seq, lats, width = tokens.shape
    place = lax.axis_index("tensor")
    index = lax.axis_index("dp")
    size = lax.axis_size("dp")
    quarter = seq // 4
    mod_cols = modulation_weight.shape[1] // 4
    order = jnp.array(SEND_FIRST, jnp.int32) ^ place
    near = jnp.array(NEAR_FIRST, jnp.int32) ^ place
    here = place[None]
    bits = dp_bits(size)
    other_bits = [bits[1], bits[0]] + bits[2:]
    places, other_places = row_places(index, size, bits), row_places(index, size, other_bits)
    to_dp = lambda value, bit: swap(value, "dp", bit)
    core = lambda value: swap(value, "tensor", 1)
    chip = lambda value: swap(value, "tensor", 2)

    proj_far = chip(proj_weight)
    w3 = jnp.transpose(qkv_weight, (1, 0, 2))
    heads = w3.shape[2]

    mod_one, (tokens0, in0, *qkv0), (tokens1, in1, *qkv1) = prepare(
        tokens, condition, modulation_weight, modulation_bias, w3, qv_bias
    )
    mixed0, total0 = attend(*qkv0, quarter, [proj_far])
    mixed_far0 = chip(mixed0)
    mod_two, mixed1, total1 = attend(
        *qkv1, quarter, [mixed0], [condition, modulation_weight, modulation_bias]
    )
    mixed_far1 = chip(mixed1)
    cot = jnp.transpose(tie(cotangent, mixed1), (1, 0, 2))
    proj = pieces_of(proj_weight, tie(proj_far, mixed1))
    gathered0 = pieces_of(mixed0, tie(mixed_far0, mod_two))

    feed_args = (cot, mod_two, up_weight, up_bias, down_weight)
    low0, hid0, pre0, gm0, upd0, tok0, cot0, send0, far0, own0, ub0, db0 = feed(
        order, gathered0, proj, proj_bias, tokens0, *feed_args, 0
    )
    near0 = core(send0)
    gathered1 = pieces_of(mixed1, tie(mixed_far1, own0))
    down0 = feed_down(order, hid0, down_weight)
    sum0 = far_sum([(far0, tie(near0, down0[1]))])
    grad_far0 = chip(sum0)
    low1, hid1, pre1, gm1, upd1, tok1, cot1, send1, far1, own1, ub1, db1 = feed(
        order, gathered1, proj, proj_bias, tokens1, *feed_args, 1, [sum0]
    )
    near1 = core(send1)
    g0, u0, stat0 = middle(own0, near0, tie(grad_far0, own1), upd0, tok0, cot0, mod_two, 0, [own1])
    u_far0 = chip(u0)
    down1 = feed_down(order, hid1, down_weight, [u0])
    sum1 = far_sum([(far1, tie(near1, down1[1]))])
    grad_far1 = chip(sum1)
    up_send, up_keep = weight_grad(places, [low0, low1], [pre0, pre1], "up_grad", [sum1])
    up_got = to_dp(up_send, bits[0])
    pieces0 = pieces_of(u0, tie(u_far0, up_keep))
    down_send, down_keep = weight_grad(other_places, [gm0, gm1], [hid0, hid1], "down_grad", [up_keep])
    down_got = to_dp(down_send, other_bits[0])
    g1, u1, stat1 = middle(own1, near1, tie(grad_far1, down_keep), upd1, tok1, cot1, mod_two, 1, [down_keep])
    u_far1 = chip(u1)

    back0 = attend_back(near, order, pieces0, proj_weight, *qkv0, total0, 0, 1, 0, ((), w3, tokens0), [u1])
    mlp_near0, mlp_near1 = core(tie(down0[0], u1)), core(tie(down1[0], u1))
    mlp_sum = far_sum([(down0[1], tie(mlp_near0, back0[1])), (down1[1], tie(mlp_near1, back0[1]))])
    mlp_far = chip(mlp_sum)
    in_near0 = core(back0[2])
    pieces1 = pieces_of(u1, tie(u_far1, back0[1]))
    (up_send, up_keep), (down_send, down_keep) = fold(
        [(up_keep, tie(up_got, back0[1])), (down_keep, tie(down_got, back0[1]))], [mlp_sum]
    )
    up_got, down_got = to_dp(up_send, bits[1]), to_dp(down_send, other_bits[1])
    in_sum0 = far_sum([(back0[3], tie(in_near0, up_keep))])
    in_far0 = chip(in_sum0)
    half1 = attend_back(near, order, pieces1, proj_weight, *qkv1, total1, 0, 2, 1, None, [in_sum0])
    (up_send, up_keep), (down_send, down_keep) = fold(
        [(up_keep, tie(up_got, half1[1])), (down_keep, tie(down_got, half1[1]))]
    )
    up_got, down_got = to_dp(up_send, bits[2]), to_dp(down_send, other_bits[2])
    first_send, first_keep = first_grad(
        near, places, [in0, in1], [back0[0], half1[0]], [(0, 2), (0, 1)], [mixed0, mixed1], [pieces0, pieces1],
        [up_keep],
    )
    first_got = to_dp(first_send, bits[0])
    output, gate = finish(
        (down0[2], mlp_near0, tie(mlp_far, first_keep), upd0, tok0, cot0),
        (down1[2], mlp_near1, tie(mlp_far, first_keep), upd1, tok1, cot1),
        mod_two, down_bias, [first_keep],
    )
    grad_tokens0 = last((back0[4], in_near0, tie(in_far0, gate), g0, tok0), mod_one, 0)
    ((first_send, first_keep),) = fold([(first_keep, tie(first_got, grad_tokens0))])
    first_got = to_dp(first_send, bits[1])
    rest1 = attend_back(
        near, order, pieces1, proj_weight, *qkv1, total1, 1, 2, 1, ((half1[0],), w3, tokens1), [first_keep]
    )

    in_near1 = core(rest1[2])
    mod = pack([back0[5], stat0, rest1[5], stat1, gate])
    mod_near = core(mod)
    second_send, second_keep = weight_grad(
        other_places, [in0, in1], [back0[0], rest1[0]], "qkv_grad", [mod, first_got], 1, [(1, 2), (0, 1)]
    )
    second_got = to_dp(second_send, other_bits[0])
    mod = mod + tie(mod_near, second_keep)
    mod_far = chip(mod)
    in_sum1 = far_sum([(rest1[3], tie(in_near1, mod))])
    in_far1 = chip(in_sum1)
    ((first_send, first_keep),) = fold([(first_keep, tie(first_got, in_sum1))])
    first_got = to_dp(first_send, bits[2])
    note, low_mod = message(
        here,
        [mod, tie(mod_far, first_keep), condition, ub0, ub1, db0, db1, back0[1], half1[1], rest1[1]],
    )
    note_got = to_dp(note, bits[0])
    up_shard, down_shard = close(
        [
            end_steps(up_keep, tie(up_got, note), bits[3:]),
            end_steps(down_keep, tie(down_got, note), other_bits[3:]),
        ],
        (width, 0),
    )
    ((second_send, second_keep),) = fold([(second_keep, tie(second_got, down_shard))])
    second_got = to_dp(second_send, other_bits[1])
    note = join(note, tie(note_got, second_keep))
    note_got = to_dp(note, bits[1])
    grad_condition = condition_grad(low_mod, modulation_weight, condition, [note])
    ((second_send, second_keep),) = fold([(second_keep, tie(second_got, grad_condition))])
    second_got = to_dp(second_send, other_bits[2])
    note = join(note, tie(note_got, second_keep))
    note_got = to_dp(note, bits[2])
    grad_tokens = last((rest1[4], in_near1, tie(in_far1, note), g1, tok1), mod_one, 1, grad_tokens0)
    first = end_steps(first_keep, tie(first_got, note), bits[3:])
    mod_rows = width // size
    ff = up_weight.shape[1]
    if len(bits) == 3 and mod_rows % 128 == 0:
        mod_shard, mod_bias_sum, up_bias_sum, down_bias_sum, qv_sum, proj_bias_sum = final(
            index[None], note, tie(note_got, grad_tokens), mod_rows, mod_cols, width, ff, heads
        )
    else:
        note = join(note, tie(note_got, grad_tokens))
        for bit in bits[3:]:
            note = join(note, to_dp(note, bit))
        rows = note.shape[0] - 2
        all_silu = note[:rows, :width].astype(BF)
        all_cols = note[:rows, width : width + mod_cols].astype(BF)
        my_silu = lax.dynamic_slice_in_dim(all_silu, index * mod_rows, mod_rows, 1)
        mod_shard = dot(my_silu, all_cols, ROWS)
        mod_bias_sum = jnp.sum(all_cols, axis=0, dtype=F32)
        up_bias_sum, down_bias_sum, qv_sum = jnp.split(note[rows, : ff + width + 2 * heads], [ff, ff + width])
        qv_sum = qv_sum.reshape(2, heads)
        proj_bias_sum = note[rows + 1, :width]
    second = end_steps(second_keep, tie(second_got, mod_shard), bits[3:])
    qkv_shard, proj_shard = close_heads(first, second, 3 * (heads // 2))
    qkv_shard = jnp.transpose(qkv_shard, (1, 0, 2))
    return (
        output,
        grad_tokens,
        grad_condition,
        mod_shard,
        mod_bias_sum,
        qkv_shard,
        qv_sum,
        proj_shard,
        proj_bias_sum,
        up_shard,
        up_bias_sum,
        down_shard,
        down_bias_sum,
    )


def solution(mesh):
    in_specs = (
        P(None, "dp", None),
        P("dp", None),
        P(),
        P(),
        P(None, None, "tensor"),
        P(None, "tensor"),
        P("tensor", None),
        P(),
        P(None, "tensor"),
        P("tensor"),
        P("tensor", None),
        P(),
        P(None, "dp", None),
    )
    out_specs = (
        P("tensor", "dp", None),
        P("tensor", "dp", None),
        P("dp", None),
        P("dp", "tensor"),
        P("tensor"),
        P("dp", None, "tensor"),
        P(None, "tensor"),
        P("tensor", "dp"),
        P(),
        P("dp", "tensor"),
        P("tensor"),
        P("tensor", "dp"),
        P(),
    )
    return jax.shard_map(shards, mesh=mesh, in_specs=in_specs, out_specs=out_specs, check_vma=False)
```

```python
import functools

import jax
import jax.numpy as jnp
from jax import lax
from jax.experimental import pallas as pl
from jax.experimental.pallas import tpu as pltpu
from jax.sharding import PartitionSpec as P

HEAD_DIM = 64
EPS = 1e-06
BF = jnp.bfloat16
F32 = jnp.float32
ROWS = ((0,), (0,))
COLS = ((1,), (1,))
MIB = 1 << 20
SCALE = HEAD_DIM**-0.5
SEND_FIRST = (3, 1, 2, 0)
NEAR_FIRST = (0, 2, 1, 3)
LIMITS = {
    "prepare": 60,
    "attend_forward": 16,
    "attend_modulate": 16,
    "feed": 24,
    "feed_down": 14,
    "far_sum": 8,
    "middle": 20,
    "up_grad": 20,
    "down_grad": 20,
    "qkv_grad": 24,
    "first_grad": 40,
    "fold": 24,
    "attend_backward": 20,
    "attend_backward_end": 32,
    "finish": 32,
    "grad_tokens": 60,
}


def dot(left, right, dims=((1,), (0,))):
    return lax.dot_general(left, right, (dims, ((), ())), preferred_element_type=F32)


def swap(value, axis, bit):
    pairs = [(i, i ^ bit) for i in range(lax.axis_size(axis))]
    return lax.ppermute(value, axis, pairs)


def normalize(values):
    centre = values - jnp.mean(values, axis=-1, keepdims=True)
    inverse = lax.rsqrt(jnp.mean(centre * centre, axis=-1, keepdims=True) + EPS)
    return centre * inverse, inverse


def norm_back(grad, normed, inverse):
    return inverse * (
        grad
        - jnp.mean(grad, axis=-1, keepdims=True)
        - normed * jnp.mean(grad * normed, axis=-1, keepdims=True)
    )


def gelu_pair(v):
    root = 0.7978845608028654
    square = v * v
    inner = jnp.tanh(v * (root + (root * 0.044715) * square))
    half = 0.5 + 0.5 * inner
    slope = half + (0.5 * v) * (1.0 - inner * inner) * (root + (3 * root * 0.044715) * square)
    return v * half, slope


def head_lanes(rows, cols, h):
    return lax.broadcasted_iota(jnp.int32, (rows, cols), 1) // HEAD_DIM == h


def spread(x, heads):
    rows, cols = x.shape
    zero = jnp.zeros_like(x)
    return jnp.concatenate([jnp.where(head_lanes(rows, cols, h), x, zero) for h in range(heads)], 0)


def whole(shape):
    return pl.BlockSpec(shape, lambda *_: (0,) * len(shape))


def shape_of(shape, dtype):
    return jax.ShapeDtypeStruct(shape, dtype)


def cost(expected):
    return pl.CostEstimate(flops=int(expected * 5.75e9), bytes_accessed=0, transcendentals=0)


ANY = pl.BlockSpec(memory_space=pl.ANY)
HBM = "hbm"


def call(kernel, name, scalars, grid, ins, in_specs, outs, out_specs, expected, after=(), scratch=()):
    skip = len(after)

    def body(*refs):
        first = len(scalars)
        kernel(*refs[:first], *refs[first + skip :])

    return pl.pallas_call(
        body,
        out_shape=[pltpu.HBM(*o[:2]) if len(o) > 2 else shape_of(*o) for o in outs],
        grid_spec=pltpu.PrefetchScalarGridSpec(
            num_scalar_prefetch=len(scalars),
            grid=grid,
            in_specs=[ANY] * skip + in_specs,
            out_specs=out_specs,
            scratch_shapes=list(scratch),
        ),
        compiler_params=pltpu.CompilerParams(vmem_limit_bytes=LIMITS.get(name, 16) * MIB),
        cost_estimate=cost(expected),
        name=name,
    )(*scalars, *after, *ins)


def silu(cond):
    value = cond.astype(F32)
    return (value * (1.0 / (1.0 + jnp.exp(-value)))).astype(BF)


def modulate(cond_ref, w_ref, bias_ref):
    return dot(silu(cond_ref[...]), w_ref[...]) + bias_ref[...].astype(F32)[None]


def mod_specs(cond, width, first):
    return [
        whole(cond.shape),
        pl.BlockSpec((width, width), lambda i: (0, first(i))),
        pl.BlockSpec((width,), lambda i: (first(i),)),
    ]


def prepare_kernel(tok_ref, w_ref, bias_ref, cond_ref, s_ref, sb_ref, cond_too, t_ref, tb_ref, mod_ref, *outs):
    rows, lats, width = tok_ref.shape

    @pl.when(pl.program_id(0) == 0)
    def _():
        mod_ref[:, :width] = modulate(cond_ref, s_ref, sb_ref)
        mod_ref[:, width:] = modulate(cond_too, t_ref, tb_ref)

    chunk = min(rows, 256 // lats)
    step = lats * chunk
    both = tok_ref[...].reshape(rows * lats, width)
    here = lax.broadcasted_iota(jnp.int32, (step, step), 0)
    there = lax.broadcasted_iota(jnp.int32, (step, step), 1)
    order = jnp.where(there == lats * lax.rem(here, chunk) + lax.div(here, chunk), 1.0, 0.0).astype(BF)
    split = [dot(order, both[j * step : (j + 1) * step]) for j in range(rows // chunk)]
    for lat in range(lats):
        x = jnp.concatenate([part[lat * chunk : (lat + 1) * chunk] for part in split], 0)
        tok_out, in_ref, q_ref, k_ref, v_ref = outs[5 * lat : 5 * lat + 5]
        tok_out[...] = x.astype(BF)
        row = lambda j: mod_ref[lat : lat + 1, j * width : (j + 1) * width]
        normed, _ = normalize(x)
        low = (normed * (1.0 + row(1)) + row(0)).astype(BF)
        in_ref[...] = low
        q_ref[...] = (dot(low, w_ref[0]) + bias_ref[0:1].astype(F32)).astype(BF)
        k_ref[...] = dot(low, w_ref[1]).astype(BF)
        v_ref[...] = (dot(low, w_ref[2]) + bias_ref[1:2].astype(F32)).astype(BF)


def prepare(tokens, cond, mod_weight, mod_bias, w3, bias, after=(), block=256):
    seq, lats, width = tokens.shape
    cols = w3.shape[2]
    rows = lambda n: pl.BlockSpec((block, n), lambda i: (i, 0))
    one = [((seq, width), BF, HBM)] * 2 + [((seq, cols), BF)] * 3
    got = call(
        prepare_kernel, "prepare", [], (seq // block,),
        [tokens, w3, bias] + [cond, mod_weight, mod_bias] * 2,
        [pl.BlockSpec((block, lats, width), lambda i: (i, 0, 0)), whole(w3.shape), whole(bias.shape)]
        + mod_specs(cond, width, lambda i: 0)
        + mod_specs(cond, width, lambda i: 1),
        [((lats, 2 * width), F32)] + one * lats,
        [whole((lats, 2 * width))] + [rows(width), rows(width), rows(cols), rows(cols), rows(cols)] * lats,
        12, after,
    )
    return got[0], got[1:6], got[6:11]


def attend_kernel(q_ref, k_ref, v_ref, *refs):
    mixed_ref, total_ref = refs[-2:]
    rows, cols = q_ref.shape
    heads = cols // HEAD_DIM
    value = v_ref[...].T
    scores = dot(k_ref[...], spread(q_ref[...] * BF(SCALE), heads), COLS)
    largest = jnp.max(scores, axis=0, keepdims=True)
    powers = jnp.exp(scores - largest)
    total = jnp.sum(powers, axis=0, keepdims=True)
    probs = (powers * (1.0 / total)).astype(BF)
    out = [
        dot(value[h * HEAD_DIM : (h + 1) * HEAD_DIM], probs[:, h * rows : (h + 1) * rows]) for h in range(heads)
    ]
    mixed_ref[...] = jnp.concatenate(out, 0).T.astype(BF)
    total_ref[0] = largest + jnp.log(total)
    if len(refs) > 2:
        cond_ref, w_ref, bias_ref, mod_ref = refs[:4]
        mod_ref[...] = modulate(cond_ref, w_ref, bias_ref)


def attend(q, k, v, block, after=(), mod=None):
    seq, cols = q.shape
    heads = cols // HEAD_DIM
    rows = pl.BlockSpec((block, cols), lambda i: (i, 0))
    ins, in_specs, outs, out_specs = [q, k, v], [rows, whole((seq, cols)), whole((seq, cols))], [], []
    if mod is not None:
        lats, width = mod[0].shape
        ins += mod
        in_specs += mod_specs(mod[0], width, lambda i: 2 + i)
        outs, out_specs = [((lats, 4 * width), F32)], [pl.BlockSpec((lats, width), lambda i: (0, i))]
    return call(
        attend_kernel, "attend_forward" if mod is None else "attend_modulate", [], (seq // block,), ins, in_specs,
        outs + [((seq, cols), BF), ((seq // block, 1, heads * block), F32)],
        out_specs + [rows, pl.BlockSpec((1, 1, heads * block), lambda i: (i, 0, 0))],
        8, after,
    )


def halves(block, width):
    return [
        pl.BlockSpec((block, width), lambda i, *_: (jnp.minimum(i, 1), 0)),
        whole((block, width)),
        whole((block, width)),
    ]


def place_quarter(step, value, send_ref, far_ref, own_ref):
    @pl.when(step < 2)
    def _():
        send_ref[...] = value.astype(send_ref.dtype)

    @pl.when(step == 2)
    def _():
        far_ref[...] = value

    @pl.when(step == 3)
    def _():
        own_ref[...] = value


def feed_kernel(
    lat, order_ref, m0, m1, m2, m3, p0, p1, p2, p3, pb_ref, tok_ref, cot_ref, mod_ref, up_ref, ub_ref, down_ref,
    in_ref, hid_ref, pre_ref, gm_ref, upd_ref, tok_out, cot_out, send_ref, far_ref, own_ref, gub_ref, gdb_ref,
):
    i = pl.program_id(0)
    width = tok_ref.shape[1]
    row = lambda j: mod_ref[lat : lat + 1, j * width : (j + 1) * width]
    update = pb_ref[...].astype(F32)[None]
    for m, p in ((m0, p0), (m1, p1), (m2, p2), (m3, p3)):
        update = update + dot(m[...], p[...])
    normed, _ = normalize(tok_ref[...].astype(F32) + row(0) * update)
    low = (normed * (1.0 + row(2)) + row(1)).astype(BF)
    in_ref[...] = low
    act, slope = gelu_pair(dot(low, up_ref[...]) + ub_ref[...].astype(F32)[None])
    hid_ref[...] = act.astype(BF)
    grad_mlp = (row(3) * cot_ref[0].astype(F32)).astype(BF)
    gm_ref[...] = grad_mlp
    grad_pre = (dot(grad_mlp, down_ref[...], COLS) * slope).astype(BF)
    pre_ref[...] = grad_pre
    place_quarter(i, dot(grad_pre, up_ref[...], COLS), send_ref, far_ref, own_ref)

    @pl.when(i == 3)
    def _():
        upd_ref[...] = update
        tok_out[...] = tok_ref[...]
        cot_out[...] = cot_ref[0]

    @pl.when(i == 0)
    def _():
        gub_ref[...] = jnp.zeros_like(gub_ref)
        gdb_ref[...] = jnp.zeros_like(gdb_ref)

    gub_ref[...] += jnp.sum(grad_pre.astype(F32), axis=0, keepdims=True)
    gdb_ref[...] += jnp.sum(grad_mlp.astype(F32), axis=0, keepdims=True)


def feed(order, mixed, proj, proj_bias, tok, cot, mod, up, up_bias, down, lat, after=()):
    seq, width = tok.shape
    block = seq // 4
    ff = up.shape[1]
    cols = mixed[0].shape[1]
    at = lambda n: pl.BlockSpec((block, n), lambda i, o: (o[i], 0))
    at3 = pl.BlockSpec((1, block, width), lambda i, o: (lat, o[i], 0))
    quarter = ((block, width), F32)
    return call(
        functools.partial(feed_kernel, lat), "feed", [order], (4,),
        [*mixed, *proj, proj_bias, tok, cot, mod, up, up_bias, down],
        [at(cols)] * 4
        + [whole((cols, width))] * 4
        + [whole((width,)), at(width), at3, whole(mod.shape)]
        + [whole(up.shape), whole((ff,)), whole(down.shape)],
        [((seq, width), BF), ((seq, ff), BF), ((seq, ff), BF), ((seq, width), BF), quarter]
        + [((block, width), BF)] * 2
        + [((2 * block, width), F32), quarter, quarter, ((1, ff), F32), ((1, width), F32)],
        [at(width), at(ff), at(ff), at(width)]
        + [whole((block, width))] * 3
        + halves(block, width)
        + [whole((1, ff)), whole((1, width))],
        18, after,
    )


def down_kernel(order_ref, hid_ref, down_ref, send_ref, far_ref, own_ref):
    out = dot(hid_ref[...], down_ref[...])
    place_quarter(pl.program_id(0), out, send_ref, far_ref, own_ref)


def feed_down(order, hidden, down, after=()):
    seq, ff = hidden.shape
    width = down.shape[1]
    block = seq // 4
    quarter = ((block, width), F32)
    return call(
        down_kernel, "feed_down", [order], (4,),
        [hidden, down],
        [pl.BlockSpec((block, ff), lambda i, o: (o[i], 0)), whole(down.shape)],
        [((2 * block, width), BF), quarter, quarter],
        halves(block, width),
        5, after,
    )


def row_blocks(rows, width, skip=0, steps=1):
    return pl.BlockSpec((rows // steps, width), lambda i: (skip * steps + i, 0))


def add_stats(ref, values, first=0):
    @pl.when(pl.program_id(0) == 0)
    def _():
        ref[first : first + len(values)] = jnp.zeros((len(values), ref.shape[1]), F32)

    for j, value in enumerate(values):
        ref[first + j : first + j + 1] += jnp.sum(value, axis=0, keepdims=True)


def middle_kernel(lat, own, near, far, upd_ref, tok_ref, cot_ref, mod_ref, g_ref, low_ref, stat_ref):
    width = upd_ref.shape[1]
    row = lambda j: mod_ref[lat : lat + 1, j * width : (j + 1) * width]
    grad_in = own[...] + near[...] + far[...].astype(F32)
    update = upd_ref[...]
    normed, inverse = normalize(tok_ref[...].astype(F32) + row(0) * update)
    grad = cot_ref[...].astype(F32) + norm_back(grad_in * (1.0 + row(2)), normed, inverse)
    g_ref[...] = grad
    low = (row(0) * grad).astype(BF)
    low_ref[...] = low
    add_stats(stat_ref, (grad * update, grad_in, grad_in * normed, low.astype(F32)))


def middle(own, near, far, update, tok, cot, mod, lat, after=()):
    rows, width = own.shape
    mine = row_blocks(rows, width, 0, 2)
    return call(
        functools.partial(middle_kernel, lat), "middle", [], (2,),
        [own, near, far, update, tok, cot, mod],
        [mine, row_blocks(rows, width, 1, 2)] + [mine] * 4 + [whole(mod.shape)],
        [((rows, width), F32, HBM), ((rows, width), BF), ((4, width), F32)],
        [mine, mine, whole((4, width))],
        2, after,
    )


def finish_kernel(*refs):
    mod_ref, bias_ref, out_ref, stat_ref = refs[-4:]
    width = mod_ref.shape[1] // 4
    for lat in range(2):
        own, near, far, upd, tok, cot = refs[6 * lat : 6 * lat + 6]
        row = lambda j: mod_ref[lat : lat + 1, j * width : (j + 1) * width]
        update = own[...] + near[...].astype(F32) + far[...].astype(F32) + bias_ref[...].astype(F32)[None]
        stream = tok[...].astype(F32) + row(0) * upd[...]
        out_ref[:, lat, :] = (stream + row(3) * update).astype(BF)
        add_stats(stat_ref, (cot[...].astype(F32) * update,), lat)


def finish(first, other, mod, bias, after=()):
    rows, width = first[0].shape
    mine = row_blocks(rows, width)
    one = lambda lat: [mine, row_blocks(rows, width, 1), row_blocks(rows, width, lat)] + [mine] * 3
    return call(
        finish_kernel, "finish", [], (1,),
        [*first, *other, mod, bias],
        one(0) + one(1) + [whole(mod.shape), whole((width,))],
        [((rows, 2, width), BF), ((2, width), F32)],
        [whole((rows, 2, width)), whole((2, width))],
        4, after,
    )


def last_kernel(lat, *refs):
    own, near, far, g_ref, tok, mod_ref = refs[:6]
    out_ref = refs[-1]
    width = mod_ref.shape[1] // 2
    grad_in = own[...] + near[...] + far[...].astype(F32)
    normed, inverse = normalize(tok[...].astype(F32))
    scale = 1.0 + mod_ref[lat : lat + 1, width : 2 * width]
    out = g_ref[...] + norm_back(grad_in * scale, normed, inverse)
    if lat == 0:
        out_ref[...] = out
    else:
        out_ref[:, 0, :] = refs[6][...]
        out_ref[:, 1, :] = out


def last(arrays, mod, lat, other=None, after=()):
    rows, width = arrays[0].shape
    steps = 2
    mine = row_blocks(rows, width, 0, steps)
    both = [] if other is None else [other]
    shape, block = (
        ((rows, width), mine) if lat == 0
        else ((rows, 2, width), pl.BlockSpec((rows // steps, 2, width), lambda i: (i, 0, 0)))
    )
    return call(
        functools.partial(last_kernel, lat), "grad_tokens", [], (steps,),
        [*arrays, mod, *both],
        [mine, row_blocks(rows, width, 1, steps)] + [mine] * 3 + [whole(mod.shape)] + [mine] * len(both),
        [(shape, F32) if lat == 0 else (shape, F32, HBM)],
        [block],
        3, after,
    )[0]


def pack_kernel(rest0, mid0, rest1, mid1, gate, out_ref):
    out_ref[...] = jnp.zeros_like(out_ref)
    for lat, (rest, mid) in enumerate(((rest0, mid0), (rest1, mid1))):
        out_ref[8 * lat : 8 * lat + 2] = rest[0:2]
        out_ref[8 * lat + 2 : 8 * lat + 5] = mid[0:3]
        out_ref[8 * lat + 5 : 8 * lat + 6] = gate[lat : lat + 1]
        out_ref[8 * lat + 6 : 8 * lat + 7] = mid[3:4]


def pack(arrays, after=()):
    width = arrays[0].shape[1]
    return call(
        pack_kernel, "pack", [], (1,), arrays, [whole(a.shape) for a in arrays],
        [((16, width), F32)], [whole((16, width))], 1, after,
    )[0]


def message_kernel(place_ref, mine, theirs, cond_ref, ub0, ub1, db0, db1, back0, half1, rest1, out_ref, low_ref):
    width = mine.shape[1]
    total = mine[...] + theirs[...]
    low_ref[...] = total.astype(BF).astype(F32)
    out_ref[...] = jnp.zeros_like(out_ref)
    unit = width // 2
    active = silu(cond_ref[...]).astype(F32)
    for lat in range(2):
        out_ref[lat : lat + 1, :width] = active[lat : lat + 1, :]
        for t in range(3):
            at = 3 * place_ref[0] + t
            cols = pl.ds(pl.multiple_of(lax.rem(at, 2) * unit, unit), unit)
            out_ref[lat : lat + 1, width + t * unit : width + (t + 1) * unit] = low_ref[
                pl.ds(8 * lat + lax.div(at, 2), 1), cols
            ]
    ff = ub0.shape[1]
    heads = half1.shape[1]
    out_ref[2:3, :ff] = ub0[...] + ub1[...]
    out_ref[2:3, ff : ff + width] = db0[...] + db1[...]
    at = ff + width
    for j in (0, 2):
        for t, other in enumerate((half1, rest1)):
            out_ref[2:3, at : at + heads] = back0[j : j + 1, t * heads : (t + 1) * heads] + other[j : j + 1]
            at += heads
    out_ref[3:4, :width] = total[6:7] + total[14:15]


def message(place, arrays, after=()):
    width = arrays[0].shape[1]
    ff, heads = arrays[3].shape[1], arrays[7].shape[1]
    shape = (4, max(width + 3 * (width // 2), ff + width + 2 * heads))
    return call(
        message_kernel, "message", [place], (1,), arrays, [whole(a.shape) for a in arrays],
        [(shape, F32), ((16, width), F32)], [whole(shape), whole((16, width))], 1, after,
    )


def join_kernel(mine, theirs, out_ref):
    rows = mine.shape[0] - 2
    out_ref[:rows] = mine[:rows]
    out_ref[rows : 2 * rows] = theirs[:rows]
    out_ref[2 * rows :] = mine[rows:] + theirs[rows:]


def join(mine, theirs, after=()):
    shape = (2 * mine.shape[0] - 2, mine.shape[1])
    return call(
        join_kernel, "join", [], (1,), [mine, theirs], [whole(mine.shape)] * 2,
        [(shape, F32)], [whole(shape)], 1, after,
    )[0]


def final_kernel(sizes, index_ref, mine, theirs, shard_ref, mod_ref, up_ref, down_ref, qv_ref, proj_ref):
    mod_rows, mod_cols, width, ff, heads = sizes
    rows = mine.shape[0] - 2
    here = pl.ds(pl.multiple_of(index_ref[0] * mod_rows, mod_rows), mod_rows)
    lows = jnp.concatenate([mine[:rows, width : width + mod_cols], theirs[:rows, width : width + mod_cols]], 0)
    active = jnp.concatenate([mine[:rows, here], theirs[:rows, here]], 0)
    shard_ref[...] = dot(active.astype(BF), lows.astype(BF), ROWS)
    mod_ref[...] = jnp.sum(lows, axis=0)
    sums = mine[rows : rows + 1, :] + theirs[rows : rows + 1, :]
    up_ref[...] = sums[0, :ff]
    down_ref[...] = sums[0, ff : ff + width]
    qv_ref[0:1] = sums[:, ff + width : ff + width + heads]
    qv_ref[1:2] = sums[:, ff + width + heads : ff + width + 2 * heads]
    proj_ref[...] = (mine[rows + 1 : rows + 2, :width] + theirs[rows + 1 : rows + 2, :width])[0]


def final(index, mine, theirs, *sizes):
    mod_rows, mod_cols, width, ff, heads = sizes
    shapes = [(mod_rows, mod_cols), (mod_cols,), (ff,), (width,), (2, heads), (width,)]
    return call(
        functools.partial(final_kernel, sizes), "final", [index], (1,),
        [mine, theirs], [whole(mine.shape)] * 2, [(a, F32) for a in shapes], [whole(a) for a in shapes], 2,
    )


def condition_kernel(low_ref, w_ref, cond_ref, out_ref, acc):
    j = pl.program_id(0)

    @pl.when(j == 0)
    def _():
        acc[...] = jnp.zeros_like(acc)

    rows = jnp.concatenate([low_ref[pl.ds(j, 1), :], low_ref[pl.ds(8 + j, 1), :]], 0)
    acc[...] += dot(rows.astype(BF), w_ref[...], COLS)

    @pl.when(j == pl.num_programs(0) - 1)
    def _():
        cond = cond_ref[...].astype(F32)
        sig = 1.0 / (1.0 + jnp.exp(-cond))
        out_ref[...] = acc[...] * (sig * (1.0 + cond * (1.0 - sig)))


def condition_grad(low, weight, cond, after=()):
    lats, width = cond.shape
    return call(
        condition_kernel, "condition_grad", [], (6,), [low, weight, cond],
        [whole(low.shape), pl.BlockSpec((width, width), lambda i: (0, i)), whole(cond.shape)],
        [((lats, width), F32)], [whole((lats, width))], 5, after, [pltpu.VMEM((lats, width), F32)],
    )[0]


def place_rows(pos_ref, send_ref, keep_ref, first, values, tiles):
    rows = send_ref.shape[0] * 2 // tiles
    for t in range(values.shape[0] // rows):
        pos = pos_ref[first + t]
        part = values[t * rows : (t + 1) * rows]

        @pl.when(pos < tiles // 2)
        def _():
            send_ref[pl.ds(pl.multiple_of(pos * rows, rows), rows), :] = part.astype(BF)

        @pl.when(pos >= tiles // 2)
        def _():
            keep_ref[pl.ds(pl.multiple_of((pos - tiles // 2) * rows, rows), rows), :] = part


def weight_kernel(tiles, lats, pos_ref, *refs):
    send_ref, keep_ref = refs[-2:]
    rows = send_ref.shape[0] * 2 // tiles
    total = None
    for l in range(lats):
        right = refs[lats + l]
        value = right[...] if len(right.shape) == 2 else jnp.concatenate([right[j] for j in range(3)], 1)
        part = dot(refs[l][...], value, ROWS)
        total = part if total is None else total + part
    first = pl.program_id(0) * (refs[0].shape[1] // rows)
    place_rows(pos_ref, send_ref, keep_ref, first, total, tiles)


def weight_grad(pos, lefts, rights, name, after=(), steps=1, parts=None):
    tiles = pos.shape[0]
    seq, depth = lefts[0].shape
    shape = rights[0].shape
    specs = [whole(shape)] * len(rights)
    if parts is not None:
        shape = shape[:-1] + (shape[-1] // parts[0][1],)
        specs = [
            pl.BlockSpec(a.shape[:-1] + (a.shape[-1] // n,), functools.partial(lambda at, *_: (0, 0, at), at))
            for a, (at, n) in zip(rights, parts)
        ]
    width = shape[1] if len(shape) == 2 else shape[0] * shape[2]
    block = depth // steps
    half = (depth // 2, width)
    return call(
        functools.partial(weight_kernel, tiles, len(lefts)), name, [pos], (steps,),
        [*lefts, *rights],
        [pl.BlockSpec((seq, block), lambda i, o: (0, i))] * len(lefts) + specs,
        [(half, BF), (half, F32)],
        [whole(half)] * 2,
        width / 128, after,
    )


def first_kernel(tiles, quarter, lats, order_ref, pos_ref, *refs):
    ins, lows, mixed, pieces = refs[:lats], refs[lats : 2 * lats], refs[2 * lats : 3 * lats], refs[3 * lats : -2]
    heads, proj = None, None
    for l in range(lats):
        part = dot(ins[l][...], jnp.concatenate([lows[l][j] for j in range(3)], 1), ROWS)
        heads = part if heads is None else heads + part
        for j in range(4):
            rows = pl.ds(pl.multiple_of(order_ref[j] * quarter, quarter), quarter)
            part = dot(pieces[4 * l + j][...], mixed[l][rows, :], ROWS)
            proj = part if proj is None else proj + part
    place_rows(pos_ref, refs[-2], refs[-1], 0, jnp.concatenate([heads, proj], 1), tiles)


def first_grad(order, pos, ins, lows, parts, mixed, pieces, after=()):
    tiles = pos.shape[0]
    quarter, width = pieces[0][0].shape
    args = [*ins, *lows, *mixed, *[p for four in pieces for p in four]]
    low_specs = [
        pl.BlockSpec(a.shape[:-1] + (a.shape[-1] // n,), functools.partial(lambda at, *_: (0, 0, at), at))
        for a, (at, n) in zip(lows, parts)
    ]
    cols = 3 * (lows[0].shape[2] // parts[0][1]) + mixed[0].shape[1]
    half = (width // 2, cols)
    return call(
        functools.partial(first_kernel, tiles, quarter, len(ins)), "first_grad", [order, pos], (1,),
        args,
        [whole(a.shape) for a in ins]
        + low_specs
        + [whole(a.shape) for a in args[2 * len(ins) :]],
        [(half, BF), (half, F32)],
        [whole(half)] * 2,
        6, after,
    )


def back_step(i, near_ref, pieces, p_ref, q_ref, k_ref, v_ref, total_ref, low_ref, bias_ref, dk_acc, dv_acc, grad_ref):
    rows, cols = q_ref.shape
    heads = cols // HEAD_DIM
    turned = dk_acc.shape[0] == cols

    @pl.when(i == 0)
    def _():
        dk_acc[...] = jnp.zeros_like(dk_acc)
        dv_acc[...] = jnp.zeros_like(dv_acc)

    for j in range(4):

        @pl.when(i == j)
        def _():
            grad_ref[...] = dot(pieces[j][...], p_ref[...], COLS).astype(BF)

    @pl.when(i < 4)
    def _():
        q = spread(q_ref[...] * BF(SCALE), heads)
        g = spread(grad_ref[...], heads)
        k, v = k_ref[...], v_ref[...]
        probs = jnp.exp(dot(k, q, COLS) - total_ref[0])
        grad_probs = dot(v, g, COLS)
        inner = jnp.sum(probs * grad_probs, axis=0, keepdims=True)
        scores = (probs * (grad_probs - inner)).astype(BF)
        probs = probs.astype(BF)
        if turned:
            dv_acc[...] += dot(g, probs, ((0,), (1,)))
            dk_acc[...] += dot(q, scores, ((0,), (1,)))
            every = dot(k, scores, ROWS)
            dq = jnp.concatenate(
                [every[h * HEAD_DIM : (h + 1) * HEAD_DIM, h * rows : (h + 1) * rows] for h in range(heads)], 0
            ).T
        else:
            dv_acc[...] += dot(probs, g)
            dk_acc[...] += dot(scores, q)
            every = dot(scores, k, ROWS)
            dq = every[:rows]
            for h in range(1, heads):
                dq = jnp.where(head_lanes(rows, cols, h), every[h * rows : (h + 1) * rows], dq)
        low_ref[0, pl.ds(pl.multiple_of(near_ref[i] * rows, rows), rows), :] = (dq * SCALE).astype(BF)

    @pl.when(i == 3)
    def _():
        low_ref[1] = (dk_acc[...].T if turned else dk_acc[...]).astype(BF)
        low_ref[2] = (dv_acc[...].T if turned else dv_acc[...]).astype(BF)
        bias_ref[...] = jnp.zeros_like(bias_ref)
        for j in range(3):
            bias_ref[j : j + 1] = jnp.sum(low_ref[j].astype(F32), axis=0, keepdims=True)


def back_kernel(near_ref, u0, u1, u2, u3, p_ref, q_ref, k_ref, v_ref, total_ref, low_ref, bias_ref, *scratch):
    back_step(
        pl.program_id(0), near_ref, (u0, u1, u2, u3), p_ref, q_ref, k_ref, v_ref, total_ref, low_ref, bias_ref,
        *scratch,
    )


def back_end_kernel(lat, others, near_ref, order_ref, u0, u1, u2, u3, p_ref, q_ref, k_ref, v_ref, total_ref, *refs):
    other_refs, (w_ref, tok_ref), refs = refs[:others], refs[others : others + 2], refs[others + 2 :]
    low_ref, bias_ref, send_ref, far_ref, own_ref, stat_ref = refs[:6]
    i = pl.program_id(0)
    rows = q_ref.shape[0]
    back_step(
        i, near_ref, (u0, u1, u2, u3), p_ref, q_ref, k_ref, v_ref, total_ref, low_ref, bias_ref, *refs[6:]
    )

    @pl.when(i == 0)
    def _():
        stat_ref[...] = jnp.zeros_like(stat_ref)

    @pl.when(i >= 4)
    def _():
        here = pl.ds(pl.multiple_of(order_ref[jnp.maximum(i - 4, 0)] * rows, rows), rows)
        out = None
        for j in range(3):
            parts = [ref[j, here, :] for ref in (*other_refs, low_ref)]
            part = dot(jnp.concatenate(parts, 1), w_ref[j], COLS)
            out = part if out is None else out + part
        normed, _ = normalize(tok_ref[...].astype(F32))
        stat_ref[0:1] += jnp.sum(out, axis=0, keepdims=True)
        stat_ref[1:2] += jnp.sum(out * normed, axis=0, keepdims=True)
        place_quarter(i - 4, out, send_ref, far_ref, own_ref)


def attend_back(near, order, pieces, proj, q, k, v, total, part, parts, lat, end=None, after=()):
    seq, cols = q.shape
    cols = cols // parts
    width = proj.shape[1]
    block = seq // 4
    heads = cols // HEAD_DIM
    first = lambda i, n, *_: n[jnp.minimum(i, 3)]
    later = lambda i, n, o: o[jnp.maximum(i - 4, 0)]
    keys = pl.BlockSpec((seq, cols), lambda *_: (0, part))
    ins = [*pieces, proj, q, k, v, total]
    in_specs = [whole((block, width))] * 4 + [
        pl.BlockSpec((cols, width), lambda *_: (part, 0)),
        pl.BlockSpec((block, cols), lambda *a: (first(*a), part)),
        keys,
        keys,
        pl.BlockSpec((1, 1, heads * block), lambda *a: (first(*a), 0, part)),
    ]
    outs = [((3, seq, cols), BF), ((8, cols), F32)]
    out_specs = [whole((3, seq, cols)), whole((8, cols))]
    sums = (seq, cols) if parts == 1 else (cols, seq)
    scratch = [pltpu.VMEM(sums, F32)] * 2 + [pltpu.VMEM((block, cols), BF)]
    if end is None:
        return call(
            back_kernel, "attend_backward", [near], (4,), ins, in_specs, outs, out_specs, 20 / parts, after, scratch
        )
    others, w3, tok = end
    quarter = ((block, width), F32)
    return call(
        functools.partial(back_end_kernel, lat, len(others)), "attend_backward_end", [near, order], (8,),
        ins + [*others, w3, tok],
        in_specs
        + [whole(other.shape) for other in others]
        + [whole(w3.shape)]
        + [pl.BlockSpec((block, width), lambda *a: (later(*a), 0))],
        outs + [((2 * block, width), F32), quarter, quarter, ((8, width), F32)],
        out_specs
        + [
            pl.BlockSpec((block, width), lambda i, *_: (jnp.clip(i - 4, 0, 1), 0)),
            whole((block, width)),
            whole((block, width)),
            whole((8, width)),
        ],
        20 / parts + 4, after, scratch,
    )


def tie(value, *others):
    return lax.optimization_barrier((value, *others))[0]


def far_kernel(*refs):
    out_ref = refs[-1]
    for j in range(len(refs) // 2):
        rows = refs[2 * j].shape[0]
        out_ref[j * rows : (j + 1) * rows] = (refs[2 * j][...] + refs[2 * j + 1][...].astype(F32)).astype(BF)


def far_sum(pairs, after=()):
    rows, width = pairs[0][0].shape
    ins = [a for pair in pairs for a in pair]
    shape = (rows * len(pairs), width)
    block = pl.BlockSpec((rows, width), lambda i: (0, 0))
    return call(
        far_kernel, "far_sum", [], (1,), ins, [block] * len(ins), [(shape, BF)], [whole(shape)], 1, after
    )[0]


def fold_kernel(*refs):
    count = len(refs) // 4
    for j in range(count):
        keep, got, send, kept = refs[2 * j], refs[2 * j + 1], refs[2 * count + 2 * j], refs[2 * count + 2 * j + 1]
        half = kept.shape[0]
        send[...] = (keep[:half] + got[:half].astype(F32)).astype(BF)
        kept[...] = keep[half:] + got[half:].astype(F32)


def fold(pairs, after=()):
    ins = [a for pair in pairs for a in pair]
    outs = []
    for keep, _ in pairs:
        half = (keep.shape[0] // 2, keep.shape[1])
        outs += [(half, BF), (half, F32)]
    got = call(
        fold_kernel, "fold", [], (1,), ins, [whole(a.shape) for a in ins], outs, [whole(o[0]) for o in outs], 2, after
    )
    return [(got[2 * j], got[2 * j + 1]) for j in range(len(pairs))]


def close_kernel(turns, *refs):
    outs = list(refs[2 * len(turns) :])
    for j, turn in enumerate(turns):
        total = refs[2 * j][...] + refs[2 * j + 1][...].astype(F32)
        if turn > 0:
            outs.pop(0)[...] = total[:, :turn]
        if turn < total.shape[1]:
            outs.pop(0)[...] = total[:, turn:].T


def close(pairs, turns, after=()):
    shapes = []
    for (keep, _), turn in zip(pairs, turns):
        rows, width = keep.shape
        shapes += ([(rows, turn)] if turn > 0 else []) + ([(width - turn, rows)] if turn < width else [])
    ins = [a for pair in pairs for a in pair]
    return call(
        functools.partial(close_kernel, turns), "close", [], (1,),
        ins, [whole(a.shape) for a in ins], [(a, F32) for a in shapes], [whole(a) for a in shapes], 1, after,
    )


def heads_kernel(split, one_ref, one_got, other_ref, other_got, qkv_ref, proj_ref):
    one = one_ref[...] + one_got[...].astype(F32)
    other = other_ref[...] + other_got[...].astype(F32)
    cols = split // 3
    for j in range(3):
        qkv_ref[j, :, :cols] = one[:, j * cols : (j + 1) * cols]
        qkv_ref[j, :, cols:] = other[:, j * cols : (j + 1) * cols]
    proj_ref[...] = one[:, split:].T


def close_heads(one, other, split, after=()):
    rows, width = one[0].shape
    ins = [*one, *other]
    shapes = [(3, rows, 2 * split // 3), (width - split, rows)]
    return call(
        functools.partial(heads_kernel, split), "close", [], (1,),
        ins, [whole(a.shape) for a in ins], [(a, F32) for a in shapes], [whole(a) for a in shapes], 1, after,
    )


def end_steps(keep, got, bits):
    for bit in bits:
        ((send, keep),) = fold([(keep, got)])
        got = swap(send, "dp", bit)
    return keep, got


def pieces_of(own, far):
    return own, far, swap(own, "tensor", 1), swap(far, "tensor", 1)


def dp_bits(size):
    return [1 << i for i in range(size.bit_length() - 1)]


def row_places(index, size, bits):
    away = jnp.arange(size, dtype=jnp.int32) ^ index
    place = jnp.zeros((size,), jnp.int32)
    for bit in bits:
        place = 2 * place + 1 - (away // bit) % 2
    return place


def shards(
    tokens,
    condition,
    modulation_weight,
    modulation_bias,
    qkv_weight,
    qv_bias,
    proj_weight,
    proj_bias,
    up_weight,
    up_bias,
    down_weight,
    down_bias,
    cotangent,
):
    seq, lats, width = tokens.shape
    place = lax.axis_index("tensor")
    index = lax.axis_index("dp")
    size = lax.axis_size("dp")
    quarter = seq // 4
    mod_cols = modulation_weight.shape[1] // 4
    order = jnp.array(SEND_FIRST, jnp.int32) ^ place
    near = jnp.array(NEAR_FIRST, jnp.int32) ^ place
    here = place[None]
    bits = dp_bits(size)
    other_bits = [bits[1], bits[0]] + bits[2:]
    places, other_places = row_places(index, size, bits), row_places(index, size, other_bits)
    to_dp = lambda value, bit: swap(value, "dp", bit)
    core = lambda value: swap(value, "tensor", 1)
    chip = lambda value: swap(value, "tensor", 2)

    proj_far = chip(proj_weight)
    w3 = jnp.transpose(qkv_weight, (1, 0, 2))
    heads = w3.shape[2]

    mod_one, (tokens0, in0, *qkv0), (tokens1, in1, *qkv1) = prepare(
        tokens, condition, modulation_weight, modulation_bias, w3, qv_bias
    )
    mixed0, total0 = attend(*qkv0, quarter, [proj_far])
    mixed_far0 = chip(mixed0)
    mod_two, mixed1, total1 = attend(
        *qkv1, quarter, [mixed0], [condition, modulation_weight, modulation_bias]
    )
    mixed_far1 = chip(mixed1)
    cot = jnp.transpose(tie(cotangent, mixed1), (1, 0, 2))
    proj = pieces_of(proj_weight, tie(proj_far, mixed1))
    gathered0 = pieces_of(mixed0, tie(mixed_far0, mod_two))

    feed_args = (cot, mod_two, up_weight, up_bias, down_weight)
    low0, hid0, pre0, gm0, upd0, tok0, cot0, send0, far0, own0, ub0, db0 = feed(
        order, gathered0, proj, proj_bias, tokens0, *feed_args, 0
    )
    near0 = core(send0)
    gathered1 = pieces_of(mixed1, tie(mixed_far1, own0))
    down0 = feed_down(order, hid0, down_weight)
    sum0 = far_sum([(far0, tie(near0, down0[1]))])
    grad_far0 = chip(sum0)
    low1, hid1, pre1, gm1, upd1, tok1, cot1, send1, far1, own1, ub1, db1 = feed(
        order, gathered1, proj, proj_bias, tokens1, *feed_args, 1, [sum0]
    )
    near1 = core(send1)
    g0, u0, stat0 = middle(own0, near0, tie(grad_far0, own1), upd0, tok0, cot0, mod_two, 0, [own1])
    u_far0 = chip(u0)
    down1 = feed_down(order, hid1, down_weight, [u0])
    sum1 = far_sum([(far1, tie(near1, down1[1]))])
    grad_far1 = chip(sum1)
    up_send, up_keep = weight_grad(places, [low0, low1], [pre0, pre1], "up_grad", [sum1])
    up_got = to_dp(up_send, bits[0])
    pieces0 = pieces_of(u0, tie(u_far0, up_keep))
    down_send, down_keep = weight_grad(other_places, [gm0, gm1], [hid0, hid1], "down_grad", [up_keep])
    down_got = to_dp(down_send, other_bits[0])
    g1, u1, stat1 = middle(own1, near1, tie(grad_far1, down_keep), upd1, tok1, cot1, mod_two, 1, [down_keep])
    u_far1 = chip(u1)

    back0 = attend_back(near, order, pieces0, proj_weight, *qkv0, total0, 0, 1, 0, ((), w3, tokens0), [u1])
    mlp_near0, mlp_near1 = core(tie(down0[0], u1)), core(tie(down1[0], u1))
    mlp_sum = far_sum([(down0[1], tie(mlp_near0, back0[1])), (down1[1], tie(mlp_near1, back0[1]))])
    mlp_far = chip(mlp_sum)
    in_near0 = core(back0[2])
    pieces1 = pieces_of(u1, tie(u_far1, back0[1]))
    (up_send, up_keep), (down_send, down_keep) = fold(
        [(up_keep, tie(up_got, back0[1])), (down_keep, tie(down_got, back0[1]))], [mlp_sum]
    )
    up_got, down_got = to_dp(up_send, bits[1]), to_dp(down_send, other_bits[1])
    in_sum0 = far_sum([(back0[3], tie(in_near0, up_keep))])
    in_far0 = chip(in_sum0)
    half1 = attend_back(near, order, pieces1, proj_weight, *qkv1, total1, 0, 2, 1, None, [in_sum0])
    (up_send, up_keep), (down_send, down_keep) = fold(
        [(up_keep, tie(up_got, half1[1])), (down_keep, tie(down_got, half1[1]))]
    )
    up_got, down_got = to_dp(up_send, bits[2]), to_dp(down_send, other_bits[2])
    first_send, first_keep = first_grad(
        near, places, [in0, in1], [back0[0], half1[0]], [(0, 2), (0, 1)], [mixed0, mixed1], [pieces0, pieces1],
        [up_keep],
    )
    first_got = to_dp(first_send, bits[0])
    output, gate = finish(
        (down0[2], mlp_near0, tie(mlp_far, first_keep), upd0, tok0, cot0),
        (down1[2], mlp_near1, tie(mlp_far, first_keep), upd1, tok1, cot1),
        mod_two, down_bias, [first_keep],
    )
    grad_tokens0 = last((back0[4], in_near0, tie(in_far0, gate), g0, tok0), mod_one, 0)
    ((first_send, first_keep),) = fold([(first_keep, tie(first_got, grad_tokens0))])
    first_got = to_dp(first_send, bits[1])
    rest1 = attend_back(
        near, order, pieces1, proj_weight, *qkv1, total1, 1, 2, 1, ((half1[0],), w3, tokens1), [first_keep]
    )

    in_near1 = core(rest1[2])
    mod = pack([back0[5], stat0, rest1[5], stat1, gate])
    mod_near = core(mod)
    second_send, second_keep = weight_grad(
        other_places, [in0, in1], [back0[0], rest1[0]], "qkv_grad", [mod, first_got], 1, [(1, 2), (0, 1)]
    )
    second_got = to_dp(second_send, other_bits[0])
    mod = mod + tie(mod_near, second_keep)
    mod_far = chip(mod)
    in_sum1 = far_sum([(rest1[3], tie(in_near1, mod))])
    in_far1 = chip(in_sum1)
    ((first_send, first_keep),) = fold([(first_keep, tie(first_got, in_sum1))])
    first_got = to_dp(first_send, bits[2])
    note, low_mod = message(
        here,
        [mod, tie(mod_far, first_keep), condition, ub0, ub1, db0, db1, back0[1], half1[1], rest1[1]],
    )
    note_got = to_dp(note, bits[0])
    up_shard, down_shard = close(
        [
            end_steps(up_keep, tie(up_got, note), bits[3:]),
            end_steps(down_keep, tie(down_got, note), other_bits[3:]),
        ],
        (width, 0),
    )
    ((second_send, second_keep),) = fold([(second_keep, tie(second_got, down_shard))])
    second_got = to_dp(second_send, other_bits[1])
    note = join(note, tie(note_got, second_keep))
    note_got = to_dp(note, bits[1])
    grad_condition = condition_grad(low_mod, modulation_weight, condition, [note])
    ((second_send, second_keep),) = fold([(second_keep, tie(second_got, grad_condition))])
    second_got = to_dp(second_send, other_bits[2])
    note = join(note, tie(note_got, second_keep))
    note_got = to_dp(note, bits[2])
    grad_tokens = last((rest1[4], in_near1, tie(in_far1, note), g1, tok1), mod_one, 1, grad_tokens0)
    first = end_steps(first_keep, tie(first_got, note), bits[3:])
    mod_rows = width // size
    ff = up_weight.shape[1]
    if len(bits) == 3 and mod_rows % 128 == 0:
        mod_shard, mod_bias_sum, up_bias_sum, down_bias_sum, qv_sum, proj_bias_sum = final(
            index[None], note, tie(note_got, grad_tokens), mod_rows, mod_cols, width, ff, heads
        )
    else:
        note = join(note, tie(note_got, grad_tokens))
        for bit in bits[3:]:
            note = join(note, to_dp(note, bit))
        rows = note.shape[0] - 2
        all_silu = note[:rows, :width].astype(BF)
        all_cols = note[:rows, width : width + mod_cols].astype(BF)
        my_silu = lax.dynamic_slice_in_dim(all_silu, index * mod_rows, mod_rows, 1)
        mod_shard = dot(my_silu, all_cols, ROWS)
        mod_bias_sum = jnp.sum(all_cols, axis=0, dtype=F32)
        up_bias_sum, down_bias_sum, qv_sum = jnp.split(note[rows, : ff + width + 2 * heads], [ff, ff + width])
        qv_sum = qv_sum.reshape(2, heads)
        proj_bias_sum = note[rows + 1, :width]
    second = end_steps(second_keep, tie(second_got, mod_shard), bits[3:])
    qkv_shard, proj_shard = close_heads(first, second, 3 * (heads // 2))
    qkv_shard = jnp.transpose(qkv_shard, (1, 0, 2))
    return (
        output,
        grad_tokens,
        grad_condition,
        mod_shard,
        mod_bias_sum,
        qkv_shard,
        qv_sum,
        proj_shard,
        proj_bias_sum,
        up_shard,
        up_bias_sum,
        down_shard,
        down_bias_sum,
    )


def solution(mesh):
    in_specs = (
        P(None, "dp", None),
        P("dp", None),
        P(),
        P(),
        P(None, None, "tensor"),
        P(None, "tensor"),
        P("tensor", None),
        P(),
        P(None, "tensor"),
        P("tensor"),
        P("tensor", None),
        P(),
        P(None, "dp", None),
    )
    out_specs = (
        P("tensor", "dp", None),
        P("tensor", "dp", None),
        P("dp", None),
        P("dp", "tensor"),
        P("tensor"),
        P("dp", None, "tensor"),
        P(None, "tensor"),
        P("tensor", "dp"),
        P(),
        P("dp", "tensor"),
        P("tensor"),
        P("tensor", "dp"),
        P(),
    )
    return jax.shard_map(shards, mesh=mesh, in_specs=in_specs, out_specs=out_specs, check_vma=False)
```

```python
import functools

import jax
import jax.numpy as jnp
from jax import lax
from jax.experimental import pallas as pl
from jax.experimental.pallas import tpu as pltpu
from jax.sharding import PartitionSpec as P

HEAD_DIM = 64
EPS = 1e-06
BF = jnp.bfloat16
F32 = jnp.float32
ROWS = ((0,), (0,))
COLS = ((1,), (1,))
MIB = 1 << 20
SCALE = HEAD_DIM**-0.5
SEND_FIRST = (3, 1, 2, 0)
NEAR_FIRST = (0, 2, 1, 3)
LIMITS = {
    "prepare": 60,
    "attend_forward": 16,
    "attend_modulate": 16,
    "feed": 24,
    "feed_down": 14,
    "far_sum": 8,
    "middle": 20,
    "up_grad": 20,
    "down_grad": 20,
    "qkv_grad": 14,
    "first_grad": 26,
    "fold": 24,
    "attend_backward": 20,
    "attend_backward_end": 32,
    "finish": 32,
    "grad_tokens": 60,
}


def dot(left, right, dims=((1,), (0,))):
    return lax.dot_general(left, right, (dims, ((), ())), preferred_element_type=F32)


def swap(value, axis, bit):
    pairs = [(i, i ^ bit) for i in range(lax.axis_size(axis))]
    return lax.ppermute(value, axis, pairs)


def normalize(values):
    centre = values - jnp.mean(values, axis=-1, keepdims=True)
    inverse = lax.rsqrt(jnp.mean(centre * centre, axis=-1, keepdims=True) + EPS)
    return centre * inverse, inverse


def norm_back(grad, normed, inverse):
    return inverse * (
        grad
        - jnp.mean(grad, axis=-1, keepdims=True)
        - normed * jnp.mean(grad * normed, axis=-1, keepdims=True)
    )


def gelu_pair(v):
    root = 0.7978845608028654
    square = v * v
    inner = jnp.tanh(v * (root + (root * 0.044715) * square))
    half = 0.5 + 0.5 * inner
    slope = half + (0.5 * v) * (1.0 - inner * inner) * (root + (3 * root * 0.044715) * square)
    return v * half, slope


def head_lanes(rows, cols, h):
    return lax.broadcasted_iota(jnp.int32, (rows, cols), 1) // HEAD_DIM == h


def spread(x, heads):
    rows, cols = x.shape
    zero = jnp.zeros_like(x)
    return jnp.concatenate([jnp.where(head_lanes(rows, cols, h), x, zero) for h in range(heads)], 0)


def whole(shape):
    return pl.BlockSpec(shape, lambda *_: (0,) * len(shape))


def shape_of(shape, dtype):
    return jax.ShapeDtypeStruct(shape, dtype)


def cost(expected):
    return pl.CostEstimate(flops=int(expected * 5.75e9), bytes_accessed=0, transcendentals=0)


ANY = pl.BlockSpec(memory_space=pl.ANY)
HBM = "hbm"


def call(kernel, name, scalars, grid, ins, in_specs, outs, out_specs, expected, after=(), scratch=()):
    skip = len(after)

    def body(*refs):
        first = len(scalars)
        kernel(*refs[:first], *refs[first + skip :])

    return pl.pallas_call(
        body,
        out_shape=[pltpu.HBM(*o[:2]) if len(o) > 2 else shape_of(*o) for o in outs],
        grid_spec=pltpu.PrefetchScalarGridSpec(
            num_scalar_prefetch=len(scalars),
            grid=grid,
            in_specs=[ANY] * skip + in_specs,
            out_specs=out_specs,
            scratch_shapes=list(scratch),
        ),
        compiler_params=pltpu.CompilerParams(vmem_limit_bytes=LIMITS.get(name, 16) * MIB),
        cost_estimate=cost(expected),
        name=name,
    )(*scalars, *after, *ins)


def silu(cond):
    value = cond.astype(F32)
    return (value * (1.0 / (1.0 + jnp.exp(-value)))).astype(BF)


def modulate(cond_ref, w_ref, bias_ref):
    return dot(silu(cond_ref[...]), w_ref[...]) + bias_ref[...].astype(F32)[None]


def mod_specs(cond, width, first):
    return [
        whole(cond.shape),
        pl.BlockSpec((width, width), lambda i: (0, first(i))),
        pl.BlockSpec((width,), lambda i: (first(i),)),
    ]


def prepare_kernel(tok_ref, w_ref, bias_ref, cond_ref, s_ref, sb_ref, cond_too, t_ref, tb_ref, mod_ref, *outs):
    rows, lats, width = tok_ref.shape

    @pl.when(pl.program_id(0) == 0)
    def _():
        mod_ref[:, :width] = modulate(cond_ref, s_ref, sb_ref)
        mod_ref[:, width:] = modulate(cond_too, t_ref, tb_ref)

    chunk = min(rows, 256 // lats)
    step = lats * chunk
    both = tok_ref[...].reshape(rows * lats, width)
    here = lax.broadcasted_iota(jnp.int32, (step, step), 0)
    there = lax.broadcasted_iota(jnp.int32, (step, step), 1)
    order = jnp.where(there == lats * lax.rem(here, chunk) + lax.div(here, chunk), 1.0, 0.0).astype(BF)
    split = [dot(order, both[j * step : (j + 1) * step]) for j in range(rows // chunk)]
    for lat in range(lats):
        x = jnp.concatenate([part[lat * chunk : (lat + 1) * chunk] for part in split], 0)
        tok_out, in_ref, q_ref, k_ref, v_ref = outs[5 * lat : 5 * lat + 5]
        tok_out[...] = x.astype(BF)
        row = lambda j: mod_ref[lat : lat + 1, j * width : (j + 1) * width]
        normed, _ = normalize(x)
        low = (normed * (1.0 + row(1)) + row(0)).astype(BF)
        in_ref[...] = low
        q_ref[...] = (dot(low, w_ref[0]) + bias_ref[0:1].astype(F32)).astype(BF)
        k_ref[...] = dot(low, w_ref[1]).astype(BF)
        v_ref[...] = (dot(low, w_ref[2]) + bias_ref[1:2].astype(F32)).astype(BF)


def prepare(tokens, cond, mod_weight, mod_bias, w3, bias, after=(), block=256):
    seq, lats, width = tokens.shape
    cols = w3.shape[2]
    rows = lambda n: pl.BlockSpec((block, n), lambda i: (i, 0))
    one = [((seq, width), BF, HBM)] * 2 + [((seq, cols), BF)] * 3
    got = call(
        prepare_kernel, "prepare", [], (seq // block,),
        [tokens, w3, bias] + [cond, mod_weight, mod_bias] * 2,
        [pl.BlockSpec((block, lats, width), lambda i: (i, 0, 0)), whole(w3.shape), whole(bias.shape)]
        + mod_specs(cond, width, lambda i: 0)
        + mod_specs(cond, width, lambda i: 1),
        [((lats, 2 * width), F32)] + one * lats,
        [whole((lats, 2 * width))] + [rows(width), rows(width), rows(cols), rows(cols), rows(cols)] * lats,
        12, after,
    )
    return got[0], got[1:6], got[6:11]


def attend_kernel(q_ref, k_ref, v_ref, *refs):
    mixed_ref, total_ref = refs[-2:]
    rows, cols = q_ref.shape
    heads = cols // HEAD_DIM
    value = v_ref[...].T
    scores = dot(k_ref[...], spread(q_ref[...] * BF(SCALE), heads), COLS)
    largest = jnp.max(scores, axis=0, keepdims=True)
    powers = jnp.exp(scores - largest)
    total = jnp.sum(powers, axis=0, keepdims=True)
    probs = (powers * (1.0 / total)).astype(BF)
    out = [
        dot(value[h * HEAD_DIM : (h + 1) * HEAD_DIM], probs[:, h * rows : (h + 1) * rows]) for h in range(heads)
    ]
    mixed_ref[...] = jnp.concatenate(out, 0).T.astype(BF)
    total_ref[0] = largest + jnp.log(total)
    if len(refs) > 2:
        cond_ref, w_ref, bias_ref, mod_ref = refs[:4]
        mod_ref[...] = modulate(cond_ref, w_ref, bias_ref)


def attend(q, k, v, block, after=(), mod=None):
    seq, cols = q.shape
    heads = cols // HEAD_DIM
    rows = pl.BlockSpec((block, cols), lambda i: (i, 0))
    ins, in_specs, outs, out_specs = [q, k, v], [rows, whole((seq, cols)), whole((seq, cols))], [], []
    if mod is not None:
        lats, width = mod[0].shape
        ins += mod
        in_specs += mod_specs(mod[0], width, lambda i: 2 + i)
        outs, out_specs = [((lats, 4 * width), F32)], [pl.BlockSpec((lats, width), lambda i: (0, i))]
    return call(
        attend_kernel, "attend_forward" if mod is None else "attend_modulate", [], (seq // block,), ins, in_specs,
        outs + [((seq, cols), BF), ((seq // block, 1, heads * block), F32)],
        out_specs + [rows, pl.BlockSpec((1, 1, heads * block), lambda i: (i, 0, 0))],
        8, after,
    )


def halves(block, width):
    return [
        pl.BlockSpec((block, width), lambda i, *_: (jnp.minimum(i, 1), 0)),
        whole((block, width)),
        whole((block, width)),
    ]


def place_quarter(step, value, send_ref, far_ref, own_ref):
    @pl.when(step < 2)
    def _():
        send_ref[...] = value.astype(send_ref.dtype)

    @pl.when(step == 2)
    def _():
        far_ref[...] = value

    @pl.when(step == 3)
    def _():
        own_ref[...] = value


def feed_kernel(
    lat, order_ref, m0, m1, m2, m3, p0, p1, p2, p3, pb_ref, tok_ref, cot_ref, mod_ref, up_ref, ub_ref, down_ref,
    in_ref, hid_ref, pre_ref, gm_ref, upd_ref, tok_out, cot_out, send_ref, far_ref, own_ref, gub_ref, gdb_ref,
):
    i = pl.program_id(0)
    width = tok_ref.shape[1]
    row = lambda j: mod_ref[lat : lat + 1, j * width : (j + 1) * width]
    update = pb_ref[...].astype(F32)[None]
    for m, p in ((m0, p0), (m1, p1), (m2, p2), (m3, p3)):
        update = update + dot(m[...], p[...])
    normed, _ = normalize(tok_ref[...].astype(F32) + row(0) * update)
    low = (normed * (1.0 + row(2)) + row(1)).astype(BF)
    in_ref[...] = low
    act, slope = gelu_pair(dot(low, up_ref[...]) + ub_ref[...].astype(F32)[None])
    hid_ref[...] = act.astype(BF)
    grad_mlp = (row(3) * cot_ref[0].astype(F32)).astype(BF)
    gm_ref[...] = grad_mlp
    grad_pre = (dot(grad_mlp, down_ref[...], COLS) * slope).astype(BF)
    pre_ref[...] = grad_pre
    place_quarter(i, dot(grad_pre, up_ref[...], COLS), send_ref, far_ref, own_ref)

    @pl.when(i == 3)
    def _():
        upd_ref[...] = update
        tok_out[...] = tok_ref[...]
        cot_out[...] = cot_ref[0]

    @pl.when(i == 0)
    def _():
        gub_ref[...] = jnp.zeros_like(gub_ref)
        gdb_ref[...] = jnp.zeros_like(gdb_ref)

    gub_ref[...] += jnp.sum(grad_pre.astype(F32), axis=0, keepdims=True)
    gdb_ref[...] += jnp.sum(grad_mlp.astype(F32), axis=0, keepdims=True)


def feed(order, mixed, proj, proj_bias, tok, cot, mod, up, up_bias, down, lat, after=()):
    seq, width = tok.shape
    block = seq // 4
    ff = up.shape[1]
    cols = mixed[0].shape[1]
    at = lambda n: pl.BlockSpec((block, n), lambda i, o: (o[i], 0))
    at3 = pl.BlockSpec((1, block, width), lambda i, o: (lat, o[i], 0))
    quarter = ((block, width), F32)
    return call(
        functools.partial(feed_kernel, lat), "feed", [order], (4,),
        [*mixed, *proj, proj_bias, tok, cot, mod, up, up_bias, down],
        [at(cols)] * 4
        + [whole((cols, width))] * 4
        + [whole((width,)), at(width), at3, whole(mod.shape)]
        + [whole(up.shape), whole((ff,)), whole(down.shape)],
        [((seq, width), BF), ((seq, ff), BF), ((seq, ff), BF), ((seq, width), BF), quarter]
        + [((block, width), BF)] * 2
        + [((2 * block, width), F32), quarter, quarter, ((1, ff), F32), ((1, width), F32)],
        [at(width), at(ff), at(ff), at(width)]
        + [whole((block, width))] * 3
        + halves(block, width)
        + [whole((1, ff)), whole((1, width))],
        18, after,
    )


def down_kernel(order_ref, hid_ref, down_ref, send_ref, far_ref, own_ref):
    out = dot(hid_ref[...], down_ref[...])
    place_quarter(pl.program_id(0), out, send_ref, far_ref, own_ref)


def feed_down(order, hidden, down, after=()):
    seq, ff = hidden.shape
    width = down.shape[1]
    block = seq // 4
    quarter = ((block, width), F32)
    return call(
        down_kernel, "feed_down", [order], (4,),
        [hidden, down],
        [pl.BlockSpec((block, ff), lambda i, o: (o[i], 0)), whole(down.shape)],
        [((2 * block, width), BF), quarter, quarter],
        halves(block, width),
        5, after,
    )


def row_blocks(rows, width, skip=0, steps=1):
    return pl.BlockSpec((rows // steps, width), lambda i: (skip * steps + i, 0))


def add_stats(ref, values, first=0):
    @pl.when(pl.program_id(0) == 0)
    def _():
        ref[first : first + len(values)] = jnp.zeros((len(values), ref.shape[1]), F32)

    for j, value in enumerate(values):
        ref[first + j : first + j + 1] += jnp.sum(value, axis=0, keepdims=True)


def middle_kernel(lat, own, near, far, upd_ref, tok_ref, cot_ref, mod_ref, g_ref, low_ref, stat_ref):
    width = upd_ref.shape[1]
    row = lambda j: mod_ref[lat : lat + 1, j * width : (j + 1) * width]
    grad_in = own[...] + near[...] + far[...].astype(F32)
    update = upd_ref[...]
    normed, inverse = normalize(tok_ref[...].astype(F32) + row(0) * update)
    grad = cot_ref[...].astype(F32) + norm_back(grad_in * (1.0 + row(2)), normed, inverse)
    g_ref[...] = grad
    low = (row(0) * grad).astype(BF)
    low_ref[...] = low
    add_stats(stat_ref, (grad * update, grad_in, grad_in * normed, low.astype(F32)))


def middle(own, near, far, update, tok, cot, mod, lat, after=()):
    rows, width = own.shape
    mine = row_blocks(rows, width, 0, 2)
    return call(
        functools.partial(middle_kernel, lat), "middle", [], (2,),
        [own, near, far, update, tok, cot, mod],
        [mine, row_blocks(rows, width, 1, 2)] + [mine] * 4 + [whole(mod.shape)],
        [((rows, width), F32, HBM), ((rows, width), BF), ((4, width), F32)],
        [mine, mine, whole((4, width))],
        2, after,
    )


def finish_kernel(*refs):
    mod_ref, bias_ref, out_ref, stat_ref = refs[-4:]
    width = mod_ref.shape[1] // 4
    for lat in range(2):
        own, near, far, upd, tok, cot = refs[6 * lat : 6 * lat + 6]
        row = lambda j: mod_ref[lat : lat + 1, j * width : (j + 1) * width]
        update = own[...] + near[...].astype(F32) + far[...].astype(F32) + bias_ref[...].astype(F32)[None]
        stream = tok[...].astype(F32) + row(0) * upd[...]
        out_ref[:, lat, :] = (stream + row(3) * update).astype(BF)
        add_stats(stat_ref, (cot[...].astype(F32) * update,), lat)


def finish(first, other, mod, bias, after=()):
    rows, width = first[0].shape
    mine = row_blocks(rows, width)
    one = lambda lat: [mine, row_blocks(rows, width, 1), row_blocks(rows, width, lat)] + [mine] * 3
    return call(
        finish_kernel, "finish", [], (1,),
        [*first, *other, mod, bias],
        one(0) + one(1) + [whole(mod.shape), whole((width,))],
        [((rows, 2, width), BF), ((2, width), F32)],
        [whole((rows, 2, width)), whole((2, width))],
        4, after,
    )


def last_kernel(lat, *refs):
    own, near, far, g_ref, tok, mod_ref = refs[:6]
    out_ref = refs[-1]
    width = mod_ref.shape[1] // 2
    grad_in = own[...] + near[...] + far[...].astype(F32)
    normed, inverse = normalize(tok[...].astype(F32))
    scale = 1.0 + mod_ref[lat : lat + 1, width : 2 * width]
    out = g_ref[...] + norm_back(grad_in * scale, normed, inverse)
    if lat == 0:
        out_ref[...] = out
    else:
        out_ref[:, 0, :] = refs[6][...]
        out_ref[:, 1, :] = out


def last(arrays, mod, lat, other=None, after=()):
    rows, width = arrays[0].shape
    steps = 2
    mine = row_blocks(rows, width, 0, steps)
    both = [] if other is None else [other]
    shape, block = (
        ((rows, width), mine) if lat == 0
        else ((rows, 2, width), pl.BlockSpec((rows // steps, 2, width), lambda i: (i, 0, 0)))
    )
    return call(
        functools.partial(last_kernel, lat), "grad_tokens", [], (steps,),
        [*arrays, mod, *both],
        [mine, row_blocks(rows, width, 1, steps)] + [mine] * 3 + [whole(mod.shape)] + [mine] * len(both),
        [(shape, F32) if lat == 0 else (shape, F32, HBM)],
        [block],
        3, after,
    )[0]


def pack_kernel(rest0, mid0, rest1, mid1, gate, out_ref):
    out_ref[...] = jnp.zeros_like(out_ref)
    for lat, (rest, mid) in enumerate(((rest0, mid0), (rest1, mid1))):
        out_ref[8 * lat : 8 * lat + 2] = rest[0:2]
        out_ref[8 * lat + 2 : 8 * lat + 5] = mid[0:3]
        out_ref[8 * lat + 5 : 8 * lat + 6] = gate[lat : lat + 1]
        out_ref[8 * lat + 6 : 8 * lat + 7] = mid[3:4]


def pack(arrays, after=()):
    width = arrays[0].shape[1]
    return call(
        pack_kernel, "pack", [], (1,), arrays, [whole(a.shape) for a in arrays],
        [((16, width), F32)], [whole((16, width))], 1, after,
    )[0]


def message_kernel(place_ref, mine, theirs, cond_ref, ub0, ub1, db0, db1, back0, half1, rest1, out_ref, low_ref):
    width = mine.shape[1]
    total = mine[...] + theirs[...]
    low_ref[...] = total.astype(BF).astype(F32)
    out_ref[...] = jnp.zeros_like(out_ref)
    unit = width // 2
    active = silu(cond_ref[...]).astype(F32)
    for lat in range(2):
        out_ref[lat : lat + 1, :width] = active[lat : lat + 1, :]
        for t in range(3):
            at = 3 * place_ref[0] + t
            cols = pl.ds(pl.multiple_of(lax.rem(at, 2) * unit, unit), unit)
            out_ref[lat : lat + 1, width + t * unit : width + (t + 1) * unit] = low_ref[
                pl.ds(8 * lat + lax.div(at, 2), 1), cols
            ]
    ff = ub0.shape[1]
    heads = half1.shape[1]
    out_ref[2:3, :ff] = ub0[...] + ub1[...]
    out_ref[2:3, ff : ff + width] = db0[...] + db1[...]
    at = ff + width
    for j in (0, 2):
        for t, other in enumerate((half1, rest1)):
            out_ref[2:3, at : at + heads] = back0[j : j + 1, t * heads : (t + 1) * heads] + other[j : j + 1]
            at += heads
    out_ref[3:4, :width] = total[6:7] + total[14:15]


def message(place, arrays, after=()):
    width = arrays[0].shape[1]
    ff, heads = arrays[3].shape[1], arrays[7].shape[1]
    shape = (4, max(width + 3 * (width // 2), ff + width + 2 * heads))
    return call(
        message_kernel, "message", [place], (1,), arrays, [whole(a.shape) for a in arrays],
        [(shape, F32), ((16, width), F32)], [whole(shape), whole((16, width))], 1, after,
    )


def join_kernel(mine, theirs, out_ref):
    rows = mine.shape[0] - 2
    out_ref[:rows] = mine[:rows]
    out_ref[rows : 2 * rows] = theirs[:rows]
    out_ref[2 * rows :] = mine[rows:] + theirs[rows:]


def join(mine, theirs, after=()):
    shape = (2 * mine.shape[0] - 2, mine.shape[1])
    return call(
        join_kernel, "join", [], (1,), [mine, theirs], [whole(mine.shape)] * 2,
        [(shape, F32)], [whole(shape)], 1, after,
    )[0]


def final_kernel(sizes, index_ref, mine, theirs, shard_ref, mod_ref, up_ref, down_ref, qv_ref, proj_ref):
    mod_rows, mod_cols, width, ff, heads = sizes
    rows = mine.shape[0] - 2
    here = pl.ds(pl.multiple_of(index_ref[0] * mod_rows, mod_rows), mod_rows)
    lows = jnp.concatenate([mine[:rows, width : width + mod_cols], theirs[:rows, width : width + mod_cols]], 0)
    active = jnp.concatenate([mine[:rows, here], theirs[:rows, here]], 0)
    shard_ref[...] = dot(active.astype(BF), lows.astype(BF), ROWS)
    mod_ref[...] = jnp.sum(lows, axis=0)
    sums = mine[rows : rows + 1, :] + theirs[rows : rows + 1, :]
    up_ref[...] = sums[0, :ff]
    down_ref[...] = sums[0, ff : ff + width]
    qv_ref[0:1] = sums[:, ff + width : ff + width + heads]
    qv_ref[1:2] = sums[:, ff + width + heads : ff + width + 2 * heads]
    proj_ref[...] = (mine[rows + 1 : rows + 2, :width] + theirs[rows + 1 : rows + 2, :width])[0]


def final(index, mine, theirs, *sizes):
    mod_rows, mod_cols, width, ff, heads = sizes
    shapes = [(mod_rows, mod_cols), (mod_cols,), (ff,), (width,), (2, heads), (width,)]
    return call(
        functools.partial(final_kernel, sizes), "final", [index], (1,),
        [mine, theirs], [whole(mine.shape)] * 2, [(a, F32) for a in shapes], [whole(a) for a in shapes], 2,
    )


def condition_kernel(low_ref, w_ref, cond_ref, out_ref, acc):
    j = pl.program_id(0)

    @pl.when(j == 0)
    def _():
        acc[...] = jnp.zeros_like(acc)

    rows = jnp.concatenate([low_ref[pl.ds(j, 1), :], low_ref[pl.ds(8 + j, 1), :]], 0)
    acc[...] += dot(rows.astype(BF), w_ref[...], COLS)

    @pl.when(j == pl.num_programs(0) - 1)
    def _():
        cond = cond_ref[...].astype(F32)
        sig = 1.0 / (1.0 + jnp.exp(-cond))
        out_ref[...] = acc[...] * (sig * (1.0 + cond * (1.0 - sig)))


def condition_grad(low, weight, cond, after=()):
    lats, width = cond.shape
    return call(
        condition_kernel, "condition_grad", [], (6,), [low, weight, cond],
        [whole(low.shape), pl.BlockSpec((width, width), lambda i: (0, i)), whole(cond.shape)],
        [((lats, width), F32)], [whole((lats, width))], 5, after, [pltpu.VMEM((lats, width), F32)],
    )[0]


def place_rows(pos_ref, send_ref, keep_ref, first, values, tiles):
    rows = send_ref.shape[0] * 2 // tiles
    for t in range(values.shape[0] // rows):
        pos = pos_ref[first + t]
        part = values[t * rows : (t + 1) * rows]

        @pl.when(pos < tiles // 2)
        def _():
            send_ref[pl.ds(pl.multiple_of(pos * rows, rows), rows), :] = part.astype(BF)

        @pl.when(pos >= tiles // 2)
        def _():
            keep_ref[pl.ds(pl.multiple_of((pos - tiles // 2) * rows, rows), rows), :] = part


def weight_kernel(tiles, lats, pos_ref, *refs):
    send_ref, keep_ref = refs[-2:]
    rows = send_ref.shape[0] * 2 // tiles
    total = None
    for l in range(lats):
        right = refs[lats + l]
        value = right[...] if len(right.shape) == 2 else jnp.concatenate([right[j] for j in range(3)], 1)
        part = dot(refs[l][...], value, ROWS)
        total = part if total is None else total + part
    first = pl.program_id(0) * (refs[0].shape[1] // rows)
    place_rows(pos_ref, send_ref, keep_ref, first, total, tiles)


def weight_grad(pos, lefts, rights, name, after=(), steps=1, parts=None):
    tiles = pos.shape[0]
    seq, depth = lefts[0].shape
    shape = rights[0].shape
    specs = [whole(shape)] * len(rights)
    if parts is not None:
        shape = shape[:-1] + (shape[-1] // parts[0][1],)
        specs = [
            pl.BlockSpec(a.shape[:-1] + (a.shape[-1] // n,), functools.partial(lambda at, *_: (0, 0, at), at))
            for a, (at, n) in zip(rights, parts)
        ]
    width = shape[1] if len(shape) == 2 else shape[0] * shape[2]
    block = depth // steps
    half = (depth // 2, width)
    return call(
        functools.partial(weight_kernel, tiles, len(lefts)), name, [pos], (steps,),
        [*lefts, *rights],
        [pl.BlockSpec((seq, block), lambda i, o: (0, i))] * len(lefts) + specs,
        [(half, BF), (half, F32)],
        [whole(half)] * 2,
        width / 128, after,
    )


def first_kernel(tiles, quarter, lats, order_ref, pos_ref, *refs):
    ins, lows, mixed, pieces = refs[:lats], refs[lats : 2 * lats], refs[2 * lats : 3 * lats], refs[3 * lats : -2]
    heads, proj = None, None
    for l in range(lats):
        part = dot(ins[l][...], jnp.concatenate([lows[l][j] for j in range(3)], 1), ROWS)
        heads = part if heads is None else heads + part
        for j in range(4):
            rows = pl.ds(pl.multiple_of(order_ref[j] * quarter, quarter), quarter)
            part = dot(pieces[4 * l + j][...], mixed[l][rows, :], ROWS)
            proj = part if proj is None else proj + part
    place_rows(pos_ref, refs[-2], refs[-1], 0, jnp.concatenate([heads, proj], 1), tiles)


def first_grad(order, pos, ins, lows, parts, mixed, pieces, after=()):
    tiles = pos.shape[0]
    quarter, width = pieces[0][0].shape
    args = [*ins, *lows, *mixed, *[p for four in pieces for p in four]]
    low_specs = [
        pl.BlockSpec(a.shape[:-1] + (a.shape[-1] // n,), functools.partial(lambda at, *_: (0, 0, at), at))
        for a, (at, n) in zip(lows, parts)
    ]
    cols = 3 * (lows[0].shape[2] // parts[0][1]) + mixed[0].shape[1]
    half = (width // 2, cols)
    return call(
        functools.partial(first_kernel, tiles, quarter, len(ins)), "first_grad", [order, pos], (1,),
        args,
        [whole(a.shape) for a in ins]
        + low_specs
        + [whole(a.shape) for a in args[2 * len(ins) :]],
        [(half, BF), (half, F32)],
        [whole(half)] * 2,
        6, after,
    )


def back_step(i, near_ref, pieces, p_ref, q_ref, k_ref, v_ref, total_ref, low_ref, bias_ref, dk_acc, dv_acc, grad_ref):
    rows, cols = q_ref.shape
    heads = cols // HEAD_DIM
    turned = dk_acc.shape[0] == cols

    @pl.when(i == 0)
    def _():
        dk_acc[...] = jnp.zeros_like(dk_acc)
        dv_acc[...] = jnp.zeros_like(dv_acc)

    for j in range(4):

        @pl.when(i == j)
        def _():
            grad_ref[...] = dot(pieces[j][...], p_ref[...], COLS).astype(BF)

    @pl.when(i < 4)
    def _():
        q = spread(q_ref[...] * BF(SCALE), heads)
        g = spread(grad_ref[...], heads)
        k, v = k_ref[...], v_ref[...]
        probs = jnp.exp(dot(k, q, COLS) - total_ref[0])
        grad_probs = dot(v, g, COLS)
        inner = jnp.sum(probs * grad_probs, axis=0, keepdims=True)
        scores = (probs * (grad_probs - inner)).astype(BF)
        probs = probs.astype(BF)
        if turned:
            dv_acc[...] += dot(g, probs, ((0,), (1,)))
            dk_acc[...] += dot(q, scores, ((0,), (1,)))
            every = dot(k, scores, ROWS)
            dq = jnp.concatenate(
                [every[h * HEAD_DIM : (h + 1) * HEAD_DIM, h * rows : (h + 1) * rows] for h in range(heads)], 0
            ).T
        else:
            dv_acc[...] += dot(probs, g)
            dk_acc[...] += dot(scores, q)
            every = dot(scores, k, ROWS)
            dq = every[:rows]
            for h in range(1, heads):
                dq = jnp.where(head_lanes(rows, cols, h), every[h * rows : (h + 1) * rows], dq)
        low_ref[0, pl.ds(pl.multiple_of(near_ref[i] * rows, rows), rows), :] = (dq * SCALE).astype(BF)

    @pl.when(i == 3)
    def _():
        low_ref[1] = (dk_acc[...].T if turned else dk_acc[...]).astype(BF)
        low_ref[2] = (dv_acc[...].T if turned else dv_acc[...]).astype(BF)
        bias_ref[...] = jnp.zeros_like(bias_ref)
        for j in range(3):
            bias_ref[j : j + 1] = jnp.sum(low_ref[j].astype(F32), axis=0, keepdims=True)


def back_kernel(near_ref, u0, u1, u2, u3, p_ref, q_ref, k_ref, v_ref, total_ref, low_ref, bias_ref, *scratch):
    back_step(
        pl.program_id(0), near_ref, (u0, u1, u2, u3), p_ref, q_ref, k_ref, v_ref, total_ref, low_ref, bias_ref,
        *scratch,
    )


def back_end_kernel(lat, others, near_ref, order_ref, u0, u1, u2, u3, p_ref, q_ref, k_ref, v_ref, total_ref, *refs):
    other_refs, (w_ref, tok_ref), refs = refs[:others], refs[others : others + 2], refs[others + 2 :]
    low_ref, bias_ref, send_ref, far_ref, own_ref, stat_ref = refs[:6]
    i = pl.program_id(0)
    rows = q_ref.shape[0]
    back_step(
        i, near_ref, (u0, u1, u2, u3), p_ref, q_ref, k_ref, v_ref, total_ref, low_ref, bias_ref, *refs[6:]
    )

    @pl.when(i == 0)
    def _():
        stat_ref[...] = jnp.zeros_like(stat_ref)

    @pl.when(i >= 4)
    def _():
        here = pl.ds(pl.multiple_of(order_ref[jnp.maximum(i - 4, 0)] * rows, rows), rows)
        out = None
        for j in range(3):
            parts = [ref[j, here, :] for ref in (*other_refs, low_ref)]
            part = dot(jnp.concatenate(parts, 1), w_ref[j], COLS)
            out = part if out is None else out + part
        normed, _ = normalize(tok_ref[...].astype(F32))
        stat_ref[0:1] += jnp.sum(out, axis=0, keepdims=True)
        stat_ref[1:2] += jnp.sum(out * normed, axis=0, keepdims=True)
        place_quarter(i - 4, out, send_ref, far_ref, own_ref)


def attend_back(near, order, pieces, proj, q, k, v, total, part, parts, lat, end=None, after=()):
    seq, cols = q.shape
    cols = cols // parts
    width = proj.shape[1]
    block = seq // 4
    heads = cols // HEAD_DIM
    first = lambda i, n, *_: n[jnp.minimum(i, 3)]
    later = lambda i, n, o: o[jnp.maximum(i - 4, 0)]
    keys = pl.BlockSpec((seq, cols), lambda *_: (0, part))
    ins = [*pieces, proj, q, k, v, total]
    in_specs = [whole((block, width))] * 4 + [
        pl.BlockSpec((cols, width), lambda *_: (part, 0)),
        pl.BlockSpec((block, cols), lambda *a: (first(*a), part)),
        keys,
        keys,
        pl.BlockSpec((1, 1, heads * block), lambda *a: (first(*a), 0, part)),
    ]
    outs = [((3, seq, cols), BF), ((8, cols), F32)]
    out_specs = [whole((3, seq, cols)), whole((8, cols))]
    sums = (seq, cols) if parts == 1 else (cols, seq)
    scratch = [pltpu.VMEM(sums, F32)] * 2 + [pltpu.VMEM((block, cols), BF)]
    if end is None:
        return call(
            back_kernel, "attend_backward", [near], (4,), ins, in_specs, outs, out_specs, 20 / parts, after, scratch
        )
    others, w3, tok = end
    quarter = ((block, width), F32)
    return call(
        functools.partial(back_end_kernel, lat, len(others)), "attend_backward_end", [near, order], (8,),
        ins + [*others, w3, tok],
        in_specs
        + [whole(other.shape) for other in others]
        + [whole(w3.shape)]
        + [pl.BlockSpec((block, width), lambda *a: (later(*a), 0))],
        outs + [((2 * block, width), F32), quarter, quarter, ((8, width), F32)],
        out_specs
        + [
            pl.BlockSpec((block, width), lambda i, *_: (jnp.clip(i - 4, 0, 1), 0)),
            whole((block, width)),
            whole((block, width)),
            whole((8, width)),
        ],
        20 / parts + 4, after, scratch,
    )


def tie(value, *others):
    return lax.optimization_barrier((value, *others))[0]


def far_kernel(*refs):
    out_ref = refs[-1]
    for j in range(len(refs) // 2):
        rows = refs[2 * j].shape[0]
        out_ref[j * rows : (j + 1) * rows] = (refs[2 * j][...] + refs[2 * j + 1][...].astype(F32)).astype(BF)


def far_sum(pairs, after=()):
    rows, width = pairs[0][0].shape
    ins = [a for pair in pairs for a in pair]
    shape = (rows * len(pairs), width)
    block = pl.BlockSpec((rows, width), lambda i: (0, 0))
    return call(
        far_kernel, "far_sum", [], (1,), ins, [block] * len(ins), [(shape, BF)], [whole(shape)], 1, after
    )[0]


def fold_kernel(*refs):
    count = len(refs) // 4
    for j in range(count):
        keep, got, send, kept = refs[2 * j], refs[2 * j + 1], refs[2 * count + 2 * j], refs[2 * count + 2 * j + 1]
        half = kept.shape[0]
        send[...] = (keep[:half] + got[:half].astype(F32)).astype(BF)
        kept[...] = keep[half:] + got[half:].astype(F32)


def fold(pairs, after=()):
    ins = [a for pair in pairs for a in pair]
    outs = []
    for keep, _ in pairs:
        half = (keep.shape[0] // 2, keep.shape[1])
        outs += [(half, BF), (half, F32)]
    got = call(
        fold_kernel, "fold", [], (1,), ins, [whole(a.shape) for a in ins], outs, [whole(o[0]) for o in outs], 2, after
    )
    return [(got[2 * j], got[2 * j + 1]) for j in range(len(pairs))]


def close_kernel(turns, *refs):
    outs = list(refs[2 * len(turns) :])
    for j, turn in enumerate(turns):
        total = refs[2 * j][...] + refs[2 * j + 1][...].astype(F32)
        if turn > 0:
            outs.pop(0)[...] = total[:, :turn]
        if turn < total.shape[1]:
            outs.pop(0)[...] = total[:, turn:].T


def close(pairs, turns, after=()):
    shapes = []
    for (keep, _), turn in zip(pairs, turns):
        rows, width = keep.shape
        shapes += ([(rows, turn)] if turn > 0 else []) + ([(width - turn, rows)] if turn < width else [])
    ins = [a for pair in pairs for a in pair]
    return call(
        functools.partial(close_kernel, turns), "close", [], (1,),
        ins, [whole(a.shape) for a in ins], [(a, F32) for a in shapes], [whole(a) for a in shapes], 1, after,
    )


def heads_kernel(split, one_ref, one_got, other_ref, other_got, qkv_ref, proj_ref):
    one = one_ref[...] + one_got[...].astype(F32)
    other = other_ref[...] + other_got[...].astype(F32)
    cols = split // 3
    for j in range(3):
        qkv_ref[j, :, :cols] = one[:, j * cols : (j + 1) * cols]
        qkv_ref[j, :, cols:] = other[:, j * cols : (j + 1) * cols]
    proj_ref[...] = one[:, split:].T


def close_heads(one, other, split, after=()):
    rows, width = one[0].shape
    ins = [*one, *other]
    shapes = [(3, rows, 2 * split // 3), (width - split, rows)]
    return call(
        functools.partial(heads_kernel, split), "close", [], (1,),
        ins, [whole(a.shape) for a in ins], [(a, F32) for a in shapes], [whole(a) for a in shapes], 1, after,
    )


def end_steps(keep, got, bits):
    for bit in bits:
        ((send, keep),) = fold([(keep, got)])
        got = swap(send, "dp", bit)
    return keep, got


def pieces_of(own, far):
    return own, far, swap(own, "tensor", 1), swap(far, "tensor", 1)


def dp_bits(size):
    return [1 << i for i in range(size.bit_length() - 1)]


def row_places(index, size, bits):
    away = jnp.arange(size, dtype=jnp.int32) ^ index
    place = jnp.zeros((size,), jnp.int32)
    for bit in bits:
        place = 2 * place + 1 - (away // bit) % 2
    return place


def shards(
    tokens,
    condition,
    modulation_weight,
    modulation_bias,
    qkv_weight,
    qv_bias,
    proj_weight,
    proj_bias,
    up_weight,
    up_bias,
    down_weight,
    down_bias,
    cotangent,
):
    seq, lats, width = tokens.shape
    place = lax.axis_index("tensor")
    index = lax.axis_index("dp")
    size = lax.axis_size("dp")
    quarter = seq // 4
    mod_cols = modulation_weight.shape[1] // 4
    order = jnp.array(SEND_FIRST, jnp.int32) ^ place
    near = jnp.array(NEAR_FIRST, jnp.int32) ^ place
    here = place[None]
    bits = dp_bits(size)
    other_bits = [bits[1], bits[0]] + bits[2:]
    places, other_places = row_places(index, size, bits), row_places(index, size, other_bits)
    to_dp = lambda value, bit: swap(value, "dp", bit)
    core = lambda value: swap(value, "tensor", 1)
    chip = lambda value: swap(value, "tensor", 2)

    proj_far = chip(proj_weight)
    w3 = jnp.transpose(qkv_weight, (1, 0, 2))
    heads = w3.shape[2]

    mod_one, (tokens0, in0, *qkv0), (tokens1, in1, *qkv1) = prepare(
        tokens, condition, modulation_weight, modulation_bias, w3, qv_bias
    )
    mixed0, total0 = attend(*qkv0, quarter, [proj_far])
    mixed_far0 = chip(mixed0)
    mod_two, mixed1, total1 = attend(
        *qkv1, quarter, [mixed0], [condition, modulation_weight, modulation_bias]
    )
    mixed_far1 = chip(mixed1)
    cot = jnp.transpose(tie(cotangent, mixed1), (1, 0, 2))
    proj = pieces_of(proj_weight, tie(proj_far, mixed1))
    gathered0 = pieces_of(mixed0, tie(mixed_far0, mod_two))

    feed_args = (cot, mod_two, up_weight, up_bias, down_weight)
    low0, hid0, pre0, gm0, upd0, tok0, cot0, send0, far0, own0, ub0, db0 = feed(
        order, gathered0, proj, proj_bias, tokens0, *feed_args, 0
    )
    near0 = core(send0)
    gathered1 = pieces_of(mixed1, tie(mixed_far1, own0))
    down0 = feed_down(order, hid0, down_weight)
    sum0 = far_sum([(far0, tie(near0, down0[1]))])
    grad_far0 = chip(sum0)
    low1, hid1, pre1, gm1, upd1, tok1, cot1, send1, far1, own1, ub1, db1 = feed(
        order, gathered1, proj, proj_bias, tokens1, *feed_args, 1, [sum0]
    )
    near1 = core(send1)
    g0, u0, stat0 = middle(own0, near0, tie(grad_far0, own1), upd0, tok0, cot0, mod_two, 0, [own1])
    u_far0 = chip(u0)
    down1 = feed_down(order, hid1, down_weight, [u0])
    sum1 = far_sum([(far1, tie(near1, down1[1]))])
    grad_far1 = chip(sum1)
    up_send, up_keep = weight_grad(places, [low0, low1], [pre0, pre1], "up_grad", [sum1])
    up_got = to_dp(up_send, bits[0])
    pieces0 = pieces_of(u0, tie(u_far0, up_keep))
    down_send, down_keep = weight_grad(other_places, [gm0, gm1], [hid0, hid1], "down_grad", [up_keep])
    down_got = to_dp(down_send, other_bits[0])
    g1, u1, stat1 = middle(own1, near1, tie(grad_far1, down_keep), upd1, tok1, cot1, mod_two, 1, [down_keep])
    u_far1 = chip(u1)

    back0 = attend_back(near, order, pieces0, proj_weight, *qkv0, total0, 0, 1, 0, ((), w3, tokens0), [u1])
    mlp_near0, mlp_near1 = core(tie(down0[0], u1)), core(tie(down1[0], u1))
    mlp_sum = far_sum([(down0[1], tie(mlp_near0, back0[1])), (down1[1], tie(mlp_near1, back0[1]))])
    mlp_far = chip(mlp_sum)
    in_near0 = core(back0[2])
    pieces1 = pieces_of(u1, tie(u_far1, back0[1]))
    (up_send, up_keep), (down_send, down_keep) = fold(
        [(up_keep, tie(up_got, back0[1])), (down_keep, tie(down_got, back0[1]))], [mlp_sum]
    )
    up_got, down_got = to_dp(up_send, bits[1]), to_dp(down_send, other_bits[1])
    in_sum0 = far_sum([(back0[3], tie(in_near0, up_keep))])
    in_far0 = chip(in_sum0)
    half1 = attend_back(near, order, pieces1, proj_weight, *qkv1, total1, 0, 2, 1, None, [in_sum0])
    (up_send, up_keep), (down_send, down_keep) = fold(
        [(up_keep, tie(up_got, half1[1])), (down_keep, tie(down_got, half1[1]))]
    )
    up_got, down_got = to_dp(up_send, bits[2]), to_dp(down_send, other_bits[2])
    first_send, first_keep = first_grad(
        near, places, [in0, in1], [back0[0], half1[0]], [(0, 2), (0, 1)], [mixed0, mixed1], [pieces0, pieces1],
        [up_keep],
    )
    first_got = to_dp(first_send, bits[0])
    output, gate = finish(
        (down0[2], mlp_near0, tie(mlp_far, first_keep), upd0, tok0, cot0),
        (down1[2], mlp_near1, tie(mlp_far, first_keep), upd1, tok1, cot1),
        mod_two, down_bias, [first_keep],
    )
    grad_tokens0 = last((back0[4], in_near0, tie(in_far0, gate), g0, tok0), mod_one, 0)
    ((first_send, first_keep),) = fold([(first_keep, tie(first_got, grad_tokens0))])
    first_got = to_dp(first_send, bits[1])
    rest1 = attend_back(
        near, order, pieces1, proj_weight, *qkv1, total1, 1, 2, 1, ((half1[0],), w3, tokens1), [first_keep]
    )

    in_near1 = core(rest1[2])
    mod = pack([back0[5], stat0, rest1[5], stat1, gate])
    mod_near = core(mod)
    second_send, second_keep = weight_grad(
        other_places, [in0, in1], [back0[0], rest1[0]], "qkv_grad", [mod, first_got], 1, [(1, 2), (0, 1)]
    )
    second_got = to_dp(second_send, other_bits[0])
    mod = mod + tie(mod_near, second_keep)
    mod_far = chip(mod)
    in_sum1 = far_sum([(rest1[3], tie(in_near1, mod))])
    in_far1 = chip(in_sum1)
    ((first_send, first_keep),) = fold([(first_keep, tie(first_got, in_sum1))])
    first_got = to_dp(first_send, bits[2])
    note, low_mod = message(
        here,
        [mod, tie(mod_far, first_keep), condition, ub0, ub1, db0, db1, back0[1], half1[1], rest1[1]],
    )
    note_got = to_dp(note, bits[0])
    up_shard, down_shard = close(
        [
            end_steps(up_keep, tie(up_got, note), bits[3:]),
            end_steps(down_keep, tie(down_got, note), other_bits[3:]),
        ],
        (width, 0),
    )
    ((second_send, second_keep),) = fold([(second_keep, tie(second_got, down_shard))])
    second_got = to_dp(second_send, other_bits[1])
    note = join(note, tie(note_got, second_keep))
    note_got = to_dp(note, bits[1])
    grad_condition = condition_grad(low_mod, modulation_weight, condition, [note])
    ((second_send, second_keep),) = fold([(second_keep, tie(second_got, grad_condition))])
    second_got = to_dp(second_send, other_bits[2])
    note = join(note, tie(note_got, second_keep))
    note_got = to_dp(note, bits[2])
    grad_tokens = last((rest1[4], in_near1, tie(in_far1, note), g1, tok1), mod_one, 1, grad_tokens0)
    first = end_steps(first_keep, tie(first_got, note), bits[3:])
    mod_rows = width // size
    ff = up_weight.shape[1]
    if len(bits) == 3 and mod_rows % 128 == 0:
        mod_shard, mod_bias_sum, up_bias_sum, down_bias_sum, qv_sum, proj_bias_sum = final(
            index[None], note, tie(note_got, grad_tokens), mod_rows, mod_cols, width, ff, heads
        )
    else:
        note = join(note, tie(note_got, grad_tokens))
        for bit in bits[3:]:
            note = join(note, to_dp(note, bit))
        rows = note.shape[0] - 2
        all_silu = note[:rows, :width].astype(BF)
        all_cols = note[:rows, width : width + mod_cols].astype(BF)
        my_silu = lax.dynamic_slice_in_dim(all_silu, index * mod_rows, mod_rows, 1)
        mod_shard = dot(my_silu, all_cols, ROWS)
        mod_bias_sum = jnp.sum(all_cols, axis=0, dtype=F32)
        up_bias_sum, down_bias_sum, qv_sum = jnp.split(note[rows, : ff + width + 2 * heads], [ff, ff + width])
        qv_sum = qv_sum.reshape(2, heads)
        proj_bias_sum = note[rows + 1, :width]
    second = end_steps(second_keep, tie(second_got, mod_shard), bits[3:])
    qkv_shard, proj_shard = close_heads(first, second, 3 * (heads // 2))
    qkv_shard = jnp.transpose(qkv_shard, (1, 0, 2))
    return (
        output,
        grad_tokens,
        grad_condition,
        mod_shard,
        mod_bias_sum,
        qkv_shard,
        qv_sum,
        proj_shard,
        proj_bias_sum,
        up_shard,
        up_bias_sum,
        down_shard,
        down_bias_sum,
    )


def solution(mesh):
    in_specs = (
        P(None, "dp", None),
        P("dp", None),
        P(),
        P(),
        P(None, None, "tensor"),
        P(None, "tensor"),
        P("tensor", None),
        P(),
        P(None, "tensor"),
        P("tensor"),
        P("tensor", None),
        P(),
        P(None, "dp", None),
    )
    out_specs = (
        P("tensor", "dp", None),
        P("tensor", "dp", None),
        P("dp", None),
        P("dp", "tensor"),
        P("tensor"),
        P("dp", None, "tensor"),
        P(None, "tensor"),
        P("tensor", "dp"),
        P(),
        P("dp", "tensor"),
        P("tensor"),
        P("tensor", "dp"),
        P(),
    )
    return jax.shard_map(shards, mesh=mesh, in_specs=in_specs, out_specs=out_specs, check_vma=False)
```
